32 devices in a mesh: dp: 16 (over z, y, x), fsdp: 2 (over core).
Axes of the slice: x: 2, y: 2, z: 4, core: 2. Of those that a mesh axis runs over, the one named last changes fastest.
Arguments:
- tokens: bfloat16 [16384, 768], P(('dp', 'fsdp')), may hold values from -6 to 6
- lengths: int32 [16, 2], P('dp'), may hold values from 1 to 1023, as said below
- in_weight: bfloat16 [768, 2304], P(('dp', 'fsdp')), may hold values from -0.21875 to 0.21875
- out_weight: bfloat16 [768, 768], P(('dp', 'fsdp')), may hold values from -3.5 to 3.5
- out_bias: bfloat16 [768], P(('dp', 'fsdp')), may hold values from -2 to 2
- norm_gain: bfloat16 [768], P(('dp', 'fsdp')), may hold values from 0.5 to 1.5
- norm_bias: bfloat16 [768], P(('dp', 'fsdp')), may hold values from -2 to 2
- up_weight: bfloat16 [768, 3072], P(('dp', 'fsdp')), may hold values from -0.21875 to 0.21875
- up_bias: bfloat16 [3072], P(('dp', 'fsdp')), may hold values from -3 to 3
- down_weight: bfloat16 [3072, 768], P(('dp', 'fsdp')), may hold values from -0.109375 to 0.109375
- down_bias: bfloat16 [768], P(('dp', 'fsdp')), may hold values from -2 to 2
- final_gain: bfloat16 [768], P(('dp', 'fsdp')), may hold values from 0.5 to 1.5
- final_bias: bfloat16 [768], P(('dp', 'fsdp')), may hold values from -2 to 2
- cotangent: bfloat16 [16384, 768], P(('dp', 'fsdp')), may hold values from -6 to 6
Outputs:
- output: bfloat16 [16384, 768], P(('dp', 'fsdp'))
- tokens_grad: float32 [16384, 768], P(('dp', 'fsdp'))
- in_weight_grad: float32 [768, 2304], P(('dp', 'fsdp'))
- out_weight_grad: float32 [768, 768], P(('dp', 'fsdp'))
- out_bias_grad: float32 [768], P(('dp', 'fsdp'))
- norm_gain_grad: float32 [768], P(('dp', 'fsdp'))
- norm_bias_grad: float32 [768], P(('dp', 'fsdp'))
- up_weight_grad: float32 [768, 3072], P(('dp', 'fsdp'))
- up_bias_grad: float32 [3072], P(('dp', 'fsdp'))
- down_weight_grad: float32 [3072, 768], P(('dp', 'fsdp'))
- down_bias_grad: float32 [768], P(('dp', 'fsdp'))
- final_gain_grad: float32 [768], P(('dp', 'fsdp'))
- final_bias_grad: float32 [768], P(('dp', 'fsdp'))
The draws below stay inside these ranges and needn't reach their ends.
Inputs may be any that keep to these rules, and one draw needn't show every extreme that they name: Each group's two lengths sum to 1024, the shorter of them is under 512, either may come first, and in some group the shorter has exactly one row.
All inputs are finite; a program needn't handle non-finite values.
Results may differ from the reference program's by a relative error of at most 0.0095.
Values may be sent and summed in bfloat16 or wider, within the bound.
A program may use at most 192 MiB of HBM per device.

```python
import math
import jax
import jax.numpy as jnp
from jax import lax

D = 768
HEADS = 12
HEAD = 64
FF = 3072
TOK_DEV = 512
BLOCK = 512
GROUP = 1024
GROUPS = 16
TOKENS = 16384
N_FSDP = 2


def draw_lengths(key, part):
    key = jax.random.fold_in(key, 5)
    key_short, key_order, key_pick = jax.random.split(key, 3)
    short = jax.random.randint(key_short, (GROUPS,), 1, TOK_DEV)
    chosen = jax.random.randint(key_pick, (), 0, GROUPS)
    short = jnp.where(jnp.arange(GROUPS, dtype=jnp.int32) == chosen, 1, short)
    order = jax.random.randint(key_order, (GROUPS,), 0, 2)
    first = jnp.where(order == 0, short, GROUP - short)
    return jnp.stack([first, GROUP - first], axis=1).astype(jnp.int32)


def draw_tokens(key, part):
    key = jax.random.fold_in(key, 7)
    key_common, key_rows = jax.random.split(key, 2)
    common = jax.random.normal(key_common, (1, D), jnp.float32)
    spread = jax.random.normal(key_rows, (TOKENS, D), jnp.float32)
    return jnp.clip(spread + common, -6.0, 6.0).astype(jnp.bfloat16)


def with_spikes(drawn, stream_key, source, target, shards_of, factor):
    owner, partner = [(jnp.arange(drawn.shape[dim]) // (drawn.shape[dim] // shards_of)).reshape([-1 if axis == dim else 1 for axis in range(drawn.ndim)]) for dim in (source, target)]
    chosen = jax.random.permutation(stream_key, shards_of)[partner]
    strong = (owner == chosen) | (owner == (partner + shards_of // 2) % shards_of)
    return jnp.where(strong, factor * drawn, drawn)


def block_levels(key, shape, cuts, least, top_value):
    level = 1.0
    for dim, blocks in cuts:
        steps = jax.random.uniform(jax.random.fold_in(jax.random.fold_in(key, 6), dim), (blocks,), jnp.float32, least / len(cuts), top_value / len(cuts))
        level = level * jnp.repeat(jnp.exp(steps), shape[dim] // blocks).reshape((-1,) + (1,) * (len(shape) - 1 - dim))
    return level


def centred(key, extent, scale, most, shards=(), held_as=jnp.bfloat16):
    level = block_levels(key, extent, shards, -0.22, 0.18) if shards else 1.0
    drawn = jax.random.normal(key, extent, jnp.float32) * scale * level
    return jnp.minimum(jnp.maximum(drawn, -most), most).astype(held_as)


def noise_with(own_key, shape, deviation, reach, pieces, heavy, kind=jnp.bfloat16):
    values = deviation * jax.random.normal(own_key, shape, jnp.float32)
    if pieces:
        values = values * block_levels(own_key, shape, pieces, -0.22, 0.18)
    return jnp.clip(with_spikes(values, jax.random.fold_in(own_key, 3), *heavy), -reach, reach).astype(kind)


def setup_inputs(seed: int = 0) -> dict:
    arg_keys = jax.random.split(jax.random.key(seed), 15)
    return {
        "tokens": draw_tokens(jax.random.fold_in(arg_keys[14], 71), 0),
        "lengths": draw_lengths(jax.random.fold_in(arg_keys[14], 71), 0),
        "in_weight": centred(arg_keys[2], (D, 3 * D), D ** -0.5, 0.21875, ((0, 32),)),
        "out_weight": centred(arg_keys[3], (D, D), (max(1, 4 * D // (TOK_DEV * N_FSDP))) ** -0.5, 3.5, ((0, 32),)),
        "out_bias": centred(arg_keys[4], (D,), 0.3, 2.0, ((0, 32),)),
        "norm_gain": jnp.clip(1.0 + 0.1 * jax.random.normal(arg_keys[5], (D,), jnp.float32), 0.5, 1.5).astype(jnp.bfloat16),
        "norm_bias": centred(arg_keys[6], (D,), 0.3, 2.0, ((0, 32),)),
        "up_weight": centred(arg_keys[7], (D, FF), D ** -0.5, 0.21875, ((0, 32),)),
        "up_bias": centred(arg_keys[8], (FF,), 0.5, 3.0, ((0, 32),)),
        "down_weight": centred(arg_keys[9], (FF, D), FF ** -0.5, 0.109375, ((0, 32),)),
        "down_bias": centred(arg_keys[10], (D,), 0.3, 2.0, ((0, 32),)),
        "final_gain": jnp.clip(1.0 + 0.1 * jax.random.normal(arg_keys[11], (D,), jnp.float32), 0.5, 1.5).astype(jnp.bfloat16),
        "final_bias": centred(arg_keys[12], (D,), 0.3, 2.0, ((0, 32),)),
        "cotangent": noise_with(arg_keys[13], (TOKENS, D), 1.0, 6.0, ((0, 32),), (0, 1, 32, 2.75)),
    }


HIGH = lax.Precision.HIGHEST
HALF_PI = math.pi / 2
NORM_EPS = 1e-05

@jax.custom_vjp
def low(v):
    return lax.optimization_barrier(v.astype(jnp.bfloat16)).astype(jnp.float32)

@jax.custom_vjp
def low_back(v):
    return v

def low_keep(v):
    return (low(v), None)

def low_pass(kept, grad):
    return (grad,)

def back_keep(v):
    return (v, None)

def back_low(kept, grad):
    return (low(grad),)
low.defvjp(low_keep, low_pass)
low_back.defvjp(back_keep, back_low)

def documents(position, pair):
    first_len = pair[0]
    doc = (position >= first_len).astype(jnp.int32)
    start = doc * first_len
    span = jnp.where(doc == 0, first_len, pair[1])
    angle = HALF_PI * (position - start).astype(jnp.float32) / span.astype(jnp.float32)
    return (doc, angle)

def features(heads, angle):
    active = jax.nn.softplus(heads)
    return jnp.concatenate([active * jnp.cos(angle)[None, :, None], active * jnp.sin(angle)[None, :, None]], axis=2)

def layer_norm(rows, gain, shift):
    mean = lax.optimization_barrier(jnp.mean(rows, axis=-1, keepdims=True))
    centered = rows - mean
    scale = lax.rsqrt(lax.optimization_barrier(jnp.mean(centered * centered, axis=-1, keepdims=True)) + NORM_EPS)
    return centered * scale * gain + shift

def exact_gelu(values):
    return jax.nn.gelu(values, approximate=False)

def attend_block(carry, block):
    state, norm, carry_doc = carry
    query, keys, values, doc_blk = block
    order = jnp.arange(doc_blk.shape[0], dtype=jnp.int32)
    mask = ((order[None, :] <= order[:, None]) & (doc_blk[None, :] == doc_blk[:, None])).astype(jnp.float32)
    use = (doc_blk == carry_doc).astype(jnp.float32)
    scores = low_back(jnp.einsum('hif,hjf->hij', query, keys, precision=HIGH) * mask[None])
    numer = jnp.einsum('hej,hij->hei', values, low(scores), precision=HIGH)
    numer = numer + use * jnp.einsum('hef,hif->hei', low(state), query, precision=HIGH)
    numer = low_back(numer)
    denom = lax.optimization_barrier(jnp.sum(scores, axis=2)) + use * jnp.einsum('hf,hif->hi', norm, query, precision=HIGH)
    ratio = numer / denom[:, None, :]
    last = doc_blk[-1]
    chosen = (doc_blk == last).astype(jnp.float32)
    picked = keys * chosen[None, :, None]
    block_state = low_back(jnp.einsum('hej,hjf->hef', values, picked, precision=HIGH))
    block_norm = lax.optimization_barrier(jnp.sum(picked, axis=1))
    keep = (carry_doc == last).astype(jnp.float32)
    return ((block_state + keep * state, block_norm + keep * norm, last), ratio)

def layer_group(rows, pair, params):
    inward, outward, out_shift, gain_first, shift_first, upward, up_shift, downward, down_shift, gain_second, shift_second = params
    size = rows.shape[0]
    width = rows.shape[1]
    position = jnp.arange(size, dtype=jnp.int32)
    doc, angle = documents(position, pair)
    projected = low_back(jnp.dot(rows, inward, precision=HIGH))
    query = low(features(projected[:, :width].reshape(size, HEADS, HEAD).transpose(1, 0, 2), angle))
    keys = low(features(projected[:, width:2 * width].reshape(size, HEADS, HEAD).transpose(1, 0, 2), angle))
    values = low(projected[:, 2 * width:].reshape(size, HEADS, HEAD).transpose(1, 2, 0))
    count = size // BLOCK
    blocks = (query.reshape(HEADS, count, BLOCK, 2 * HEAD).transpose(1, 0, 2, 3), keys.reshape(HEADS, count, BLOCK, 2 * HEAD).transpose(1, 0, 2, 3), values.reshape(HEADS, HEAD, count, BLOCK).transpose(2, 0, 1, 3), doc.reshape(count, BLOCK))
    start = (jnp.zeros((HEADS, HEAD, 2 * HEAD), jnp.float32), jnp.zeros((HEADS, 2 * HEAD), jnp.float32), jnp.array(-1, jnp.int32))
    finish, ratios = lax.scan(jax.checkpoint(attend_block), start, blocks)
    attended = low(ratios.transpose(0, 3, 1, 2).reshape(size, width))
    branch = low_back(jnp.dot(attended, outward, precision=HIGH) + out_shift)
    normed = layer_norm(rows + branch, gain_first, shift_first)
    hidden = low_back(jnp.dot(low(normed), upward, precision=HIGH) + up_shift)
    activated = low(exact_gelu(hidden))
    second = low_back(jnp.dot(activated, downward, precision=HIGH) + down_shift)
    return layer_norm(normed + second, gain_second, shift_second)

def reference(tokens, lengths, in_weight, out_weight, out_bias, norm_gain, norm_bias, up_weight, up_bias, down_weight, down_bias, final_gain, final_bias, cotangent):
    params = tuple((item.astype(jnp.float32) for item in (in_weight, out_weight, out_bias, norm_gain, norm_bias, up_weight, up_bias, down_weight, down_bias, final_gain, final_bias)))
    rows = tokens.astype(jnp.float32).reshape(GROUPS, GROUP, D)

    def forward(rows_all, params_all):

        def one(item):
            return jax.checkpoint(layer_group)(item[0], item[1], params_all)
        return lax.map(one, (rows_all, lengths))
    result, pull = jax.vjp(forward, rows, params)
    grad_rows, grads = pull(cotangent.astype(jnp.float32).reshape(GROUPS, GROUP, D))
    return (result.reshape(TOKENS, D).astype(jnp.bfloat16), grad_rows.reshape(TOKENS, D), grads[0], grads[1], grads[2], grads[3], grads[4], grads[5], grads[6], grads[7], grads[8], grads[9], grads[10])
```

```python
from functools import partial
import math

import jax
import jax.numpy as jnp
from jax import lax
from jax.experimental import pallas as pl
from jax.experimental.pallas import tpu as pltpu
from jax.sharding import PartitionSpec as P

HEADS = 12
HEAD = 64
BLOCK = 512


HALF_PI = math.pi / 2
NORM_EPS = 1e-05

def prefix(shard, axis, combine, identity, reverse):
    devices, position = (lax.axis_size(axis), lax.axis_index(axis))
    everything = jax.tree.map(lambda part: lax.all_gather(part, axis), shard)
    start = jax.tree.map(
        lambda part, zero: jnp.broadcast_to(jnp.asarray(zero, part.dtype), part.shape),
        shard,
        identity,
    )

    def turn(k, before):
        at = devices - 1 - k if reverse else k
        reached = at > position if reverse else at < position
        new = combine(before, jax.tree.map(lambda part: part[at], everything))
        return jax.tree.map(lambda a, b: jnp.where(reached, a, b), new, before)

    return lax.fori_loop(0, devices, turn, start)


def documents(position, pair):
    first_len = pair[0]
    doc = (position >= first_len).astype(jnp.int32)
    start = doc * first_len
    span = jnp.where(doc == 0, first_len, pair[1])
    angle = HALF_PI * (position - start).astype(jnp.float32) / span.astype(jnp.float32)
    return (doc, angle)


def features(heads, angle):
    active = jax.nn.softplus(heads)
    return jnp.concatenate(
        [active * jnp.cos(angle)[None, :, None], active * jnp.sin(angle)[None, :, None]], axis=2
    )


def layer_norm(rows, gain, shift):
    mean = jnp.mean(rows, axis=-1, keepdims=True)
    centered = rows - mean
    scale = lax.rsqrt(jnp.mean(centered * centered, axis=-1, keepdims=True) + NORM_EPS)
    return centered * scale * gain + shift


def exact_gelu(values):
    return jax.nn.gelu(values, approximate=False)


def merge_state(earlier, later):
    return (
        later[0] + later[2] * earlier[0],
        later[1] + later[2] * earlier[1],
        later[2] * earlier[2],
    )


def block_forward(query, keys, values, doc_blk, state, norm, carry_doc):
    order = jnp.arange(doc_blk.shape[0], dtype=jnp.int32)
    mask = (order[None, :] <= order[:, None]) & (doc_blk[None, :] == doc_blk[:, None])
    raw = jnp.einsum("hif,hjf->hij", query, keys, preferred_element_type=jnp.float32)
    scores = jnp.where(mask[None], raw, 0.0)
    use = (doc_blk == carry_doc).astype(jnp.float32)
    carried = jnp.einsum(
        "hef,hif->hei", state.astype(jnp.bfloat16), query, preferred_element_type=jnp.float32
    )
    numer = (
        jnp.einsum(
            "hej,hij->hei", values, scores.astype(jnp.bfloat16), preferred_element_type=jnp.float32
        )
        + use * carried
    )
    denom = jnp.sum(scores, axis=2) + use * jnp.einsum(
        "hf,hif->hi", norm, query.astype(jnp.float32)
    )
    return (mask, scores, use, numer, denom)


def block_summary(keys, values, doc_blk):
    chosen = doc_blk == doc_blk[-1]
    picked = jnp.where(chosen[None, :, None], keys, jnp.zeros((), keys.dtype))
    state = jnp.einsum("hej,hjf->hef", values, picked, preferred_element_type=jnp.float32)
    norm = jnp.sum(picked.astype(jnp.float32), axis=1)
    return (chosen, picked, state, norm)


def per_device(
    tokens,
    lengths,
    in_weight,
    out_weight,
    out_bias,
    norm_gain,
    norm_bias,
    up_weight,
    up_bias,
    down_weight,
    down_bias,
    final_gain,
    final_bias,
    cotangent,
):
    rows = tokens.shape[0]
    width = tokens.shape[1]
    count = rows // BLOCK
    gathered = (
        lax.all_gather(in_weight, ("dp", "fsdp"), axis=0, tiled=True),
        lax.all_gather(out_weight, ("dp", "fsdp"), axis=0, tiled=True),
        lax.all_gather(out_bias, ("dp", "fsdp"), axis=0, tiled=True),
        lax.all_gather(norm_gain, ("dp", "fsdp"), axis=0, tiled=True),
        lax.all_gather(norm_bias, ("dp", "fsdp"), axis=0, tiled=True),
        lax.all_gather(up_weight, ("dp", "fsdp"), axis=0, tiled=True),
        lax.all_gather(up_bias, ("dp", "fsdp"), axis=0, tiled=True),
        lax.all_gather(down_weight, ("dp", "fsdp"), axis=0, tiled=True),
        lax.all_gather(down_bias, ("dp", "fsdp"), axis=0, tiled=True),
        lax.all_gather(final_gain, ("dp", "fsdp"), axis=0, tiled=True),
        lax.all_gather(final_bias, ("dp", "fsdp"), axis=0, tiled=True),
    )
    (
        inward,
        outward,
        out_shift,
        gain_first,
        shift_first,
        upward,
        up_shift,
        downward,
        down_shift,
        gain_second,
        shift_second,
    ) = gathered
    first = lax.axis_index("fsdp") * rows
    position = first + jnp.arange(rows, dtype=jnp.int32)
    pair = lengths[0]
    doc, angle = documents(position, pair)
    prior_doc = jnp.where(first > 0, (first - 1 >= pair[0]).astype(jnp.int32), -1)
    projected = jnp.dot(tokens, inward, preferred_element_type=jnp.float32)
    query_raw = projected[:, :width].reshape(rows, HEADS, HEAD).transpose(1, 0, 2)
    key_raw = projected[:, width : 2 * width].reshape(rows, HEADS, HEAD).transpose(1, 0, 2)
    query_feat, query_pull = jax.vjp(partial(features, angle=angle), query_raw)
    key_feat, key_pull = jax.vjp(partial(features, angle=angle), key_raw)
    query = query_feat.astype(jnp.bfloat16)
    keys = key_feat.astype(jnp.bfloat16)
    values = (
        projected[:, 2 * width :].reshape(rows, HEADS, HEAD).transpose(1, 2, 0).astype(jnp.bfloat16)
    )
    device_summary = block_summary(keys, values, doc)
    device_keep = (prior_doc == doc[-1]).astype(jnp.float32)
    identity = (
        jnp.zeros_like(device_summary[2]),
        jnp.zeros_like(device_summary[3]),
        jnp.ones((), jnp.float32),
    )
    state, norm, passed = prefix(
        (device_summary[2], device_summary[3], device_keep), "fsdp", merge_state, identity, False
    )
    keys_blk = keys
    values_blk = values
    doc_blk = doc
    carries = [(state, norm, prior_doc)]
    outcome = block_forward(query, keys_blk, values_blk, doc_blk, state, norm, prior_doc)
    ratios = outcome[3] / outcome[4][:, None, :]
    summary = block_summary(keys_blk, values_blk, doc_blk)
    attended = ratios.transpose(2, 0, 1).reshape(rows, width).astype(jnp.bfloat16)
    branch = jnp.dot(attended, outward, preferred_element_type=jnp.float32) + out_shift.astype(
        jnp.float32
    )
    first_sum = tokens.astype(jnp.float32) + branch
    normed, first_pull = jax.vjp(
        layer_norm, first_sum, gain_first.astype(jnp.float32), shift_first.astype(jnp.float32)
    )
    normed_low = normed.astype(jnp.bfloat16)
    hidden = jnp.dot(normed_low, upward, preferred_element_type=jnp.float32) + up_shift.astype(
        jnp.float32
    )
    activated, gelu_pull = jax.vjp(exact_gelu, hidden)
    activated_low = activated.astype(jnp.bfloat16)
    second_sum = (
        normed
        + jnp.dot(activated_low, downward, preferred_element_type=jnp.float32)
        + down_shift.astype(jnp.float32)
    )
    result, second_pull = jax.vjp(
        layer_norm, second_sum, gain_second.astype(jnp.float32), shift_second.astype(jnp.float32)
    )
    again = (
        lax.all_gather(in_weight, ("dp", "fsdp"), axis=0, tiled=True),
        lax.all_gather(out_weight, ("dp", "fsdp"), axis=0, tiled=True),
        lax.all_gather(out_bias, ("dp", "fsdp"), axis=0, tiled=True),
        lax.all_gather(norm_gain, ("dp", "fsdp"), axis=0, tiled=True),
        lax.all_gather(norm_bias, ("dp", "fsdp"), axis=0, tiled=True),
        lax.all_gather(up_weight, ("dp", "fsdp"), axis=0, tiled=True),
        lax.all_gather(up_bias, ("dp", "fsdp"), axis=0, tiled=True),
        lax.all_gather(down_weight, ("dp", "fsdp"), axis=0, tiled=True),
        lax.all_gather(down_bias, ("dp", "fsdp"), axis=0, tiled=True),
        lax.all_gather(final_gain, ("dp", "fsdp"), axis=0, tiled=True),
        lax.all_gather(final_bias, ("dp", "fsdp"), axis=0, tiled=True),
    )
    inward = again[0]
    outward = again[1]
    upward = again[5]
    downward = again[7]
    second_grad, final_gain_grad, final_shift_grad = second_pull(cotangent.astype(jnp.float32))
    down_grad = second_grad.astype(jnp.bfloat16)
    down_weight_grad = jnp.dot(activated_low.T, down_grad, preferred_element_type=jnp.float32)
    down_shift_grad = jnp.sum(down_grad.astype(jnp.float32), axis=0)
    (activated_grad,) = gelu_pull(
        jnp.dot(down_grad, downward.T, preferred_element_type=jnp.float32)
    )
    hidden_grad = activated_grad.astype(jnp.bfloat16)
    up_weight_grad = jnp.dot(normed_low.T, hidden_grad, preferred_element_type=jnp.float32)
    up_shift_grad = jnp.sum(hidden_grad.astype(jnp.float32), axis=0)
    normed_grad = second_grad + jnp.dot(hidden_grad, upward.T, preferred_element_type=jnp.float32)
    first_grad, norm_gain_grad, norm_shift_grad = first_pull(normed_grad)
    branch_grad = first_grad.astype(jnp.bfloat16)
    out_weight_grad = jnp.dot(attended.T, branch_grad, preferred_element_type=jnp.float32)
    out_shift_grad = jnp.sum(branch_grad.astype(jnp.float32), axis=0)
    attended_grad = jnp.dot(branch_grad, outward.T, preferred_element_type=jnp.float32)
    ratio_grad = attended_grad.reshape(rows, HEADS, HEAD).transpose(1, 2, 0)
    index = 0
    keys_blk = keys
    values_blk = values
    doc_blk = doc
    state_in, norm_in, doc_in = carries[index]
    mask, scores, use, numer, denom = block_forward(
        query, keys_blk, values_blk, doc_blk, state_in, norm_in, doc_in
    )
    numer_grad = (ratio_grad / denom[:, None, :]).astype(jnp.bfloat16)
    denom_grad = -jnp.sum(ratio_grad * numer, axis=1) / (denom * denom)
    scores_grad = (
        jnp.einsum("hei,hej->hij", numer_grad, values_blk, preferred_element_type=jnp.float32)
        + denom_grad[:, :, None]
    )
    scores_grad = jnp.where(mask[None], scores_grad, 0.0).astype(jnp.bfloat16)
    used_numer = jnp.where(use[None, None, :] > 0, numer_grad, jnp.zeros((), jnp.bfloat16))
    used_denom = use * denom_grad
    query_part = jnp.einsum(
        "hij,hjf->hif", scores_grad, keys_blk, preferred_element_type=jnp.float32
    )
    query_part = query_part + jnp.einsum(
        "hei,hef->hif",
        used_numer,
        state_in.astype(jnp.bfloat16),
        preferred_element_type=jnp.float32,
    )
    query_grads = query_part + used_denom[:, :, None] * norm_in[:, None, :]
    key_grads = [jnp.einsum("hij,hif->hjf", scores_grad, query, preferred_element_type=jnp.float32)]
    value_grads = [
        jnp.einsum(
            "hei,hij->hej",
            numer_grad,
            scores.astype(jnp.bfloat16),
            preferred_element_type=jnp.float32,
        )
    ]
    contribs = [
        (
            jnp.einsum("hei,hif->hef", used_numer, query, preferred_element_type=jnp.float32),
            jnp.einsum("hi,hif->hf", used_denom, query.astype(jnp.float32)),
        )
    ]
    keeps = [(doc_in == doc_blk[-1]).astype(jnp.float32)]
    local_state = jnp.zeros_like(device_summary[2])
    local_norm = jnp.zeros_like(device_summary[3])
    for index in reversed(range(count)):
        local_state = contribs[index][0] + keeps[index] * local_state
        local_norm = contribs[index][1] + keeps[index] * local_norm
    leave_state, leave_norm, through = prefix(
        (local_state, local_norm, device_keep), "fsdp", merge_state, identity, True
    )
    for index in reversed(range(count)):
        keys_blk = keys
        values_blk = values
        doc_blk = doc
        summary = block_summary(keys_blk, values_blk, doc_blk)
        state_low = leave_state.astype(jnp.bfloat16)
        key_extra = (
            jnp.einsum("hej,hef->hjf", values_blk, state_low, preferred_element_type=jnp.float32)
            + leave_norm[:, None, :]
        )
        key_grads[index] = key_grads[index] + jnp.where(summary[0][None, :, None], key_extra, 0.0)
        value_grads[index] = value_grads[index] + jnp.einsum(
            "hef,hjf->hej", state_low, summary[1], preferred_element_type=jnp.float32
        )
        leave_state = contribs[index][0] + keeps[index] * leave_state
        leave_norm = contribs[index][1] + keeps[index] * leave_norm
    (query_raw_grad,) = query_pull(query_grads)
    (key_raw_grad,) = key_pull(key_grads[0])
    value_grad = value_grads[0].transpose(2, 0, 1).reshape(rows, width)
    projected_grad = jnp.concatenate(
        [
            query_raw_grad.transpose(1, 0, 2).reshape(rows, width),
            key_raw_grad.transpose(1, 0, 2).reshape(rows, width),
            value_grad,
        ],
        axis=1,
    ).astype(jnp.bfloat16)
    in_weight_grad = jnp.dot(tokens.T, projected_grad, preferred_element_type=jnp.float32)
    tokens_grad = first_grad + jnp.dot(projected_grad, inward.T, preferred_element_type=jnp.float32)
    summed = (
        lax.psum_scatter(in_weight_grad, ("dp", "fsdp"), scatter_dimension=0, tiled=True),
        lax.psum_scatter(out_weight_grad, ("dp", "fsdp"), scatter_dimension=0, tiled=True),
        lax.psum_scatter(out_shift_grad, ("dp", "fsdp"), scatter_dimension=0, tiled=True),
        lax.psum_scatter(norm_gain_grad, ("dp", "fsdp"), scatter_dimension=0, tiled=True),
        lax.psum_scatter(norm_shift_grad, ("dp", "fsdp"), scatter_dimension=0, tiled=True),
        lax.psum_scatter(up_weight_grad, ("dp", "fsdp"), scatter_dimension=0, tiled=True),
        lax.psum_scatter(up_shift_grad, ("dp", "fsdp"), scatter_dimension=0, tiled=True),
        lax.psum_scatter(down_weight_grad, ("dp", "fsdp"), scatter_dimension=0, tiled=True),
        lax.psum_scatter(down_shift_grad, ("dp", "fsdp"), scatter_dimension=0, tiled=True),
        lax.psum_scatter(final_gain_grad, ("dp", "fsdp"), scatter_dimension=0, tiled=True),
        lax.psum_scatter(final_shift_grad, ("dp", "fsdp"), scatter_dimension=0, tiled=True),
    )
    return (result.astype(jnp.bfloat16), tokens_grad) + tuple(summed)


MESH = pl.DeviceIdType.MESH
F32 = jnp.float32
BF16 = jnp.bfloat16
ROWS = 512
WIDTH = 768
FF = 3072
HALF = 1536
GATHER_ORDER = ("zyx", "zxy", "xzy", "yzx")
REDUCE_ORDER = ("xyz", "yxz", "yzx", "xzy")


def dot(a, b, ca, cb):
    return lax.dot_general(a, b, (((ca,), (cb,)), ((), ())), preferred_element_type=F32)


class Place:
    def __init__(self):
        self.dp = lax.axis_index("dp")
        self.c = lax.axis_index("fsdp")
        self.x = lax.rem(self.dp, 2)
        self.y = lax.rem(lax.div(self.dp, 2), 2)
        self.z = lax.div(self.dp, 4)

    def peer(self, d, k=1):
        if d == "x":
            return (self.dp + 1 - 2 * self.x, self.c)
        if d == "y":
            return (self.dp + 2 - 4 * self.y, self.c)
        if d == "z":
            return (lax.rem(self.dp + 4 * k, 16), self.c)
        if d == "up":
            return (self.dp + 4, self.c)
        if d == "down":
            return (self.dp - 4, self.c)
        return (self.dp, 1 - self.c)

    def at(self, known, flip=None, z=None):
        out = []
        for d in "zyx":
            if d in known:
                out.append(slice(None))
                continue
            v = getattr(self, d)
            if flip == d:
                v = 1 - v
            if d == "z" and z is not None:
                v = z
            out.append(v)
        return tuple(out)


def remote(src, dst, send, recv, to):
    return pltpu.make_async_remote_copy(
        src_ref=src, dst_ref=dst, send_sem=send, recv_sem=recv, device_id=to, device_id_type=MESH
    )


def guarded(cond, action):
    if cond is None:
        action()
    else:
        pl.when(cond)(action)


class Sends:
    def __init__(self, sems, size):
        self.sems, self.size, self.count, self.open = sems, size, 0, {}

    def start(self, make, cond=None):
        i = self.count % self.size
        self.count += 1
        self.wait(i)
        guarded(cond, lambda: make(self.sems.at[i]).start())
        self.open[i] = (cond, make)
        return i, make

    def wait(self, i):
        if i in self.open:
            cond, make = self.open.pop(i)
            guarded(cond, lambda: make(self.sems.at[i]).wait_send())

    def left(self, handle):
        if self.open.get(handle[0], (None, None))[1] is handle[1]:
            self.wait(handle[0])

    def now_open(self):
        return [(i, make) for i, (_, make) in self.open.items()]

    def finish(self):
        for i in list(self.open):
            self.wait(i)


class Gather:
    def __init__(self, place, units, view, sends, sems):
        self.p, self.units, self.view, self.sends, self.sems = place, units, view, sends, sems
        self.waited = set()

    def order(self, u):
        return GATHER_ORDER[self.units[u][1]]

    def copy(self, u, slot, blocks, to):
        src = self.view(u, blocks, self.p.c)
        return lambda sem: remote(src, src, sem, self.sems.at[10 * u + slot], to)

    def issue(self, u, ph, hop):
        p, o = self.p, self.order(u)
        known, d = o[:ph], o[ph]
        if hop == 1 and ph > 0:
            self.arrive(u, ph - 1)
        if d != "z":
            self.sends.start(self.copy(u, "xy".index(d), p.at(known), p.peer(d)))
            return
        if hop > 1:
            self.arrive_hop(u, ph, hop - 1)
        up = (jnp.logical_and(p.z < 3, p.z - (hop - 1) >= 0), p.z - (hop - 1), p.peer("up"))
        down = (jnp.logical_and(p.z > 0, p.z + (hop - 1) <= 3), p.z + (hop - 1), p.peer("down"))
        for way, (cond, z, to) in enumerate((up, down)):
            self.sends.start(self.copy(u, 1 + 3 * way + hop, p.at(known, z=z), to), cond)

    def expect(self, u, slot, blocks, core):
        dst = self.view(u, blocks, core)
        remote(dst, dst, self.sems.at[10 * u + slot], self.sems.at[10 * u + slot], self.p.peer("core")).wait_recv()

    def arrive_hop(self, u, ph, hop):
        if (u, ph, hop) in self.waited:
            return
        self.waited.add((u, ph, hop))
        p, known = self.p, self.order(u)[:ph]
        for way, (cond, z) in enumerate(((p.z - hop >= 0, p.z - hop), (p.z + hop <= 3, p.z + hop))):
            slot, blocks = 1 + 3 * way + hop, p.at(known, z=z)
            guarded(cond, lambda slot=slot, blocks=blocks: self.expect(u, slot, blocks, p.c))

    def arrive(self, u, ph):
        p, o = self.p, self.order(u)
        known, d = o[:ph], o[ph]
        if d == "z":
            for hop in (1, 2, 3):
                self.arrive_hop(u, ph, hop)
        elif (u, ph, 0) not in self.waited:
            self.waited.add((u, ph, 0))
            self.expect(u, "xy".index(d), p.at(known, flip=d), p.c)

    def shared(self, u, part):
        o = self.order(u)
        return self.p.at(o[:2], flip=o[2] if part else None)

    def share(self, u, part):
        self.arrive(u, 1 + part)
        self.sends.start(self.copy(u, 8 + part, self.shared(u, part), self.p.peer("core")))

    def ready(self, u):
        if (u, 0) not in self.waited:
            self.waited.add((u, 0))
            for part in (0, 1):
                self.expect(u, 8 + part, self.shared(u, part), 1 - self.p.c)


class Reduce:
    def __init__(self, place, units, blocks, landing, final, sends, sems):
        self.p, self.units = place, units
        self.blocks, self.landing, self.final = blocks, landing, final
        self.sends, self.sems = sends, sems

    def plan(self, u, ph):
        arr, kind, r0, nr, c0, nc = self.units[u]
        o = REDUCE_ORDER[kind]
        return arr, o[ph], o[ph + 1 :], (pl.ds(r0, nr), pl.ds(c0, nc))

    def moves(self, u, ph):
        p = self.p
        arr, d, left, cut = self.plan(u, ph)
        land = self.landing[arr][min(ph, 1)]
        if d != "z":
            lead = {0: (slice(None), slice(None)), 1: (pl.ds(0, 4),), 2: (6,)}[ph]
            return [(self.sems.at[5 * u + "xy".index(d)], p.at(left, flip=d), p.peer(d), land.at[lead + cut])]
        out = []
        for k in (1, 2, 3):
            lead = (pl.ds(2 * (k - 1), 2),) if ph == 1 else (3 + k,)
            blocks = p.at(left, z=lax.rem(p.z + k, 4))
            out.append((self.sems.at[5 * u + 1 + k], blocks, p.peer("z", k), land.at[lead + cut]))
        return out

    def send(self, u, ph):
        arr, _, _, cut = self.plan(u, ph)
        for sem, sel, to, dst in self.moves(u, ph):
            src = self.blocks[arr].at[sel + cut]
            self.sends.start(lambda send, src=src, dst=dst, sem=sem, to=to: remote(src, dst, send, sem, to))

    def add(self, u, ph):
        p = self.p
        arr, d, left, cut = self.plan(u, ph)
        for sem, _, to, dst in self.moves(u, ph):
            remote(dst, dst, sem, sem, to).wait_recv()
        ref, land = self.blocks[arr], self.landing[arr][min(ph, 1)]
        if ph == 2:
            total = ref[p.at("") + cut].astype(F32)
            for k in (4, 5, 6) if d == "z" else (6,):
                total = total + land[(k,) + cut].astype(F32)
            self.final[arr][cut] = total
            return
        for n in range({0: 8, 1: 4 if d != "z" else 2}[ph]):
            idx = {"z": p.z, "y": p.y, "x": p.x}
            if ph == 0:
                lead, other = divmod(n, 2), left.replace("z", "")
                idx["z"], idx[other] = lead
                leads = [lead]
            else:
                idx[left] = n
                leads = [(n,)] if d != "z" else [(2 * k + n,) for k in range(3)]
            sel = (idx["z"], idx["y"], idx["x"]) + cut
            total = ref[sel].astype(F32)
            for lead in leads:
                total = total + land[lead + cut].astype(F32)
            ref[sel] = total.astype(ref.dtype)


IN_OUT, UP, DOWN, SMALL = range(4)
STEP, ISSUE, SHARE = range(3)
SENDS = 48

GATHER_UNITS = [
    (3, 2, 0, 8, 0, 128), (0, 0, 0, 48, 0, 384), (0, 1, 0, 48, 384, 384), (0, 2, 0, 48, 768, 384), (0, 3, 0, 48, 1152, 384),
    (1, 0, 0, 48, 0, 128), (1, 1, 0, 48, 256, 128), (1, 2, 0, 48, 512, 256), (1, 3, 0, 48, 1024, 256), (1, 0, 0, 48, 128, 128),
    (1, 1, 0, 48, 384, 128), (1, 2, 0, 48, 768, 256), (1, 3, 0, 48, 1280, 256), (2, 2, 0, 32, 0, 256), (2, 3, 0, 32, 256, 256),
    (2, 0, 0, 32, 512, 128), (2, 1, 0, 32, 640, 128), (2, 2, 32, 32, 0, 256), (2, 3, 32, 32, 256, 256),
    (2, 0, 32, 32, 512, 128), (2, 1, 32, 32, 640, 128), (2, 2, 64, 32, 0, 256), (2, 3, 64, 32, 256, 256),
    (2, 0, 64, 32, 512, 128), (2, 1, 64, 32, 640, 128),
]
GATHER_PLAN = [
    (1, 19, 0, 1), (1, 20, 0, 1), (1, 22, 0, 1), (1, 18, 0, 1), (1, 23, 0, 1), (1, 21, 0, 1), (1, 17, 0, 1), (1, 15, 0, 1),
    (1, 24, 0, 1), (1, 16, 0, 1), (1, 19, 0, 2), (0, 0, ()), (1, 1, 0, 1), (1, 2, 0, 1), (1, 4, 0, 1), (1, 16, 0, 2),
    (1, 13, 0, 1), (1, 15, 0, 2), (1, 11, 0, 1), (1, 10, 0, 1), (1, 19, 0, 3), (1, 9, 0, 1), (1, 19, 1, 1), (1, 14, 0, 1),
    (1, 23, 0, 2), (1, 1, 0, 2), (1, 3, 0, 1), (1, 0, 0, 1), (1, 12, 0, 1), (1, 2, 0, 2), (1, 16, 0, 3), (1, 8, 0, 1),
    (1, 16, 1, 1), (1, 10, 0, 2), (1, 23, 0, 3), (1, 9, 0, 2), (1, 19, 2, 1), (1, 15, 0, 3), (1, 24, 0, 2), (1, 1, 0, 3),
    (1, 23, 1, 1), (1, 7, 0, 1), (1, 2, 0, 3), (1, 3, 1, 1), (1, 4, 1, 1), (1, 15, 1, 1), (1, 6, 0, 1), (1, 10, 0, 3),
    (1, 9, 0, 3), (1, 1, 1, 1), (1, 2, 1, 1), (1, 16, 2, 1), (1, 24, 0, 3), (1, 23, 2, 1), (1, 10, 1, 1), (1, 9, 1, 1),
    (1, 0, 1, 1), (1, 7, 1, 1), (1, 2, 2, 1), (1, 24, 1, 1), (2, 19, 0), (1, 5, 0, 1), (1, 3, 1, 2), (1, 20, 0, 2),
    (1, 1, 2, 1), (1, 4, 1, 2), (0, 1, ()), (1, 3, 1, 3), (1, 6, 0, 2), (1, 4, 1, 3), (1, 11, 1, 1), (1, 12, 1, 1), (2, 24, 0),
    (1, 13, 1, 1), (1, 3, 2, 1), (2, 16, 0), (1, 5, 0, 2), (1, 14, 1, 1), (2, 23, 1), (1, 20, 0, 3), (1, 0, 1, 2), (1, 4, 2, 1),
    (1, 6, 0, 3), (1, 10, 2, 1), (2, 2, 0), (2, 1, 0), (2, 3, 0), (2, 1, 1), (2, 10, 0), (1, 7, 1, 2), (1, 0, 1, 3),
    (1, 0, 2, 1), (1, 5, 0, 3), (2, 15, 0), (1, 7, 1, 3), (1, 14, 1, 2), (1, 12, 1, 2), (1, 6, 1, 1), (2, 4, 0), (2, 2, 1),
    (1, 17, 1, 1), (1, 5, 1, 1), (1, 15, 2, 1), (2, 9, 0), (2, 3, 1), (1, 8, 1, 1), (1, 14, 1, 3), (2, 4, 1), (1, 20, 1, 1),
    (1, 13, 1, 2), (1, 7, 2, 1), (2, 6, 0), (1, 11, 1, 2), (1, 9, 2, 1), (0, 3, (1, 2, 3, 4)), (1, 14, 2, 1), (0, 4, ()),
    (1, 6, 2, 1), (1, 5, 2, 1), (1, 13, 1, 3), (1, 22, 1, 1), (0, 5, ()), (1, 8, 1, 2), (1, 12, 1, 3), (1, 13, 2, 1), (2, 0, 0),
    (1, 20, 2, 1), (2, 0, 1), (1, 21, 1, 1), (2, 14, 0), (2, 16, 1), (0, 6, ()), (2, 9, 1), (2, 13, 0), (1, 17, 1, 2),
    (2, 7, 0), (0, 2, (0,)), (1, 11, 1, 3), (2, 10, 1), (1, 8, 1, 3), (1, 18, 1, 1), (1, 12, 2, 1), (2, 12, 0), (0, 7, ()),
    (1, 17, 1, 3), (0, 8, ()), (1, 22, 1, 2), (1, 11, 2, 1), (0, 9, ()), (2, 6, 1), (1, 8, 2, 1), (1, 21, 1, 2), (0, 10, ()),
    (2, 5, 0), (2, 7, 1), (0, 11, ()), (2, 8, 0), (1, 22, 1, 3), (0, 12, ()), (1, 18, 1, 2), (2, 17, 0), (1, 21, 1, 3),
    (2, 12, 1), (2, 11, 0), (2, 19, 1), (2, 5, 1), (1, 17, 2, 1), (2, 20, 1), (1, 22, 2, 1), (0, 13, ()), (1, 18, 1, 3),
    (2, 21, 0), (1, 21, 2, 1), (2, 11, 1), (2, 13, 1), (2, 20, 0), (0, 14, (5, 6, 9, 10)), (2, 8, 1), (1, 18, 2, 1),
    (1, 24, 2, 1), (2, 14, 1), (0, 15, (7, 11)), (2, 22, 0), (0, 16, (8, 12)), (2, 17, 1), (0, 17, ()), (2, 18, 0), (0, 18, ()),
    (2, 23, 0), (2, 22, 1), (2, 21, 1), (0, 19, ()), (2, 15, 1), (2, 18, 1), (2, 24, 1), (0, 20, (13, 17, 21)),
    (0, 21, (14, 18, 22)), (0, 22, (15, 16, 19, 20, 23, 24)),
]
REDUCE_UNITS = [
    (2, 0, 0, 96, 0, 128), (2, 2, 0, 96, 128, 128), (2, 0, 0, 96, 256, 128), (2, 1, 0, 96, 384, 128), (2, 1, 0, 96, 512, 128),
    (2, 3, 0, 96, 640, 128), (1, 0, 0, 48, 0, 128), (1, 1, 0, 48, 128, 256), (1, 2, 0, 48, 384, 128), (1, 0, 0, 48, 512, 256),
    (1, 1, 0, 48, 768, 128), (1, 2, 0, 48, 896, 128), (1, 0, 0, 48, 1024, 128), (1, 1, 0, 48, 1152, 128),
    (1, 3, 0, 48, 1280, 256), (1, 0, 0, 48, 2688, 128), (1, 1, 0, 48, 2816, 128), (1, 2, 0, 48, 2944, 128),
    (1, 0, 0, 48, 1536, 256), (1, 1, 0, 48, 1792, 128), (1, 0, 0, 48, 1920, 128), (1, 1, 0, 48, 2048, 128),
    (1, 2, 0, 48, 2176, 128), (1, 0, 0, 48, 2304, 256), (1, 1, 0, 48, 2560, 128), (3, 3, 0, 8, 0, 128),
]
REDUCE_GROUP = [
    0, 0, 0, 0, 0, 0, 1, 1, 1, 1, 1, 1, 1, 1, 1, 2, 2, 2, 3, 3, 3, 3, 3, 3, 3, 4,
]
REDUCE_PLAN = [
    (0, 23), (0, 27), (0, 28), (0, 29), (0, 24), (1, 1, 0), (1, 0, 0), (0, 30), (0, 31), (0, 25), (1, 3, 0), (0, 32), (0, 26),
    (1, 5, 0), (0, 33), (0, 34), (0, 35), (2, 1, 0), (1, 2, 0), (1, 1, 1), (0, 36), (1, 8, 0), (0, 37), (1, 11, 0), (0, 38),
    (2, 0, 0), (1, 14, 0), (2, 5, 0), (1, 5, 1), (1, 0, 1), (1, 4, 0), (0, 39), (1, 9, 0), (0, 42), (2, 11, 0), (0, 43),
    (1, 11, 1), (2, 3, 0), (2, 2, 0), (0, 44), (2, 8, 0), (1, 8, 1), (0, 45), (1, 17, 0), (1, 16, 0), (2, 14, 0), (1, 14, 1),
    (0, 46), (1, 3, 1), (2, 4, 0), (1, 4, 1), (0, 47), (1, 10, 0), (1, 15, 0), (2, 0, 1), (2, 17, 0), (2, 9, 0), (1, 12, 0),
    (1, 9, 1), (1, 6, 0), (1, 17, 1), (2, 8, 1), (0, 48), (2, 16, 0), (1, 0, 2), (1, 13, 0), (2, 3, 1), (0, 49), (0, 50),
    (1, 3, 2), (1, 2, 1), (0, 51), (0, 52), (1, 7, 0), (2, 9, 1), (1, 9, 2), (2, 10, 0), (1, 16, 1), (2, 4, 1), (2, 13, 0),
    (2, 12, 0), (1, 13, 1), (2, 17, 1), (0, 40), (1, 4, 2), (1, 10, 1), (2, 15, 0), (0, 53), (2, 11, 1), (1, 15, 1), (1, 12, 1),
    (1, 18, 0), (2, 2, 1), (1, 2, 2), (2, 16, 1), (2, 9, 2), (2, 1, 1), (0, 54), (1, 16, 2), (2, 6, 0), (2, 10, 1), (2, 13, 1),
    (0, 41), (1, 6, 1), (1, 22, 0), (1, 25, 0), (2, 14, 1), (0, 55), (2, 7, 0), (1, 7, 1), (1, 13, 2), (2, 15, 1), (1, 10, 2),
    (1, 24, 0), (2, 12, 1), (1, 21, 0), (1, 15, 2), (1, 12, 2), (1, 23, 0), (2, 6, 1), (2, 25, 0), (1, 6, 2), (2, 2, 2),
    (2, 0, 2), (2, 16, 2), (2, 22, 0), (2, 18, 0), (1, 25, 1), (2, 7, 1), (1, 22, 1), (1, 7, 2), (1, 18, 1), (2, 24, 0),
    (1, 20, 0), (1, 19, 0), (2, 21, 0), (2, 25, 1), (1, 24, 1), (1, 21, 1), (0, 56), (2, 10, 2), (2, 23, 0), (2, 12, 2),
    (1, 23, 1), (2, 18, 1), (1, 18, 2), (2, 5, 1), (0, 57), (2, 24, 1), (2, 22, 1), (1, 25, 2), (2, 20, 0), (1, 24, 2),
    (2, 15, 2), (2, 19, 0), (1, 20, 1), (1, 19, 1), (1, 11, 2), (2, 21, 1), (1, 21, 2), (1, 14, 2), (1, 1, 2), (2, 13, 2),
    (2, 4, 2), (1, 5, 2), (0, 58), (2, 23, 1), (1, 23, 2), (2, 24, 2), (1, 17, 2), (2, 19, 1), (2, 6, 2), (2, 11, 2),
    (2, 20, 1), (2, 3, 2), (1, 19, 2), (1, 8, 2), (2, 14, 2), (2, 18, 2), (1, 22, 2), (2, 7, 2), (2, 21, 2), (2, 1, 2),
    (1, 20, 2), (2, 19, 2), (2, 5, 2), (2, 17, 2), (2, 25, 2), (2, 8, 2), (2, 23, 2), (2, 22, 2), (2, 20, 2),
]


def whole_layer(*refs):
    (
        tokens_in, lengths, cot_in, in_w, out_w, up_w, down_w, b0, b1, b2, b3, b4, b5, b6,
        result, tokens_grad, in_g, out_g, up_g, down_g, small_g,
        WQ, WU, WD, stage_s, stage_r, SP, PV, UB, TS, SIG, QF, KF, VX, SES, SER, LER,
        MSK, CS, USE, LAST, RD, ATT, ATS, N1, S1, F1, NL, NLS, ACT, GP, AT, ATS2, DG, DGS, HGS,
        BG, BGS, PGS, OUT, RB0D, RB1D, RB0W, RB1W, FD, FW, SG, SGR, RB0S, RB1S, FS,
        VEC, HID, tokens, cot, send_sems, gather_sems, reduce_sems, core_sems, hbm, load_sems,
    ) = refs
    p = Place()
    c = p.c

    W5 = {IN_OUT: WQ.reshape(4, 2, 2, 48, FF), UP: WU.reshape(4, 2, 2, 48, FF)}
    WD6 = WD.reshape(4, 2, 2, 2, 96, WIDTH)
    AT4 = AT.reshape(16, 2, 96, ROWS)
    ATS3 = ATS2.reshape(16, 96, ROWS)
    DW = ACT.reshape(2048, WIDTH)

    def gather_view(u, blocks, core):
        arr, _, r0, nr, c0, nc = GATHER_UNITS[u]
        if arr == SMALL:
            return SP.at[blocks + (core,)]
        if arr == DOWN:
            return WD6.at[blocks + (core, pl.ds(r0, nr), pl.ds(c0, nc))]
        return W5[arr].at[blocks + (pl.ds(r0, nr), pl.ds(pl.multiple_of(core * HALF + c0, 128), nc))]

    sends = Sends(send_sems, SENDS)
    gather = Gather(p, GATHER_UNITS, gather_view, sends, gather_sems)
    reduce = Reduce(
        p, REDUCE_UNITS,
        {DOWN: DW.at[pl.ds(0, HALF)].reshape(4, 2, 2, 96, WIDTH), UP: W5[UP], SMALL: SG},
        {DOWN: (RB0D, RB1D), UP: (RB0W, RB1W), SMALL: (RB0S, RB1S)},
        {DOWN: FD, UP: FW, SMALL: FS},
        sends, reduce_sems,
    )
    copies, sent, leaving = [], {}, {}

    def to_core(name, src, dst, mine=None):
        sem = core_sems.at[len(sent)]
        sent[name] = (dst if mine is None else mine, sem)
        leaving[name] = sends.start(lambda send: remote(src, dst, send, sem, p.peer("core")))

    def got(name):
        dst, sem = sent[name]
        remote(dst, dst, sem, sem, p.peer("core")).wait_recv()

    def left(name):
        sends.left(leaving[name])

    def write(src, dst):
        copy = pltpu.make_async_copy(src, dst, hbm.at[len(copies)])
        copy.start()
        copies.append(copy)

    def at128(start, size):
        return pl.ds(pl.multiple_of(start, 128), size)

    def rows_loop(body, carry, size=64):
        for n in range(0, ROWS, size):
            carry = body(slice(n, n + size), carry)
        return carry

    def mean(v):
        return jnp.sum(v, axis=1, keepdims=True) * (1.0 / WIDTH)

    def fold(v):
        return jnp.sum(v.reshape(-1, 8, v.shape[1]), axis=0)

    def low_lanes(rows):
        return lax.broadcasted_iota(jnp.int32, (rows, 128), 1) < HEAD

    zero = jnp.zeros((8, WIDTH), F32)
    first_len, second_len = lengths[0, 0], lengths[0, 1]
    first = c * ROWS
    own_half = at128(c * HALF, HALF)
    out_b, n_gain, n_bias, down_b, f_gain, f_bias = (lambda i=i: PV[i : i + 1, :] for i in range(6))

    loads = [pltpu.make_async_copy(a, b, load_sems.at[i]) for i, (a, b) in enumerate(((tokens_in, tokens), (cot_in, cot)))]
    for copy in loads:
        copy.start()
    bar = pltpu.get_barrier_semaphore()
    for to in (p.peer("x"), p.peer("y"), p.peer("core"), p.peer("z", 1), p.peer("z", 2), p.peer("z", 3)):
        pl.semaphore_signal(bar, inc=1, device_id=to, device_id_type=MESH)
    stage_s[0:24, 0:2304] = in_w[...]
    stage_s[0:24, 2304:3072] = out_w[...]
    stage_s[0:24, 3072:6144] = up_w[...]
    WD6[p.z, p.y, p.x, c] = down_w[...]
    FS[...] = jnp.zeros((8, 128), F32)
    for i, ref in enumerate((b0, b1, b2, b3, b4, b5)):
        FS[i : i + 1, 0:24] = ref[...].astype(F32)
    FS[6:7, 0:96] = b6[...].astype(F32)
    SP[p.z, p.y, p.x, c] = FS[...]
    pl.semaphore_wait(bar, 6)
    to_core("stage", stage_s, stage_r)
    to_core("tokens", tokens_in, TS)

    def prep():
        got("stage")
        mine, other = stage_s[0:24, :].astype(F32), stage_r[0:24, :].astype(F32)
        top, bottom = jnp.where(c == 0, mine, other), jnp.where(c == 0, other, mine)
        share = jnp.concatenate([top, bottom], axis=0).astype(BF16)
        W5[IN_OUT][p.z, p.y, p.x, :, own_half] = jnp.where(c == 0, share[:, 0:HALF], share[:, HALF:FF])
        W5[UP][p.z, p.y, p.x, :, own_half] = jnp.where(c == 0, share[:, FF : FF + HALF], share[:, FF + HALF :])

    def docs():
        pos = lax.broadcasted_iota(jnp.int32, (ROWS, 128), 0) + first
        doc = (pos >= first_len).astype(jnp.int32)
        span = jnp.where(doc == 0, first_len, second_len).astype(F32)
        angle = HALF_PI * (pos - doc * first_len).astype(F32) / span
        CS[...] = jnp.where(low_lanes(ROWS), jnp.cos(angle), jnp.sin(angle))
        prior_doc = jnp.where(first > 0, (first - 1 >= first_len).astype(jnp.int32), -1)
        last_doc = (first + (ROWS - 1) >= first_len).astype(jnp.int32)
        USE[...] = (doc == prior_doc).astype(F32)
        LAST[...] = (doc == last_doc).astype(BF16)
        row = lax.broadcasted_iota(jnp.int32, (ROWS, ROWS), 0)
        col = lax.broadcasted_iota(jnp.int32, (ROWS, ROWS), 1)
        row_doc = (row + first >= first_len).astype(jnp.int32)
        col_doc = (col + first >= first_len).astype(jnp.int32)
        MSK[...] = ((col <= row) & (row_doc == col_doc)).astype(BF16)

    def params():
        wide = jnp.zeros((8, 256), F32)
        for step, dst in ((24, PV), (96, UB)):
            n = 384 // step
            for g in range(32 // n):
                total = jnp.zeros((8, 384), F32)
                for k in range(n):
                    d = n * g + k
                    tile = SP[d // 8, (d // 4) % 2, (d // 2) % 2, d % 2]
                    total = total + pltpu.roll(jnp.concatenate([tile, wide], axis=1), step * k, 1)
                dst[:, 384 * g : 384 * (g + 1)] = total

    def project(j):
        if j == 0:
            loads[0].wait()
        rows = tokens[...]
        low = low_lanes(ROWS)
        for k, feat in ((0, QF), (1, KF)):
            raw = dot(rows, WQ[:, k * WIDTH + 256 * j : k * WIDTH + 256 * (j + 1)], 1, 0)
            for i in range(2):
                r = raw[:, 128 * i : 128 * (i + 1)]
                e = jnp.exp(-jnp.abs(r))
                active = jnp.maximum(r, 0.0) + jnp.log1p(e)
                slope = jnp.where(r >= 0, 1.0, e) / (1.0 + e)
                at = k * WIDTH + 256 * j + 128 * i
                SIG[:, at : at + 128] = slope.astype(BF16)
                turned = pltpu.roll(active, HEAD, 1)
                feat[4 * j + 2 * i] = (jnp.where(low, active, turned) * CS[...]).astype(BF16)
                feat[4 * j + 2 * i + 1] = (jnp.where(low, turned, active) * CS[...]).astype(BF16)
        value = dot(rows, WQ[:, 2 * WIDTH + 256 * j : 2 * WIDTH + 256 * (j + 1)], 1, 0)
        for i in range(2):
            v = value[:, 128 * i : 128 * (i + 1)]
            VX[4 * j + 2 * i] = jnp.where(low, v, 1.0).astype(BF16)
            VX[4 * j + 2 * i + 1] = jnp.where(low, 1.0, v).astype(BF16)

    def summary():
        def one(h, carry):
            SES[h] = dot(KF[h] * LAST[...], VX[h], 0, 0).astype(BF16)
            return carry

        lax.fori_loop(0, HEADS, one, 0)
        to_core("state", SES, SER)

    def attend(n):
        if n == 0:
            got("state")
        at = slice(128 * n, 128 * (n + 1))
        low = low_lanes(256)
        for half in range(2):
            width = 256 * (half + 1)
            rows = slice(256 * half, width)
            outs = []
            for h in (2 * n, 2 * n + 1):
                q = QF[h, rows, :]
                scores = dot(q, KF[h, 0:width, :], 1, 1).astype(BF16) * MSK[rows, 0:width]
                outs.append(dot(scores, VX[h, 0:width, :], 1, 0) + USE[rows, :] * dot(q, SER[h], 1, 0))
            numer = jnp.where(low, outs[0], outs[1])
            denom = jnp.where(low, pltpu.roll(outs[0], HEAD, 1), pltpu.roll(outs[1], HEAD, 1))
            inverse = 1.0 / denom
            RD[rows, at] = inverse
            ATT[rows, at] = (numer * inverse).astype(BF16)

    def out_project():
        to_core("attended", ATT, ATS)
        for j in range(3):
            cols = slice(256 * j, 256 * (j + 1))
            F1[:, cols] = (
                tokens[:, cols].astype(F32)
                + dot(ATT[...], WQ[:, 2304 + 256 * j : 2304 + 256 * (j + 1)], 1, 0)
                + out_b()[:, cols]
            )

        def norm(at, carry):
            x = F1[at, :]
            centered = x - mean(x)
            scale = lax.rsqrt(mean(centered * centered) + NORM_EPS)
            normal = centered * scale
            N1[at, :] = normal
            S1[at, :] = jnp.broadcast_to(scale, (normal.shape[0], 128))
            NL[at, :] = (normal * n_gain() + n_bias()).astype(BF16)
            return carry

        rows_loop(norm, 0)
        to_core("normed", NL, NLS)

    def up(j):
        cols = slice(512 * j, 512 * (j + 1))
        hidden = dot(NL[...], WU[:, cols], 1, 0) + UB[6:7, cols]
        phi = 0.5 + 0.5 * lax.erf(hidden * math.sqrt(0.5))
        active = (hidden * phi).astype(BF16)
        slope = phi + hidden * (jnp.exp(-0.5 * hidden * hidden) * (1.0 / math.sqrt(2 * math.pi)))
        GP[:, cols] = slope.astype(BF16)
        AT[cols, :] = active.T
        for piece in range(4):
            a, b = max(512 * j, 768 * piece), min(512 * (j + 1), 768 * (piece + 1))
            if a < b:
                ACT[piece, :, a - 768 * piece : b - 768 * piece] = active[:, a - 512 * j : b - 512 * j]
        if j == 5:
            to_core("activated", AT4.at[:, 1 - c], ATS3)

    def down(j):
        cols = slice(256 * j, 256 * (j + 1))
        total = down_b()[:, cols] + (N1[:, cols] * n_gain()[:, cols] + n_bias()[:, cols])
        for piece in range(4):
            total = total + dot(ACT[piece], WD[768 * piece : 768 * (piece + 1), cols], 1, 0)
        F1[:, cols] = total

    def norm_second():
        loads[1].wait()

        def norm(at, carry):
            gain_sum, bias_sum, down_sum = carry
            x = F1[at, :]
            centered = x - mean(x)
            scale = lax.rsqrt(mean(centered * centered) + NORM_EPS)
            normal = centered * scale
            OUT[at, :] = (normal * f_gain() + f_bias()).astype(BF16)
            ct = cot[at, :].astype(F32)
            e = ct * f_gain()
            grad = scale * (e - mean(e) - normal * mean(e * normal))
            F1[at, :] = grad
            low = grad.astype(BF16)
            DG[at, :] = low
            return gain_sum + fold(ct * normal), bias_sum + fold(ct), down_sum + fold(low.astype(F32))

        sums = rows_loop(norm, (zero, zero, zero))
        to_core("down", DG, DGS)
        for i, s in zip((4, 5, 3), sums):
            VEC[i : i + 1, :] = jnp.sum(s, axis=0, keepdims=True)
        write(OUT, result)

    def down_weight(j):
        cols = slice(256 * j, 256 * (j + 1))
        if j == 0:
            got("activated")
        part = dot(AT4[:, c].reshape(HALF, ROWS), DG[:, cols], 1, 0)
        if j == 0:
            got("down")
        DW[0:HALF, cols] = (part + dot(ATS2[...], DGS[:, cols], 1, 0)).astype(BF16)

    def free_up():
        while gathered:
            sends.left(gathered.pop())

    def hidden_back(j):
        cols = slice(512 * j, 512 * (j + 1))
        grad = dot(DG[...], WD[cols, :], 1, 1) * GP[:, cols].astype(F32)
        low = grad.astype(BF16)
        GP[:, cols] = low
        HID[0:1, cols] = jnp.sum(low.astype(F32), axis=0, keepdims=True)
        if j == 5:
            to_core("hidden", GP.at[:, at128((1 - c) * HALF, HALF)], HGS)

    def normed_back(j):
        cols = slice(256 * j, 256 * (j + 1))
        F1[:, cols] = F1[:, cols] + dot(GP[...], WU[cols, :], 1, 1)

    def up_weight(j):
        if j == 0:
            free_up()
            got("normed")
            got("hidden")
        cols = slice(512 * j, 512 * (j + 1))
        part = dot(NL[...], GP[:, at128(c * HALF + 512 * j, 512)], 0, 0) + dot(NLS[...], HGS[:, cols], 0, 0)
        WU[:, cols] = part.astype(BF16)

    def norm_first_back():
        def norm(at, carry):
            gain_sum, bias_sum, out_sum = carry
            g, normal, scale = F1[at, :], N1[at, :], S1[at, 0:1]
            e = g * n_gain()
            grad = scale * (e - mean(e) - normal * mean(e * normal))
            F1[at, :] = grad
            low = grad.astype(BF16)
            BG[at, :] = low
            return gain_sum + fold(g * normal), bias_sum + fold(g), out_sum + fold(low.astype(F32))

        sums = rows_loop(norm, (zero, zero, zero))
        to_core("branch", BG.at[:, at128((1 - c) * 384, 384)], BGS)
        for i, s in zip((1, 2, 0), sums):
            VEC[i : i + 1, :] = jnp.sum(s, axis=0, keepdims=True)

    def small_tiles():
        line = lax.broadcasted_iota(jnp.int32, (8, 128), 0)
        lane = lax.broadcasted_iota(jnp.int32, (8, 128), 1)
        for d in range(32):
            g, k = divmod(d, 16)
            part = VEC[:, 384 * g : 384 * (g + 1)]
            a = (pltpu.roll(part, 384 - 24 * k, 1) if k else part)[:, 0:128]
            g, k = divmod(d, 4)
            part = jnp.broadcast_to(HID[0:1, 384 * g : 384 * (g + 1)], (8, 384))
            b = (pltpu.roll(part, 384 - 96 * k, 1) if k else part)[:, 0:128]
            tile = jnp.where((line < 6) & (lane < 24), a, jnp.where((line == 6) & (lane < 96), b, 0.0))
            SGR[0, d % 2, d // 8, (d // 4) % 2, (d // 2) % 2] = tile
        to_core("small", SGR.at[0, 1 - c], SGR.at[1, 0])

    def small_sum():
        got("small")
        SG[...] = SGR[0, c] + SGR[1, 0]

    def slot(h):
        return (slice(512 * (h // 4), 512 * (h // 4 + 1)), slice(128 * (h % 4), 128 * (h % 4 + 1)))

    def numer_back(j):
        if j == 0:
            left("activated")
            left("state")
        low = low_lanes(ROWS)
        lane = lax.broadcasted_iota(jnp.int32, (ROWS, 128), 1)
        across = low_lanes(128) != (lax.broadcasted_iota(jnp.int32, (128, 128), 0) < HEAD)
        across = across.astype(F32).astype(BF16)
        grads = dot(BG[...], WQ[256 * j : 256 * (j + 1), 2304:FF], 1, 1)
        for i in range(2):
            at = slice(256 * j + 128 * i, 256 * j + 128 * (i + 1))
            ng = grads[:, 128 * i : 128 * (i + 1)] * RD[:, at]
            scaled = ng * ATT[:, at].astype(F32)
            high = scaled.astype(BF16)
            rest = (scaled - high.astype(F32)).astype(BF16)
            dgrad = -(dot(high, across, 1, 0) + dot(rest, across, 1, 0))
            hi = dgrad.astype(BF16).astype(F32)
            beside = jnp.where(
                (lane == 0) | (lane == HEAD), hi, jnp.where((lane == 1) | (lane == HEAD + 1), dgrad - hi, 0.0)
            )
            for par in range(2):
                h = 4 * j + 2 * i + par
                ngx = jnp.where(low, ng, beside) if par == 0 else jnp.where(low, beside, ng)
                AT[slot(h)] = ngx.astype(BF16)
                SES[h] = dot(QF[h], (ngx * USE[...]).astype(BF16), 0, 0).astype(BF16)
        if j == 2:
            to_core("leave", SES, LER)

    def out_weight():
        free_up()
        got("attended")
        part = dot(ATT[...], BG[:, at128(c * 384, 384)], 0, 0)
        got("branch")
        WU[:, 2688:FF] = (part + dot(ATS[...], BGS[...], 0, 0)).astype(BF16)

    def attend_back(n):
        if n == 0:
            left("hidden")
            got("leave")
        low = low_lanes(ROWS)
        lead = c == 0
        last = LAST[...].astype(F32) * jnp.where(lead, 1.0, 0.0).astype(F32)
        m0, m1 = MSK[0:256, 0:256], MSK[256:ROWS, :]
        top, bottom = slice(0, 256), slice(256, ROWS)
        pieces = [], [], []
        for h in (2 * n, 2 * n + 1):
            ngx, qf, kf, vx = AT[slot(h)], QF[h], KF[h], VX[h]
            d0 = dot(ngx[top], vx[top], 1, 1).astype(BF16) * m0
            d1 = dot(ngx[bottom], vx, 1, 1).astype(BF16) * m1
            s0 = dot(qf[top], kf[top], 1, 1).astype(BF16) * m0
            s1 = dot(qf[bottom], kf, 1, 1).astype(BF16) * m1
            q_grad = jnp.concatenate([dot(d0, kf[top], 1, 0), dot(d1, kf, 1, 0)], axis=0)
            k_top = dot(d0, qf[top], 0, 0) + dot(d1[:, top], qf[bottom], 0, 0)
            k_grad = jnp.concatenate([k_top, dot(d1[:, bottom], qf[bottom], 0, 0)], axis=0)
            v_top = dot(s0, ngx[top], 0, 0) + dot(s1[:, top], ngx[bottom], 0, 0)
            v_grad = jnp.concatenate([v_top, dot(s1[:, bottom], ngx[bottom], 0, 0)], axis=0)
            past = dot(jnp.where(lead, vx, ngx), jnp.where(lead, LER[h], SER[h]), 1, 1)
            q_grad = (q_grad + USE[...] * past) * CS[...]
            k_grad = (k_grad + last * past) * CS[...]
            pieces[0].append(q_grad + pltpu.roll(q_grad, HEAD, 1))
            pieces[1].append(k_grad + pltpu.roll(k_grad, HEAD, 1))
            pieces[2].append(v_grad + last * dot(kf, LER[h], 1, 0))
        for k, (even, odd) in enumerate(pieces):
            both = jnp.where(low, even, odd)
            at = slice(k * WIDTH + 128 * n, k * WIDTH + 128 * (n + 1))
            if k < 2:
                both = both * SIG[:, at].astype(F32)
            GP[:, at] = both.astype(BF16)

    def projected_out():
        to_core("projected", GP.at[:, at128((1 - c) * 1152, 1152)], PGS)

    def in_weight(j):
        cols = slice(384 * j, 384 * (j + 1))
        if j == 0:
            got("tokens")
        part = dot(tokens[...], GP[:, at128(c * 1152 + 384 * j, 384)], 0, 0)
        if j == 0:
            got("projected")
        WU[:, HALF + 384 * j : HALF + 384 * (j + 1)] = (part + dot(TS[...], PGS[:, cols], 0, 0)).astype(BF16)

    def tokens_back(j):
        cols = slice(256 * j, 256 * (j + 1))
        F1[:, cols] = F1[:, cols] + dot(GP[:, 0:2304], WQ[cols, 0:2304], 1, 1)
        if j == 2:
            write(F1, tokens_grad)

    steps = []
    for step, count in (
        (prep, 0), (docs, 0), (params, 0), (project, 3), (summary, 0), (attend, 6), (out_project, 0), (up, 6), (down, 3),
        (norm_second, 0), (down_weight, 3), (hidden_back, 6), (normed_back, 3), (up_weight, 3), (norm_first_back, 0),
        (small_tiles, 0), (small_sum, 0), (numer_back, 3), (out_weight, 0), (attend_back, 6), (projected_out, 0),
        (in_weight, 3), (tokens_back, 3),
    ):
        steps += [partial(step, j) for j in range(count)] if count else [step]

    for kind, *op in GATHER_PLAN:
        if kind == STEP:
            for u in op[1]:
                gather.ready(u)
            steps[op[0]]()
        elif kind == ISSUE:
            gather.issue(*op)
        else:
            gather.share(*op)

    gathered = sends.now_open()

    outputs = {1: (up_g, 0, HALF), 2: (out_g, 2688, 384), 3: (in_g, HALF, 1152)}
    mine, other = pl.ds(pl.multiple_of(24 * c, 8), 24), pl.ds(pl.multiple_of(24 * (1 - c), 8), 24)
    open_units = list(REDUCE_GROUP)

    def done(u):
        group = REDUCE_GROUP[u]
        open_units.remove(group)
        if group in open_units:
            return
        if group == 0:
            write(FD, down_g)
        elif group == 4:
            small_g[...] = FS[...]
        else:
            ref, at, width = outputs[group]
            theirs, here = (ref.at[:, at128(core * width, width)] for core in (c, 1 - c))
            to_core(group, FW.at[other, pl.ds(at, width)], theirs, here)
            write(FW.at[mine, pl.ds(at, width)], ref.at[:, at128(c * width, width)])

    for kind, *op in REDUCE_PLAN:
        if kind == STEP:
            steps[op[0]]()
        elif kind == ISSUE:
            reduce.send(*op)
        else:
            reduce.add(*op)
            if op[1] == 2:
                done(op[0])

    for group in outputs:
        got(group)
    sends.finish()
    for copy in copies:
        copy.wait()


def hand_out(*refs):
    made, small, outs, vectors = refs[0:6], refs[6], refs[7:13], refs[13:20]
    held, lines, sems = refs[20:26], refs[26:33], refs[33]
    pieces = []
    for a, b, c in zip(made, held, outs):
        rows = a.shape[0]
        step = 128 if rows == ROWS else rows
        for r in range(0, rows, step):
            pieces.append(tuple(ref.at[pl.ds(r, step)] for ref in (a, b, c)))
    ins = [pltpu.make_async_copy(a, b, sems.at[0, i]) for i, (a, b, _) in enumerate(pieces)]
    back = [pltpu.make_async_copy(b, c, sems.at[1, i]) for i, (_, b, c) in enumerate(pieces)]
    for copy in ins:
        copy.start()
    for i, line in enumerate(lines):
        line[...] = small[i : i + 1, 0 : line.shape[1]]
        back.append(pltpu.make_async_copy(line, vectors[i], sems.at[1, len(pieces) + i]))
        back[-1].start()
    for copy, then in zip(ins, back):
        copy.wait()
        then.start()
    for copy in back:
        copy.wait()


def layer_2x2x4(tokens, lengths, in_weight, out_weight, out_bias, norm_gain, norm_bias, up_weight, up_bias,
                down_weight, down_bias, final_gain, final_bias, cotangent):
    vmem, anywhere = pl.BlockSpec(memory_space=pltpu.VMEM), pl.BlockSpec(memory_space=pl.ANY)

    def v(*shape, dtype=BF16):
        return pltpu.VMEM(shape, dtype)

    dma = pltpu.SemaphoreType.DMA
    scratch = [
        v(WIDTH, FF), v(WIDTH, FF), v(FF, WIDTH),
        v(32, 6144), v(32, 6144), v(4, 2, 2, 2, 8, 128, dtype=F32),
        v(8, WIDTH, dtype=F32), v(8, FF, dtype=F32),
        v(ROWS, WIDTH), v(ROWS, HALF),
        v(HEADS, ROWS, 128), v(HEADS, ROWS, 128), v(HEADS, ROWS, 128),
        v(HEADS, 128, 128), v(HEADS, 128, 128), v(HEADS, 128, 128),
        v(ROWS, ROWS), v(ROWS, 128, dtype=F32), v(ROWS, 128, dtype=F32), v(ROWS, 128),
        v(ROWS, WIDTH, dtype=F32), v(ROWS, WIDTH), v(ROWS, WIDTH),
        v(ROWS, WIDTH, dtype=F32), v(ROWS, 128, dtype=F32), v(ROWS, WIDTH, dtype=F32),
        v(ROWS, WIDTH), v(ROWS, WIDTH), v(4, ROWS, WIDTH), v(ROWS, FF),
        v(FF, ROWS), v(HALF, ROWS), v(ROWS, WIDTH), v(ROWS, WIDTH), v(ROWS, HALF),
        v(ROWS, WIDTH), v(ROWS, 384), v(ROWS, 1152), v(ROWS, WIDTH),
        v(4, 2, 96, WIDTH), v(7, 96, WIDTH),
        v(4, 2, 48, FF), v(7, 48, FF),
        v(96, WIDTH, dtype=F32), v(48, FF, dtype=F32),
        v(4, 2, 2, 8, 128, dtype=F32), v(2, 2, 4, 2, 2, 8, 128, dtype=F32),
        v(4, 2, 8, 128, dtype=F32), v(7, 8, 128, dtype=F32), v(8, 128, dtype=F32),
        v(8, WIDTH, dtype=F32), v(8, FF, dtype=F32),
        v(ROWS, WIDTH), v(ROWS, WIDTH),
        dma((SENDS,)), dma((10 * len(GATHER_UNITS),)), dma((5 * len(REDUCE_UNITS),)), dma((16,)), dma((10,)), dma((2,)),
    ]
    shapes = (
        jax.ShapeDtypeStruct((ROWS, WIDTH), BF16),
        jax.ShapeDtypeStruct((ROWS, WIDTH), F32),
        jax.ShapeDtypeStruct((24, 2304), F32),
        jax.ShapeDtypeStruct((24, WIDTH), F32),
        jax.ShapeDtypeStruct((24, FF), F32),
        jax.ShapeDtypeStruct((96, WIDTH), F32),
    )
    lines = (jax.ShapeDtypeStruct((1, 24), F32),) * 6 + (jax.ShapeDtypeStruct((1, 96), F32),)
    vectors = (out_bias, norm_gain, norm_bias, down_bias, final_gain, final_bias, up_bias)
    made = pl.pallas_call(
        whole_layer,
        out_shape=shapes + (jax.ShapeDtypeStruct((8, 128), F32),),
        in_specs=[anywhere, pl.BlockSpec(memory_space=pltpu.SMEM), anywhere] + [vmem] * 11,
        out_specs=(anywhere,) * 6 + (vmem,),
        scratch_shapes=scratch,
        compiler_params=pltpu.CompilerParams(
            collective_id=0, has_side_effects=True, vmem_limit_bytes=VMEM_LIMIT
        ),
    )(tokens, lengths, cotangent, in_weight, out_weight, up_weight, down_weight, *(b.reshape(1, -1) for b in vectors))
    result, tokens_grad, in_g, out_g, up_g, down_g, *small = pl.pallas_call(
        hand_out,
        out_shape=shapes + lines,
        in_specs=[anywhere] * 6 + [vmem],
        out_specs=(anywhere,) * 13,
        scratch_shapes=[pltpu.VMEM(s.shape, s.dtype) for s in shapes + lines] + [dma((2, 19))],
        compiler_params=pltpu.CompilerParams(vmem_limit_bytes=VMEM_LIMIT),
    )(*made)
    out_bias_g, norm_gain_g, norm_bias_g, down_bias_g, final_gain_g, final_bias_g, up_bias_g = (
        g.reshape(-1) for g in small
    )
    return (result, tokens_grad, in_g, out_g, out_bias_g, norm_gain_g, norm_bias_g, up_g,
            up_bias_g, down_g, down_bias_g, final_gain_g, final_bias_g)


VMEM_LIMIT = 64 * 2**20 - 2**18


def solution(mesh):
    both = ("dp", "fsdp")
    rows, vector = P(both, None), P(both)
    in_specs = (rows, P("dp", None), rows, rows, vector, vector, vector, rows, vector, rows, vector, vector, vector, rows)
    out_specs = (rows, rows, rows, rows, vector, vector, vector, rows, vector, rows, vector, vector, vector)
    body = layer_2x2x4 if dict(mesh.shape) == {"dp": 16, "fsdp": 2} else per_device
    return jax.shard_map(body, mesh=mesh, in_specs=in_specs, out_specs=out_specs, check_vma=False)
```

```python
from functools import partial
import math

import jax
import jax.numpy as jnp
from jax import lax
from jax.experimental import pallas as pl
from jax.experimental.pallas import tpu as pltpu
from jax.sharding import PartitionSpec as P

HEADS = 12
HEAD = 64
BLOCK = 512


HALF_PI = math.pi / 2
NORM_EPS = 1e-05

def prefix(shard, axis, combine, identity, reverse):
    devices, position = (lax.axis_size(axis), lax.axis_index(axis))
    everything = jax.tree.map(lambda part: lax.all_gather(part, axis), shard)
    start = jax.tree.map(
        lambda part, zero: jnp.broadcast_to(jnp.asarray(zero, part.dtype), part.shape),
        shard,
        identity,
    )

    def turn(k, before):
        at = devices - 1 - k if reverse else k
        reached = at > position if reverse else at < position
        new = combine(before, jax.tree.map(lambda part: part[at], everything))
        return jax.tree.map(lambda a, b: jnp.where(reached, a, b), new, before)

    return lax.fori_loop(0, devices, turn, start)


def documents(position, pair):
    first_len = pair[0]
    doc = (position >= first_len).astype(jnp.int32)
    start = doc * first_len
    span = jnp.where(doc == 0, first_len, pair[1])
    angle = HALF_PI * (position - start).astype(jnp.float32) / span.astype(jnp.float32)
    return (doc, angle)


def features(heads, angle):
    active = jax.nn.softplus(heads)
    return jnp.concatenate(
        [active * jnp.cos(angle)[None, :, None], active * jnp.sin(angle)[None, :, None]], axis=2
    )


def layer_norm(rows, gain, shift):
    mean = jnp.mean(rows, axis=-1, keepdims=True)
    centered = rows - mean
    scale = lax.rsqrt(jnp.mean(centered * centered, axis=-1, keepdims=True) + NORM_EPS)
    return centered * scale * gain + shift


def exact_gelu(values):
    return jax.nn.gelu(values, approximate=False)


def merge_state(earlier, later):
    return (
        later[0] + later[2] * earlier[0],
        later[1] + later[2] * earlier[1],
        later[2] * earlier[2],
    )


def block_forward(query, keys, values, doc_blk, state, norm, carry_doc):
    order = jnp.arange(doc_blk.shape[0], dtype=jnp.int32)
    mask = (order[None, :] <= order[:, None]) & (doc_blk[None, :] == doc_blk[:, None])
    raw = jnp.einsum("hif,hjf->hij", query, keys, preferred_element_type=jnp.float32)
    scores = jnp.where(mask[None], raw, 0.0)
    use = (doc_blk == carry_doc).astype(jnp.float32)
    carried = jnp.einsum(
        "hef,hif->hei", state.astype(jnp.bfloat16), query, preferred_element_type=jnp.float32
    )
    numer = (
        jnp.einsum(
            "hej,hij->hei", values, scores.astype(jnp.bfloat16), preferred_element_type=jnp.float32
        )
        + use * carried
    )
    denom = jnp.sum(scores, axis=2) + use * jnp.einsum(
        "hf,hif->hi", norm, query.astype(jnp.float32)
    )
    return (mask, scores, use, numer, denom)


def block_summary(keys, values, doc_blk):
    chosen = doc_blk == doc_blk[-1]
    picked = jnp.where(chosen[None, :, None], keys, jnp.zeros((), keys.dtype))
    state = jnp.einsum("hej,hjf->hef", values, picked, preferred_element_type=jnp.float32)
    norm = jnp.sum(picked.astype(jnp.float32), axis=1)
    return (chosen, picked, state, norm)


def per_device(
    tokens,
    lengths,
    in_weight,
    out_weight,
    out_bias,
    norm_gain,
    norm_bias,
    up_weight,
    up_bias,
    down_weight,
    down_bias,
    final_gain,
    final_bias,
    cotangent,
):
    rows = tokens.shape[0]
    width = tokens.shape[1]
    count = rows // BLOCK
    gathered = (
        lax.all_gather(in_weight, ("dp", "fsdp"), axis=0, tiled=True),
        lax.all_gather(out_weight, ("dp", "fsdp"), axis=0, tiled=True),
        lax.all_gather(out_bias, ("dp", "fsdp"), axis=0, tiled=True),
        lax.all_gather(norm_gain, ("dp", "fsdp"), axis=0, tiled=True),
        lax.all_gather(norm_bias, ("dp", "fsdp"), axis=0, tiled=True),
        lax.all_gather(up_weight, ("dp", "fsdp"), axis=0, tiled=True),
        lax.all_gather(up_bias, ("dp", "fsdp"), axis=0, tiled=True),
        lax.all_gather(down_weight, ("dp", "fsdp"), axis=0, tiled=True),
        lax.all_gather(down_bias, ("dp", "fsdp"), axis=0, tiled=True),
        lax.all_gather(final_gain, ("dp", "fsdp"), axis=0, tiled=True),
        lax.all_gather(final_bias, ("dp", "fsdp"), axis=0, tiled=True),
    )
    (
        inward,
        outward,
        out_shift,
        gain_first,
        shift_first,
        upward,
        up_shift,
        downward,
        down_shift,
        gain_second,
        shift_second,
    ) = gathered
    first = lax.axis_index("fsdp") * rows
    position = first + jnp.arange(rows, dtype=jnp.int32)
    pair = lengths[0]
    doc, angle = documents(position, pair)
    prior_doc = jnp.where(first > 0, (first - 1 >= pair[0]).astype(jnp.int32), -1)
    projected = jnp.dot(tokens, inward, preferred_element_type=jnp.float32)
    query_raw = projected[:, :width].reshape(rows, HEADS, HEAD).transpose(1, 0, 2)
    key_raw = projected[:, width : 2 * width].reshape(rows, HEADS, HEAD).transpose(1, 0, 2)
    query_feat, query_pull = jax.vjp(partial(features, angle=angle), query_raw)
    key_feat, key_pull = jax.vjp(partial(features, angle=angle), key_raw)
    query = query_feat.astype(jnp.bfloat16)
    keys = key_feat.astype(jnp.bfloat16)
    values = (
        projected[:, 2 * width :].reshape(rows, HEADS, HEAD).transpose(1, 2, 0).astype(jnp.bfloat16)
    )
    device_summary = block_summary(keys, values, doc)
    device_keep = (prior_doc == doc[-1]).astype(jnp.float32)
    identity = (
        jnp.zeros_like(device_summary[2]),
        jnp.zeros_like(device_summary[3]),
        jnp.ones((), jnp.float32),
    )
    state, norm, passed = prefix(
        (device_summary[2], device_summary[3], device_keep), "fsdp", merge_state, identity, False
    )
    keys_blk = keys
    values_blk = values
    doc_blk = doc
    carries = [(state, norm, prior_doc)]
    outcome = block_forward(query, keys_blk, values_blk, doc_blk, state, norm, prior_doc)
    ratios = outcome[3] / outcome[4][:, None, :]
    summary = block_summary(keys_blk, values_blk, doc_blk)
    attended = ratios.transpose(2, 0, 1).reshape(rows, width).astype(jnp.bfloat16)
    branch = jnp.dot(attended, outward, preferred_element_type=jnp.float32) + out_shift.astype(
        jnp.float32
    )
    first_sum = tokens.astype(jnp.float32) + branch
    normed, first_pull = jax.vjp(
        layer_norm, first_sum, gain_first.astype(jnp.float32), shift_first.astype(jnp.float32)
    )
    normed_low = normed.astype(jnp.bfloat16)
    hidden = jnp.dot(normed_low, upward, preferred_element_type=jnp.float32) + up_shift.astype(
        jnp.float32
    )
    activated, gelu_pull = jax.vjp(exact_gelu, hidden)
    activated_low = activated.astype(jnp.bfloat16)
    second_sum = (
        normed
        + jnp.dot(activated_low, downward, preferred_element_type=jnp.float32)
        + down_shift.astype(jnp.float32)
    )
    result, second_pull = jax.vjp(
        layer_norm, second_sum, gain_second.astype(jnp.float32), shift_second.astype(jnp.float32)
    )
    again = (
        lax.all_gather(in_weight, ("dp", "fsdp"), axis=0, tiled=True),
        lax.all_gather(out_weight, ("dp", "fsdp"), axis=0, tiled=True),
        lax.all_gather(out_bias, ("dp", "fsdp"), axis=0, tiled=True),
        lax.all_gather(norm_gain, ("dp", "fsdp"), axis=0, tiled=True),
        lax.all_gather(norm_bias, ("dp", "fsdp"), axis=0, tiled=True),
        lax.all_gather(up_weight, ("dp", "fsdp"), axis=0, tiled=True),
        lax.all_gather(up_bias, ("dp", "fsdp"), axis=0, tiled=True),
        lax.all_gather(down_weight, ("dp", "fsdp"), axis=0, tiled=True),
        lax.all_gather(down_bias, ("dp", "fsdp"), axis=0, tiled=True),
        lax.all_gather(final_gain, ("dp", "fsdp"), axis=0, tiled=True),
        lax.all_gather(final_bias, ("dp", "fsdp"), axis=0, tiled=True),
    )
    inward = again[0]
    outward = again[1]
    upward = again[5]
    downward = again[7]
    second_grad, final_gain_grad, final_shift_grad = second_pull(cotangent.astype(jnp.float32))
    down_grad = second_grad.astype(jnp.bfloat16)
    down_weight_grad = jnp.dot(activated_low.T, down_grad, preferred_element_type=jnp.float32)
    down_shift_grad = jnp.sum(down_grad.astype(jnp.float32), axis=0)
    (activated_grad,) = gelu_pull(
        jnp.dot(down_grad, downward.T, preferred_element_type=jnp.float32)
    )
    hidden_grad = activated_grad.astype(jnp.bfloat16)
    up_weight_grad = jnp.dot(normed_low.T, hidden_grad, preferred_element_type=jnp.float32)
    up_shift_grad = jnp.sum(hidden_grad.astype(jnp.float32), axis=0)
    normed_grad = second_grad + jnp.dot(hidden_grad, upward.T, preferred_element_type=jnp.float32)
    first_grad, norm_gain_grad, norm_shift_grad = first_pull(normed_grad)
    branch_grad = first_grad.astype(jnp.bfloat16)
    out_weight_grad = jnp.dot(attended.T, branch_grad, preferred_element_type=jnp.float32)
    out_shift_grad = jnp.sum(branch_grad.astype(jnp.float32), axis=0)
    attended_grad = jnp.dot(branch_grad, outward.T, preferred_element_type=jnp.float32)
    ratio_grad = attended_grad.reshape(rows, HEADS, HEAD).transpose(1, 2, 0)
    index = 0
    keys_blk = keys
    values_blk = values
    doc_blk = doc
    state_in, norm_in, doc_in = carries[index]
    mask, scores, use, numer, denom = block_forward(
        query, keys_blk, values_blk, doc_blk, state_in, norm_in, doc_in
    )
    numer_grad = (ratio_grad / denom[:, None, :]).astype(jnp.bfloat16)
    denom_grad = -jnp.sum(ratio_grad * numer, axis=1) / (denom * denom)
    scores_grad = (
        jnp.einsum("hei,hej->hij", numer_grad, values_blk, preferred_element_type=jnp.float32)
        + denom_grad[:, :, None]
    )
    scores_grad = jnp.where(mask[None], scores_grad, 0.0).astype(jnp.bfloat16)
    used_numer = jnp.where(use[None, None, :] > 0, numer_grad, jnp.zeros((), jnp.bfloat16))
    used_denom = use * denom_grad
    query_part = jnp.einsum(
        "hij,hjf->hif", scores_grad, keys_blk, preferred_element_type=jnp.float32
    )
    query_part = query_part + jnp.einsum(
        "hei,hef->hif",
        used_numer,
        state_in.astype(jnp.bfloat16),
        preferred_element_type=jnp.float32,
    )
    query_grads = query_part + used_denom[:, :, None] * norm_in[:, None, :]
    key_grads = [jnp.einsum("hij,hif->hjf", scores_grad, query, preferred_element_type=jnp.float32)]
    value_grads = [
        jnp.einsum(
            "hei,hij->hej",
            numer_grad,
            scores.astype(jnp.bfloat16),
            preferred_element_type=jnp.float32,
        )
    ]
    contribs = [
        (
            jnp.einsum("hei,hif->hef", used_numer, query, preferred_element_type=jnp.float32),
            jnp.einsum("hi,hif->hf", used_denom, query.astype(jnp.float32)),
        )
    ]
    keeps = [(doc_in == doc_blk[-1]).astype(jnp.float32)]
    local_state = jnp.zeros_like(device_summary[2])
    local_norm = jnp.zeros_like(device_summary[3])
    for index in reversed(range(count)):
        local_state = contribs[index][0] + keeps[index] * local_state
        local_norm = contribs[index][1] + keeps[index] * local_norm
    leave_state, leave_norm, through = prefix(
        (local_state, local_norm, device_keep), "fsdp", merge_state, identity, True
    )
    for index in reversed(range(count)):
        keys_blk = keys
        values_blk = values
        doc_blk = doc
        summary = block_summary(keys_blk, values_blk, doc_blk)
        state_low = leave_state.astype(jnp.bfloat16)
        key_extra = (
            jnp.einsum("hej,hef->hjf", values_blk, state_low, preferred_element_type=jnp.float32)
            + leave_norm[:, None, :]
        )
        key_grads[index] = key_grads[index] + jnp.where(summary[0][None, :, None], key_extra, 0.0)
        value_grads[index] = value_grads[index] + jnp.einsum(
            "hef,hjf->hej", state_low, summary[1], preferred_element_type=jnp.float32
        )
        leave_state = contribs[index][0] + keeps[index] * leave_state
        leave_norm = contribs[index][1] + keeps[index] * leave_norm
    (query_raw_grad,) = query_pull(query_grads)
    (key_raw_grad,) = key_pull(key_grads[0])
    value_grad = value_grads[0].transpose(2, 0, 1).reshape(rows, width)
    projected_grad = jnp.concatenate(
        [
            query_raw_grad.transpose(1, 0, 2).reshape(rows, width),
            key_raw_grad.transpose(1, 0, 2).reshape(rows, width),
            value_grad,
        ],
        axis=1,
    ).astype(jnp.bfloat16)
    in_weight_grad = jnp.dot(tokens.T, projected_grad, preferred_element_type=jnp.float32)
    tokens_grad = first_grad + jnp.dot(projected_grad, inward.T, preferred_element_type=jnp.float32)
    summed = (
        lax.psum_scatter(in_weight_grad, ("dp", "fsdp"), scatter_dimension=0, tiled=True),
        lax.psum_scatter(out_weight_grad, ("dp", "fsdp"), scatter_dimension=0, tiled=True),
        lax.psum_scatter(out_shift_grad, ("dp", "fsdp"), scatter_dimension=0, tiled=True),
        lax.psum_scatter(norm_gain_grad, ("dp", "fsdp"), scatter_dimension=0, tiled=True),
        lax.psum_scatter(norm_shift_grad, ("dp", "fsdp"), scatter_dimension=0, tiled=True),
        lax.psum_scatter(up_weight_grad, ("dp", "fsdp"), scatter_dimension=0, tiled=True),
        lax.psum_scatter(up_shift_grad, ("dp", "fsdp"), scatter_dimension=0, tiled=True),
        lax.psum_scatter(down_weight_grad, ("dp", "fsdp"), scatter_dimension=0, tiled=True),
        lax.psum_scatter(down_shift_grad, ("dp", "fsdp"), scatter_dimension=0, tiled=True),
        lax.psum_scatter(final_gain_grad, ("dp", "fsdp"), scatter_dimension=0, tiled=True),
        lax.psum_scatter(final_shift_grad, ("dp", "fsdp"), scatter_dimension=0, tiled=True),
    )
    return (result.astype(jnp.bfloat16), tokens_grad) + tuple(summed)


MESH = pl.DeviceIdType.MESH
F32 = jnp.float32
BF16 = jnp.bfloat16
ROWS = 512
WIDTH = 768
FF = 3072
HALF = 1536
GATHER_ORDER = ("zyx", "zxy", "xzy", "yzx", "xyz", "yxz", "zyx", "zxy")
DIRECT = (6, 7)
REDUCE_ORDER = ("xyz", "yxz", "yzx", "xzy")


def dot(a, b, ca, cb):
    return lax.dot_general(a, b, (((ca,), (cb,)), ((), ())), preferred_element_type=F32)


class Place:
    def __init__(self):
        self.dp = lax.axis_index("dp")
        self.c = lax.axis_index("fsdp")
        self.x = lax.rem(self.dp, 2)
        self.y = lax.rem(lax.div(self.dp, 2), 2)
        self.z = lax.div(self.dp, 4)

    def peer(self, d, k=1):
        if d == "x":
            return (self.dp + 1 - 2 * self.x, self.c)
        if d == "y":
            return (self.dp + 2 - 4 * self.y, self.c)
        if d == "z":
            return (lax.rem(self.dp + 4 * k, 16), self.c)
        if d == "up":
            return (self.dp + 4, self.c)
        if d == "down":
            return (self.dp - 4, self.c)
        return (self.dp, 1 - self.c)

    def at(self, known, flip=None, z=None):
        out = []
        for d in "zyx":
            if d in known:
                out.append(slice(None))
                continue
            v = getattr(self, d)
            if flip == d:
                v = 1 - v
            if d == "z" and z is not None:
                v = z
            out.append(v)
        return tuple(out)


def remote(src, dst, send, recv, to):
    return pltpu.make_async_remote_copy(
        src_ref=src, dst_ref=dst, send_sem=send, recv_sem=recv, device_id=to, device_id_type=MESH
    )


def guarded(cond, action):
    if cond is None:
        action()
    else:
        pl.when(cond)(action)


class Sends:
    def __init__(self, sems, size):
        self.sems, self.size, self.count, self.open = sems, size, 0, {}

    def start(self, make, cond=None):
        i = self.count % self.size
        self.count += 1
        self.wait(i)
        guarded(cond, lambda: make(self.sems.at[i]).start())
        self.open[i] = (cond, make)
        return i, make

    def wait(self, i):
        if i in self.open:
            cond, make = self.open.pop(i)
            guarded(cond, lambda: make(self.sems.at[i]).wait_send())

    def left(self, handle):
        if self.open.get(handle[0], (None, None))[1] is handle[1]:
            self.wait(handle[0])

    def now_open(self):
        return [(i, make) for i, (_, make) in self.open.items()]

    def finish(self):
        for i in list(self.open):
            self.wait(i)


class Gather:
    def __init__(self, place, units, view, sends, sems):
        self.p, self.units, self.view, self.sends, self.sems = place, units, view, sends, sems
        self.waited = set()

    def order(self, u):
        return GATHER_ORDER[self.units[u][1]]

    def copy(self, u, slot, blocks, to):
        src = self.view(u, blocks, self.p.c)
        return lambda sem: remote(src, src, sem, self.sems.at[6 * u + slot], to)

    def issue(self, u, ph, hop):
        p, o = self.p, self.order(u)
        known, d = o[:ph], o[ph]
        if hop == 1 and ph > 0:
            self.arrive(u, ph - 1)
        if d != "z":
            self.sends.start(self.copy(u, "xy".index(d), p.at(known), p.peer(d)))
            return
        if self.units[u][1] in DIRECT:
            for k in (1, 2, 3):
                self.sends.start(self.copy(u, 2, p.at(known), p.peer("z", k)))
            return
        if hop > 1:
            self.arrive_hop(u, ph, hop - 1)
        up = (jnp.logical_and(p.z < 3, p.z - (hop - 1) >= 0), p.z - (hop - 1), p.peer("up"))
        down = (jnp.logical_and(p.z > 0, p.z + (hop - 1) <= 3), p.z + (hop - 1), p.peer("down"))
        for cond, z, to in (up, down):
            self.sends.start(self.copy(u, 1 + hop, p.at(known, z=z), to), cond)

    def expect(self, u, slot, blocks, core):
        dst = self.view(u, blocks, core)
        remote(dst, dst, self.sems.at[6 * u + slot], self.sems.at[6 * u + slot], self.p.peer("core")).wait_recv()

    def arrive_hop(self, u, ph, hop):
        if (u, ph, hop) in self.waited:
            return
        self.waited.add((u, ph, hop))
        p, known = self.p, self.order(u)[:ph]
        above, below = p.z + hop <= 3, p.z - hop >= 0
        one = jnp.logical_xor(above, below)
        guarded(one, lambda: self.expect(u, 1 + hop, p.at(known), p.c))
        if hop == 1:
            two = jnp.logical_and(above, below)
            guarded(two, lambda: self.expect(u, 1 + hop, (pl.ds(0, 2),) + p.at(known)[1:], p.c))

    def arrive(self, u, ph):
        p, o = self.p, self.order(u)
        known, d = o[:ph], o[ph]
        if d == "z" and self.units[u][1] not in DIRECT:
            for hop in (1, 2, 3):
                self.arrive_hop(u, ph, hop)
        elif (u, ph, 0) not in self.waited:
            self.waited.add((u, ph, 0))
            if d == "z":
                self.expect(u, 2, (pl.ds(0, 3),) + p.at(known)[1:], p.c)
            else:
                self.expect(u, "xy".index(d), p.at(known, flip=d), p.c)

    def shared(self, u, part):
        o = self.order(u)
        if o[2] == "z":
            return self.p.at(o) if part else None
        return self.p.at(o[:2], flip=o[2] if part else None)

    def share(self, u, part):
        if self.shared(u, part):
            self.arrive(u, 1 + part)
            self.sends.start(self.copy(u, 5, self.shared(u, part), self.p.peer("core")))

    def ready(self, u):
        if (u, 0) not in self.waited:
            self.waited.add((u, 0))
            self.expect(u, 5, self.p.at("zyx"), 1 - self.p.c)


class Reduce:
    def __init__(self, place, units, blocks, landing, final, sends, sems):
        self.p, self.units = place, units
        self.blocks, self.landing, self.final = blocks, landing, final
        self.sends, self.sems = sends, sems

    def plan(self, u, ph):
        arr, kind, r0, nr, c0, nc = self.units[u]
        o = REDUCE_ORDER[kind]
        return arr, o[ph], o[ph + 1 :], (pl.ds(r0, nr), pl.ds(c0, nc))

    def moves(self, u, ph):
        p = self.p
        arr, d, left, cut = self.plan(u, ph)
        land = self.landing[arr][min(ph, 1)]
        if d != "z":
            lead = {0: (slice(None), slice(None)), 1: (pl.ds(0, 4),), 2: (6,)}[ph]
            return [(self.sems.at[3 * u + "xy".index(d)], p.at(left, flip=d), p.peer(d), land.at[lead + cut])]
        out = []
        for k in (1, 2, 3):
            lead = (pl.ds(2 * (k - 1), 2),) if ph == 1 else (3 + k,)
            blocks = p.at(left, z=lax.rem(p.z + k, 4))
            out.append((self.sems.at[3 * u + 2], blocks, p.peer("z", k), land.at[lead + cut]))
        return out

    def send(self, u, ph):
        arr, _, _, cut = self.plan(u, ph)
        for sem, sel, to, dst in self.moves(u, ph):
            src = self.blocks[arr].at[sel + cut]
            self.sends.start(lambda send, src=src, dst=dst, sem=sem, to=to: remote(src, dst, send, sem, to))

    def add(self, u, ph):
        p = self.p
        arr, d, left, cut = self.plan(u, ph)
        sem, _, to, dst = self.moves(u, ph)[0]
        if d == "z":
            dst = self.landing[arr][1].at[(pl.ds(0, 6) if ph == 1 else pl.ds(4, 3),) + cut]
        remote(dst, dst, sem, sem, to).wait_recv()
        ref, land = self.blocks[arr], self.landing[arr][min(ph, 1)]
        if ph == 2:
            total = ref[p.at("") + cut].astype(F32)
            for k in (4, 5, 6) if d == "z" else (6,):
                total = total + land[(k,) + cut].astype(F32)
            self.final[arr][cut] = total
            return
        for n in range({0: 8, 1: 4 if d != "z" else 2}[ph]):
            idx = {"z": p.z, "y": p.y, "x": p.x}
            if ph == 0:
                lead, other = divmod(n, 2), left.replace("z", "")
                idx["z"], idx[other] = lead
                leads = [lead]
            else:
                idx[left] = n
                leads = [(n,)] if d != "z" else [(2 * k + n,) for k in range(3)]
            sel = (idx["z"], idx["y"], idx["x"]) + cut
            total = ref[sel].astype(F32)
            for lead in leads:
                total = total + land[lead + cut].astype(F32)
            ref[sel] = total.astype(ref.dtype)


IN_OUT, UP, DOWN, SMALL = range(4)
STEP, ISSUE, SHARE = range(3)
SENDS = 56

GATHER_UNITS = [
    (3, 2, 0, 8, 0, 128), (0, 0, 0, 48, 0, 256), (0, 1, 0, 48, 256, 256), (0, 2, 0, 48, 512, 256), (0, 3, 0, 48, 768, 256),
    (0, 6, 0, 48, 1024, 256), (0, 7, 0, 48, 1280, 256), (1, 6, 0, 48, 0, 256), (1, 7, 0, 48, 512, 256),
    (1, 4, 0, 48, 1024, 128), (1, 5, 0, 48, 1280, 128), (1, 6, 0, 48, 256, 256), (1, 7, 0, 48, 768, 256),
    (1, 4, 0, 48, 1152, 128), (1, 5, 0, 48, 1408, 128), (2, 4, 0, 32, 0, 128), (2, 5, 0, 32, 128, 128), (2, 0, 0, 32, 256, 256),
    (2, 1, 0, 32, 512, 256), (2, 4, 32, 32, 0, 128), (2, 5, 32, 32, 128, 128), (2, 0, 32, 32, 256, 256),
    (2, 1, 32, 32, 512, 256), (2, 4, 64, 32, 0, 128), (2, 5, 64, 32, 128, 128), (2, 0, 64, 32, 256, 256),
    (2, 1, 64, 32, 512, 256),
]
GATHER_PLAN = [
    (1, 19, 0, 1), (1, 15, 0, 1), (1, 26, 0, 1), (1, 22, 0, 1), (1, 17, 0, 1), (1, 18, 0, 1), (1, 21, 0, 1), (1, 25, 0, 1),
    (0, 0, ()), (1, 26, 0, 2), (1, 14, 0, 1), (1, 6, 0, 1), (1, 16, 0, 1), (1, 2, 0, 1), (1, 24, 0, 1), (1, 9, 0, 1),
    (1, 19, 1, 1), (1, 13, 0, 1), (1, 3, 0, 1), (1, 1, 0, 1), (1, 0, 0, 1), (1, 10, 0, 1), (1, 4, 0, 1), (1, 26, 0, 3),
    (1, 20, 0, 1), (1, 23, 0, 1), (1, 24, 1, 1), (1, 5, 0, 1), (2, 24, 0), (1, 13, 1, 1), (1, 6, 1, 1), (1, 16, 1, 1),
    (1, 15, 1, 1), (1, 2, 0, 2), (1, 4, 1, 1), (1, 10, 1, 1), (1, 3, 1, 1), (1, 9, 1, 1), (1, 23, 1, 1), (1, 14, 1, 1),
    (1, 1, 0, 2), (1, 26, 1, 1), (1, 20, 1, 1), (1, 5, 1, 1), (1, 2, 0, 3), (2, 19, 0), (1, 17, 0, 2), (2, 13, 0),
    (1, 25, 0, 2), (1, 6, 2, 1), (1, 0, 1, 1), (1, 4, 1, 2), (1, 2, 1, 1), (1, 1, 0, 3), (1, 3, 1, 2), (1, 21, 0, 2),
    (1, 5, 2, 1), (2, 6, 0), (1, 11, 0, 1), (1, 4, 1, 3), (1, 24, 2, 1), (1, 1, 1, 1), (1, 0, 1, 2), (1, 25, 0, 3),
    (1, 2, 2, 1), (1, 3, 1, 3), (1, 22, 0, 2), (1, 8, 0, 1), (1, 18, 0, 2), (1, 13, 2, 1), (1, 4, 2, 1), (2, 5, 0),
    (1, 12, 0, 1), (1, 1, 2, 1), (1, 3, 2, 1), (1, 22, 0, 3), (1, 16, 2, 1), (2, 3, 0), (2, 5, 1), (1, 0, 1, 3), (1, 17, 0, 3),
    (1, 11, 1, 1), (1, 21, 0, 3), (1, 7, 0, 1), (0, 1, ()), (2, 1, 0), (2, 6, 1), (1, 18, 0, 3), (1, 23, 2, 1), (1, 9, 2, 1),
    (2, 10, 0), (1, 8, 1, 1), (2, 2, 0), (1, 0, 2, 1), (2, 4, 1), (1, 14, 2, 1), (1, 15, 2, 1), (2, 0, 0), (1, 20, 2, 1),
    (1, 10, 2, 1), (2, 4, 0), (1, 25, 1, 1), (1, 19, 2, 1), (1, 16, 2, 2), (2, 3, 1), (1, 24, 2, 2), (1, 22, 1, 1), (2, 2, 1),
    (1, 7, 1, 1), (1, 12, 1, 1), (1, 17, 1, 1), (1, 21, 1, 1), (2, 23, 0), (2, 1, 1), (2, 26, 0), (2, 11, 0), (1, 18, 1, 1),
    (1, 11, 2, 1), (1, 23, 2, 2), (1, 13, 2, 2), (0, 3, (1, 2, 3, 4, 5, 6)), (1, 8, 2, 1), (0, 4, ()), (0, 5, ()), (2, 20, 0),
    (1, 10, 2, 2), (2, 7, 0), (1, 9, 2, 2), (2, 0, 1), (0, 6, ()), (2, 12, 0), (1, 12, 2, 1), (1, 19, 2, 2), (2, 8, 0),
    (1, 7, 2, 1), (1, 26, 2, 1), (2, 25, 0), (0, 2, (0,)), (1, 14, 2, 2), (2, 9, 0), (1, 22, 2, 1), (1, 18, 2, 1),
    (1, 17, 2, 1), (1, 20, 2, 2), (2, 14, 0), (2, 22, 0), (2, 17, 0), (0, 7, ()), (1, 13, 2, 3), (0, 8, ()), (0, 9, ()),
    (2, 21, 0), (0, 10, ()), (2, 8, 1), (1, 10, 2, 3), (1, 21, 2, 1), (0, 11, ()), (1, 9, 2, 3), (1, 25, 2, 1), (2, 18, 0),
    (0, 12, ()), (1, 14, 2, 3), (2, 11, 1), (2, 13, 1), (1, 15, 2, 2), (1, 20, 2, 3), (1, 19, 2, 3), (1, 24, 2, 3), (2, 7, 1),
    (0, 13, ()), (2, 12, 1), (2, 16, 0), (2, 9, 1), (1, 23, 2, 3), (2, 10, 1), (1, 16, 2, 3), (2, 14, 1), (2, 15, 0),
    (0, 14, (7, 11)), (2, 26, 1), (2, 20, 1), (1, 15, 2, 3), (2, 17, 1), (0, 15, (8, 12)), (0, 16, (9, 10, 13, 14)), (2, 24, 1),
    (2, 22, 1), (2, 19, 1), (2, 21, 1), (0, 17, ()), (2, 16, 1), (2, 23, 1), (2, 15, 1), (0, 18, ()), (2, 25, 1), (0, 19, ()),
    (2, 18, 1), (0, 20, (15, 16, 19, 20, 23, 24)), (0, 21, (17, 21, 25)), (0, 22, (18, 22, 26)),
]
REDUCE_UNITS = [
    (2, 2, 0, 96, 0, 128), (2, 3, 0, 96, 128, 128), (2, 0, 0, 96, 256, 128), (2, 1, 0, 96, 384, 128), (2, 0, 0, 96, 512, 128),
    (2, 1, 0, 96, 640, 128), (1, 2, 0, 48, 0, 256), (1, 3, 0, 48, 256, 256), (1, 0, 0, 48, 512, 256), (1, 1, 0, 48, 768, 256),
    (1, 0, 0, 48, 1024, 256), (1, 1, 0, 48, 1280, 256), (1, 2, 0, 48, 2688, 128), (1, 3, 0, 48, 2816, 128),
    (1, 0, 0, 48, 2944, 128), (1, 2, 0, 48, 1536, 128), (1, 3, 0, 48, 1664, 128), (1, 0, 0, 48, 1792, 128),
    (1, 0, 0, 48, 1920, 256), (1, 1, 0, 48, 2176, 128), (1, 1, 0, 48, 2304, 256), (1, 0, 0, 48, 2560, 128),
    (3, 3, 0, 8, 0, 128),
]
REDUCE_GROUP = [
    0, 0, 0, 0, 0, 0, 1, 1, 1, 1, 1, 1, 2, 2, 2, 3, 3, 3, 3, 3, 3, 3, 4,
]
REDUCE_PLAN = [
    (0, 23), (0, 27), (0, 28), (0, 24), (1, 1, 0), (1, 0, 0), (0, 29), (0, 30), (0, 25), (1, 2, 0), (0, 31), (0, 32), (1, 3, 0),
    (0, 26), (0, 33), (0, 34), (1, 4, 0), (2, 1, 0), (1, 1, 1), (0, 35), (0, 36), (1, 6, 0), (2, 0, 0), (1, 0, 1), (0, 39),
    (1, 7, 0), (2, 2, 0), (2, 3, 0), (1, 2, 1), (0, 42), (0, 45), (1, 12, 0), (2, 4, 0), (0, 37), (2, 6, 0), (1, 6, 1),
    (1, 8, 0), (1, 9, 0), (1, 13, 0), (0, 43), (1, 3, 1), (2, 2, 1), (1, 2, 2), (1, 4, 1), (0, 44), (1, 5, 0), (2, 12, 0),
    (0, 38), (2, 7, 0), (1, 7, 1), (1, 12, 1), (0, 46), (0, 47), (1, 10, 0), (0, 48), (1, 11, 0), (2, 4, 1), (2, 9, 0),
    (1, 9, 1), (0, 49), (2, 3, 1), (1, 3, 2), (0, 50), (1, 4, 2), (1, 14, 0), (0, 51), (0, 52), (1, 15, 0), (2, 13, 0),
    (1, 13, 1), (1, 16, 0), (0, 40), (2, 8, 0), (2, 9, 1), (1, 9, 2), (1, 17, 0), (1, 8, 1), (2, 10, 0), (2, 5, 0), (1, 10, 1),
    (0, 41), (1, 5, 1), (2, 6, 1), (1, 22, 0), (0, 53), (2, 15, 0), (1, 15, 1), (1, 19, 0), (2, 14, 0), (0, 54), (2, 16, 0),
    (1, 16, 1), (2, 17, 0), (1, 14, 1), (2, 8, 1), (2, 13, 1), (1, 8, 2), (1, 18, 0), (0, 55), (1, 20, 0), (2, 1, 1),
    (2, 11, 0), (2, 7, 1), (2, 10, 1), (2, 5, 1), (1, 5, 2), (0, 56), (2, 19, 0), (1, 19, 1), (2, 12, 1), (1, 11, 1),
    (2, 22, 0), (1, 17, 1), (2, 16, 1), (2, 9, 2), (2, 14, 1), (1, 21, 0), (1, 1, 2), (1, 22, 1), (1, 12, 2), (1, 10, 2),
    (2, 15, 1), (1, 14, 2), (0, 57), (2, 2, 2), (2, 3, 2), (1, 13, 2), (2, 18, 0), (2, 19, 1), (1, 6, 2), (2, 8, 2), (1, 18, 1),
    (1, 19, 2), (2, 20, 0), (2, 11, 1), (1, 11, 2), (1, 20, 1), (2, 17, 1), (1, 16, 2), (2, 1, 2), (2, 22, 1), (1, 17, 2),
    (2, 21, 0), (2, 4, 2), (1, 15, 2), (2, 0, 1), (2, 18, 1), (1, 21, 1), (1, 0, 2), (1, 18, 2), (2, 20, 1), (2, 11, 2),
    (1, 20, 2), (1, 22, 2), (2, 10, 2), (2, 15, 2), (2, 13, 2), (2, 0, 2), (2, 19, 2), (2, 16, 2), (2, 6, 2), (2, 12, 2),
    (1, 7, 2), (2, 21, 1), (2, 17, 2), (2, 14, 2), (1, 21, 2), (2, 7, 2), (2, 5, 2), (2, 18, 2), (2, 22, 2), (2, 20, 2),
    (2, 21, 2),
]


def whole_layer(*refs):
    (
        tokens_in, lengths, cot_in, in_w, out_w, up_w, down_w, b0, b1, b2, b3, b4, b5, b6,
        result, tokens_grad, in_g, out_g, up_g, down_g, small_g,
        WQ, WU, WD, stage_s, stage_r, SP, PV, UB, TS, SIG, QF, KF, VX, SES, SER, LER,
        MSK, CS, USE, LAST, RD, ATT, ATS, N1, S1, F1, NL, NLS, ACT, GP, AT, ATS2, DG, DGS, HGS,
        BG, BGS, PGS, OUT, RB0D, RB1D, RB0W, RB1W, FD, FW, SG, SGR, RB0S, RB1S, FS,
        VEC, HID, tokens, cot, send_sems, gather_sems, reduce_sems, core_sems, hbm, load_sems,
    ) = refs
    p = Place()
    c = p.c

    W5 = {IN_OUT: WQ.reshape(4, 2, 2, 48, FF), UP: WU.reshape(4, 2, 2, 48, FF)}
    WD6 = WD.reshape(4, 2, 2, 2, 96, WIDTH)
    AT4 = AT.reshape(16, 2, 96, ROWS)
    ATS3 = ATS2.reshape(16, 96, ROWS)
    DW = ACT.reshape(2048, WIDTH)

    def gather_view(u, blocks, core):
        arr, _, r0, nr, c0, nc = GATHER_UNITS[u]
        if arr == SMALL:
            return SP.at[blocks + (core,)]
        if arr == DOWN:
            return WD6.at[blocks + (core, pl.ds(r0, nr), pl.ds(c0, nc))]
        return W5[arr].at[blocks + (pl.ds(r0, nr), pl.ds(pl.multiple_of(core * HALF + c0, 128), nc))]

    sends = Sends(send_sems, SENDS)
    gather = Gather(p, GATHER_UNITS, gather_view, sends, gather_sems)
    reduce = Reduce(
        p, REDUCE_UNITS,
        {DOWN: DW.at[pl.ds(0, HALF)].reshape(4, 2, 2, 96, WIDTH), UP: W5[UP], SMALL: SG},
        {DOWN: (RB0D, RB1D), UP: (RB0W, RB1W), SMALL: (RB0S, RB1S)},
        {DOWN: FD, UP: FW, SMALL: FS},
        sends, reduce_sems,
    )
    copies, sent, leaving = [], {}, {}

    def to_core(name, src, dst, mine=None):
        sem = core_sems.at[len(sent)]
        sent[name] = (dst if mine is None else mine, sem)
        leaving[name] = sends.start(lambda send: remote(src, dst, send, sem, p.peer("core")))

    def got(name):
        dst, sem = sent[name]
        remote(dst, dst, sem, sem, p.peer("core")).wait_recv()

    def left(name):
        sends.left(leaving[name])

    def write(src, dst):
        copy = pltpu.make_async_copy(src, dst, hbm.at[len(copies)])
        copy.start()
        copies.append(copy)

    def at128(start, size):
        return pl.ds(pl.multiple_of(start, 128), size)

    def rows_loop(body, carry, rows=slice(0, ROWS), size=64):
        for n in range(rows.start, rows.stop, size):
            carry = body(slice(n, n + size), carry)
        return carry

    def mean(v):
        return jnp.sum(v, axis=1, keepdims=True) * (1.0 / WIDTH)

    def fold(v):
        return jnp.sum(v.reshape(-1, 8, v.shape[1]), axis=0)

    def low_lanes(rows):
        return lax.broadcasted_iota(jnp.int32, (rows, 128), 1) < HEAD

    zero = jnp.zeros((8, WIDTH), F32)
    first_len, second_len = lengths[0, 0], lengths[0, 1]
    first = c * ROWS
    own_half = at128(c * HALF, HALF)
    out_b, n_gain, n_bias, down_b, f_gain, f_bias = (lambda i=i: PV[i : i + 1, :] for i in range(6))

    loads = [pltpu.make_async_copy(a, b, load_sems.at[i]) for i, (a, b) in enumerate(((tokens_in, tokens), (cot_in, cot)))]
    for copy in loads:
        copy.start()
    bar = pltpu.get_barrier_semaphore()
    for to in (p.peer("x"), p.peer("y"), p.peer("core"), p.peer("z", 1), p.peer("z", 2), p.peer("z", 3)):
        pl.semaphore_signal(bar, inc=1, device_id=to, device_id_type=MESH)
    stage_s[0:24, 0:2304] = in_w[...]
    stage_s[0:24, 2304:3072] = out_w[...]
    stage_s[0:24, 3072:6144] = up_w[...]
    WD6[p.z, p.y, p.x, c] = down_w[...]
    FS[...] = jnp.zeros((8, 128), F32)
    for i, ref in enumerate((b0, b1, b2, b3, b4, b5)):
        FS[i : i + 1, 0:24] = ref[...].astype(F32)
    FS[6:7, 0:96] = b6[...].astype(F32)
    SP[p.z, p.y, p.x, c] = FS[...]
    pl.semaphore_wait(bar, 6)
    to_core("stage", stage_s, stage_r)
    to_core("tokens", tokens_in, TS)

    def prep():
        got("stage")
        mine, other = stage_s[0:24, :].astype(F32), stage_r[0:24, :].astype(F32)
        top, bottom = jnp.where(c == 0, mine, other), jnp.where(c == 0, other, mine)
        share = jnp.concatenate([top, bottom], axis=0).astype(BF16)
        W5[IN_OUT][p.z, p.y, p.x, :, own_half] = jnp.where(c == 0, share[:, 0:HALF], share[:, HALF:FF])
        W5[UP][p.z, p.y, p.x, :, own_half] = jnp.where(c == 0, share[:, FF : FF + HALF], share[:, FF + HALF :])

    def docs():
        pos = lax.broadcasted_iota(jnp.int32, (ROWS, 128), 0) + first
        doc = (pos >= first_len).astype(jnp.int32)
        span = jnp.where(doc == 0, first_len, second_len).astype(F32)
        angle = HALF_PI * (pos - doc * first_len).astype(F32) / span
        CS[...] = jnp.where(low_lanes(ROWS), jnp.cos(angle), jnp.sin(angle))
        prior_doc = jnp.where(first > 0, (first - 1 >= first_len).astype(jnp.int32), -1)
        last_doc = (first + (ROWS - 1) >= first_len).astype(jnp.int32)
        USE[...] = (doc == prior_doc).astype(F32)
        LAST[...] = (doc == last_doc).astype(BF16)
        row = lax.broadcasted_iota(jnp.int32, (ROWS, ROWS), 0)
        col = lax.broadcasted_iota(jnp.int32, (ROWS, ROWS), 1)
        row_doc = (row + first >= first_len).astype(jnp.int32)
        col_doc = (col + first >= first_len).astype(jnp.int32)
        MSK[...] = ((col <= row) & (row_doc == col_doc)).astype(BF16)

    def params():
        wide = jnp.zeros((8, 256), F32)
        for step, dst in ((24, PV), (96, UB)):
            n = 384 // step
            for g in range(32 // n):
                total = jnp.zeros((8, 384), F32)
                for k in range(n):
                    d = n * g + k
                    tile = SP[d // 8, (d // 4) % 2, (d // 2) % 2, d % 2]
                    total = total + pltpu.roll(jnp.concatenate([tile, wide], axis=1), step * k, 1)
                dst[:, 384 * g : 384 * (g + 1)] = total

    def project(j):
        if j == 0:
            loads[0].wait()
        rows = tokens[...]
        low = low_lanes(ROWS)
        for k, feat in ((0, QF), (1, KF)):
            raw = dot(rows, WQ[:, k * WIDTH + 256 * j : k * WIDTH + 256 * (j + 1)], 1, 0)
            for i in range(2):
                r = raw[:, 128 * i : 128 * (i + 1)]
                e = jnp.exp(-jnp.abs(r))
                active = jnp.maximum(r, 0.0) + jnp.log1p(e)
                slope = jnp.where(r >= 0, 1.0, e) / (1.0 + e)
                at = k * WIDTH + 256 * j + 128 * i
                SIG[:, at : at + 128] = slope.astype(BF16)
                turned = pltpu.roll(active, HEAD, 1)
                feat[4 * j + 2 * i] = (jnp.where(low, active, turned) * CS[...]).astype(BF16)
                feat[4 * j + 2 * i + 1] = (jnp.where(low, turned, active) * CS[...]).astype(BF16)
        value = dot(rows, WQ[:, 2 * WIDTH + 256 * j : 2 * WIDTH + 256 * (j + 1)], 1, 0)
        for i in range(2):
            v = value[:, 128 * i : 128 * (i + 1)]
            VX[4 * j + 2 * i] = jnp.where(low, v, 1.0).astype(BF16)
            VX[4 * j + 2 * i + 1] = jnp.where(low, 1.0, v).astype(BF16)

    def summary():
        def one(h, carry):
            SES[h] = dot(KF[h] * LAST[...], VX[h], 0, 0).astype(BF16)
            return carry

        lax.fori_loop(0, HEADS, one, 0)
        to_core("state", SES, SER)

    def attend(n):
        if n == 0:
            got("state")
        at = slice(128 * n, 128 * (n + 1))
        low = low_lanes(256)
        for half in range(2):
            width = 256 * (half + 1)
            rows = slice(256 * half, width)
            outs = []
            for h in (2 * n, 2 * n + 1):
                q = QF[h, rows, :]
                scores = dot(q, KF[h, 0:width, :], 1, 1).astype(BF16) * MSK[rows, 0:width]
                outs.append(dot(scores, VX[h, 0:width, :], 1, 0) + USE[rows, :] * dot(q, SER[h], 1, 0))
            numer = jnp.where(low, outs[0], outs[1])
            denom = jnp.where(low, pltpu.roll(outs[0], HEAD, 1), pltpu.roll(outs[1], HEAD, 1))
            inverse = 1.0 / denom
            RD[rows, at] = inverse
            ATT[rows, at] = (numer * inverse).astype(BF16)

    def out_project():
        to_core("attended", ATT, ATS)
        for j in range(3):
            cols = slice(256 * j, 256 * (j + 1))
            F1[:, cols] = (
                tokens[:, cols].astype(F32)
                + dot(ATT[...], WQ[:, 2304 + 256 * j : 2304 + 256 * (j + 1)], 1, 0)
                + out_b()[:, cols]
            )

        def norm(at, carry):
            x = F1[at, :]
            centered = x - mean(x)
            scale = lax.rsqrt(mean(centered * centered) + NORM_EPS)
            normal = centered * scale
            N1[at, :] = normal
            S1[at, :] = jnp.broadcast_to(scale, (normal.shape[0], 128))
            NL[at, :] = (normal * n_gain() + n_bias()).astype(BF16)
            return carry

        rows_loop(norm, 0)
        to_core("normed", NL, NLS)

    def up(j):
        cols = slice(512 * j, 512 * (j + 1))
        hidden = dot(NL[...], WU[:, cols], 1, 0) + UB[6:7, cols]
        phi = 0.5 + 0.5 * lax.erf(hidden * math.sqrt(0.5))
        active = (hidden * phi).astype(BF16)
        slope = phi + hidden * (jnp.exp(-0.5 * hidden * hidden) * (1.0 / math.sqrt(2 * math.pi)))
        GP[:, cols] = slope.astype(BF16)
        AT[cols, :] = active.T
        for piece in range(4):
            a, b = max(512 * j, 768 * piece), min(512 * (j + 1), 768 * (piece + 1))
            if a < b:
                ACT[piece, :, a - 768 * piece : b - 768 * piece] = active[:, a - 512 * j : b - 512 * j]
        if j == 5:
            to_core("activated", AT4.at[:, 1 - c], ATS3)

    def down(j):
        cols = slice(256 * j, 256 * (j + 1))
        total = down_b()[:, cols] + (N1[:, cols] * n_gain()[:, cols] + n_bias()[:, cols])
        for piece in range(4):
            total = total + dot(ACT[piece], WD[768 * piece : 768 * (piece + 1), cols], 1, 0)
        F1[:, cols] = total

    def norm_second():
        loads[1].wait()

        def norm(at, carry):
            gain_sum, bias_sum, down_sum = carry
            x = F1[at, :]
            centered = x - mean(x)
            scale = lax.rsqrt(mean(centered * centered) + NORM_EPS)
            normal = centered * scale
            OUT[at, :] = (normal * f_gain() + f_bias()).astype(BF16)
            ct = cot[at, :].astype(F32)
            e = ct * f_gain()
            grad = scale * (e - mean(e) - normal * mean(e * normal))
            F1[at, :] = grad
            low = grad.astype(BF16)
            DG[at, :] = low
            return gain_sum + fold(ct * normal), bias_sum + fold(ct), down_sum + fold(low.astype(F32))

        half = slice(0, ROWS // 2), slice(ROWS // 2, ROWS)
        sums = rows_loop(norm, (zero, zero, zero), half[0])
        to_core("down", DG.at[half[0]], DGS.at[half[0]])
        sums = rows_loop(norm, sums, half[1])
        to_core("down2", DG.at[half[1]], DGS.at[half[1]])
        for i, s in zip((4, 5, 3), sums):
            VEC[i : i + 1, :] = jnp.sum(s, axis=0, keepdims=True)
        write(OUT, result)

    def down_weight(j):
        cols = slice(256 * j, 256 * (j + 1))
        if j == 0:
            got("activated")
        part = dot(AT4[:, c].reshape(HALF, ROWS), DG[:, cols], 1, 0)
        if j == 0:
            got("down")
            got("down2")
        DW[0:HALF, cols] = (part + dot(ATS2[...], DGS[:, cols], 1, 0)).astype(BF16)

    def free_up():
        while gathered:
            sends.left(gathered.pop())

    def hidden_back(j):
        cols = slice(512 * j, 512 * (j + 1))
        grad = dot(DG[...], WD[cols, :], 1, 1) * GP[:, cols].astype(F32)
        low = grad.astype(BF16)
        GP[:, cols] = low
        HID[0:1, cols] = jnp.sum(low.astype(F32), axis=0, keepdims=True)
        if j == 5:
            to_core("hidden", GP.at[:, at128((1 - c) * HALF, HALF)], HGS)

    def normed_back(j):
        cols = slice(256 * j, 256 * (j + 1))
        F1[:, cols] = F1[:, cols] + dot(GP[...], WU[cols, :], 1, 1)

    def up_weight(j):
        if j == 0:
            free_up()
            got("normed")
            got("hidden")
        cols = slice(512 * j, 512 * (j + 1))
        part = dot(NL[...], GP[:, at128(c * HALF + 512 * j, 512)], 0, 0) + dot(NLS[...], HGS[:, cols], 0, 0)
        WU[:, cols] = part.astype(BF16)

    def norm_first_back():
        def norm(at, carry):
            gain_sum, bias_sum, out_sum = carry
            g, normal, scale = F1[at, :], N1[at, :], S1[at, 0:1]
            e = g * n_gain()
            grad = scale * (e - mean(e) - normal * mean(e * normal))
            F1[at, :] = grad
            low = grad.astype(BF16)
            BG[at, :] = low
            return gain_sum + fold(g * normal), bias_sum + fold(g), out_sum + fold(low.astype(F32))

        sums = rows_loop(norm, (zero, zero, zero))
        to_core("branch", BG.at[:, at128((1 - c) * 384, 384)], BGS)
        for i, s in zip((1, 2, 0), sums):
            VEC[i : i + 1, :] = jnp.sum(s, axis=0, keepdims=True)

    def small_tiles():
        line = lax.broadcasted_iota(jnp.int32, (8, 128), 0)
        lane = lax.broadcasted_iota(jnp.int32, (8, 128), 1)
        for d in range(32):
            g, k = divmod(d, 16)
            part = VEC[:, 384 * g : 384 * (g + 1)]
            a = (pltpu.roll(part, 384 - 24 * k, 1) if k else part)[:, 0:128]
            g, k = divmod(d, 4)
            part = jnp.broadcast_to(HID[0:1, 384 * g : 384 * (g + 1)], (8, 384))
            b = (pltpu.roll(part, 384 - 96 * k, 1) if k else part)[:, 0:128]
            tile = jnp.where((line < 6) & (lane < 24), a, jnp.where((line == 6) & (lane < 96), b, 0.0))
            SGR[0, d % 2, d // 8, (d // 4) % 2, (d // 2) % 2] = tile
        to_core("small", SGR.at[0, 1 - c], SGR.at[1, 0])

    def small_sum():
        got("small")
        SG[...] = SGR[0, c] + SGR[1, 0]

    def slot(h):
        if isinstance(h, int):
            return slice(512 * (h // 4), 512 * (h // 4 + 1)), slice(128 * (h % 4), 128 * (h % 4 + 1))
        return at128(512 * lax.div(h, 4), 512), at128(128 * lax.rem(h, 4), 128)

    def numer_back(j):
        if j == 0:
            left("activated")
            left("state")
        low = low_lanes(ROWS)
        lane = lax.broadcasted_iota(jnp.int32, (ROWS, 128), 1)
        across = low_lanes(128) != (lax.broadcasted_iota(jnp.int32, (128, 128), 0) < HEAD)
        across = across.astype(F32).astype(BF16)
        grads = dot(BG[...], WQ[256 * j : 256 * (j + 1), 2304:FF], 1, 1)
        for i in range(2):
            at = slice(256 * j + 128 * i, 256 * j + 128 * (i + 1))
            ng = grads[:, 128 * i : 128 * (i + 1)] * RD[:, at]
            scaled = ng * ATT[:, at].astype(F32)
            high = scaled.astype(BF16)
            rest = (scaled - high.astype(F32)).astype(BF16)
            dgrad = -(dot(high, across, 1, 0) + dot(rest, across, 1, 0))
            hi = dgrad.astype(BF16).astype(F32)
            beside = jnp.where(
                (lane == 0) | (lane == HEAD), hi, jnp.where((lane == 1) | (lane == HEAD + 1), dgrad - hi, 0.0)
            )
            for par in range(2):
                h = 4 * j + 2 * i + par
                ngx = jnp.where(low, ng, beside) if par == 0 else jnp.where(low, beside, ng)
                AT[slot(h)] = ngx.astype(BF16)
                SES[h] = dot(QF[h], (ngx * USE[...]).astype(BF16), 0, 0).astype(BF16)
        if j == 2:
            to_core("leave", SES, LER)

    def out_weight():
        free_up()
        got("attended")
        part = dot(ATT[...], BG[:, at128(c * 384, 384)], 0, 0)
        got("branch")
        WU[:, 2688:FF] = (part + dot(ATS[...], BGS[...], 0, 0)).astype(BF16)

    def attend_back(j):
        if j == 0:
            left("hidden")
            got("leave")
        n = 3 * (1 - c if j < 3 else c) + j % 3
        low = low_lanes(ROWS)
        lead = c == 0
        last = LAST[...].astype(F32) * jnp.where(lead, 1.0, 0.0).astype(F32)
        m0, m1 = MSK[0:256, 0:256], MSK[256:ROWS, :]
        top, bottom = slice(0, 256), slice(256, ROWS)
        pieces = [], [], []
        for h in (2 * n, 2 * n + 1):
            ngx, qf, kf, vx = AT[slot(h)], QF[h], KF[h], VX[h]
            d0 = dot(ngx[top], vx[top], 1, 1).astype(BF16) * m0
            d1 = dot(ngx[bottom], vx, 1, 1).astype(BF16) * m1
            s0 = dot(qf[top], kf[top], 1, 1).astype(BF16) * m0
            s1 = dot(qf[bottom], kf, 1, 1).astype(BF16) * m1
            q_grad = jnp.concatenate([dot(d0, kf[top], 1, 0), dot(d1, kf, 1, 0)], axis=0)
            k_top = dot(d0, qf[top], 0, 0) + dot(d1[:, top], qf[bottom], 0, 0)
            k_grad = jnp.concatenate([k_top, dot(d1[:, bottom], qf[bottom], 0, 0)], axis=0)
            v_top = dot(s0, ngx[top], 0, 0) + dot(s1[:, top], ngx[bottom], 0, 0)
            v_grad = jnp.concatenate([v_top, dot(s1[:, bottom], ngx[bottom], 0, 0)], axis=0)
            past = dot(jnp.where(lead, vx, ngx), jnp.where(lead, LER[h], SER[h]), 1, 1)
            q_grad = (q_grad + USE[...] * past) * CS[...]
            k_grad = (k_grad + last * past) * CS[...]
            pieces[0].append(q_grad + pltpu.roll(q_grad, HEAD, 1))
            pieces[1].append(k_grad + pltpu.roll(k_grad, HEAD, 1))
            pieces[2].append(v_grad + last * dot(kf, LER[h], 1, 0))
        for k, (even, odd) in enumerate(pieces):
            both = jnp.where(low, even, odd)
            at = at128(k * WIDTH + 128 * n, 128)
            if k < 2:
                both = both * SIG[:, at].astype(F32)
            GP[:, at] = both.astype(BF16)
        if j == 2:
            for k in range(3):
                src = GP.at[:, at128(k * WIDTH + (1 - c) * 384, 384)]
                to_core(("projected", k), src, PGS.at[:, pl.ds(384 * k, 384)])

    def in_weight(j):
        cols = slice(384 * j, 384 * (j + 1))
        if j == 0:
            got("tokens")
        part = dot(tokens[...], GP[:, at128(j * WIDTH + c * 384, 384)], 0, 0)
        got(("projected", j))
        WU[:, HALF + 384 * j : HALF + 384 * (j + 1)] = (part + dot(TS[...], PGS[:, cols], 0, 0)).astype(BF16)

    def tokens_back(j):
        cols = slice(256 * j, 256 * (j + 1))
        F1[:, cols] = F1[:, cols] + dot(GP[:, 0:2304], WQ[cols, 0:2304], 1, 1)
        if j == 2:
            write(F1, tokens_grad)

    steps = []
    for step, count in (
        (prep, 0), (docs, 0), (params, 0), (project, 3), (summary, 0), (attend, 6), (out_project, 0), (up, 6), (down, 3),
        (norm_second, 0), (down_weight, 3), (hidden_back, 6), (normed_back, 3), (up_weight, 3), (norm_first_back, 0),
        (small_tiles, 0), (small_sum, 0), (numer_back, 3), (out_weight, 0), (attend_back, 6),
        (in_weight, 3), (tokens_back, 3),
    ):
        steps += [partial(step, j) for j in range(count)] if count else [step]

    for kind, *op in GATHER_PLAN:
        if kind == STEP:
            for u in op[1]:
                gather.ready(u)
            steps[op[0]]()
        elif kind == ISSUE:
            gather.issue(*op)
        else:
            gather.share(*op)

    gathered = sends.now_open()

    outputs = {1: [(up_g, 0, 0, HALF)], 2: [(out_g, 2688, 0, 384)]}
    outputs[3] = [(in_g, HALF + 384 * k, WIDTH * k, 384) for k in range(3)]
    mine, other = pl.ds(pl.multiple_of(24 * c, 8), 24), pl.ds(pl.multiple_of(24 * (1 - c), 8), 24)
    open_units = list(REDUCE_GROUP)

    def done(u):
        group = REDUCE_GROUP[u]
        open_units.remove(group)
        if group in open_units:
            return
        if group == 0:
            write(FD, down_g)
        elif group == 4:
            small_g[...] = FS[...]
        else:
            for i, (ref, at, to, width) in enumerate(outputs[group]):
                here, there = (ref.at[:, at128(to + core * width, width)] for core in (c, 1 - c))
                to_core((group, i), FW.at[other, pl.ds(at, width)], here, there)
                write(FW.at[mine, pl.ds(at, width)], here)

    for kind, *op in REDUCE_PLAN:
        if kind == STEP:
            steps[op[0]]()
        elif kind == ISSUE:
            reduce.send(*op)
        else:
            reduce.add(*op)
            if op[1] == 2:
                done(op[0])

    for group in outputs:
        for i in range(len(outputs[group])):
            got((group, i))
    sends.finish()
    for copy in copies:
        copy.wait()


def hand_out(*refs):
    made, small, outs, vectors = refs[0:6], refs[6], refs[7:13], refs[13:20]
    held, lines, sems = refs[20:26], refs[26:33], refs[33]
    pieces = []
    for a, b, c in zip(made, held, outs):
        rows = a.shape[0]
        step = 128 if rows == ROWS else rows
        for r in range(0, rows, step):
            pieces.append(tuple(ref.at[pl.ds(r, step)] for ref in (a, b, c)))
    ins = [pltpu.make_async_copy(a, b, sems.at[0, i]) for i, (a, b, _) in enumerate(pieces)]
    back = [pltpu.make_async_copy(b, c, sems.at[1, i]) for i, (_, b, c) in enumerate(pieces)]
    for copy in ins:
        copy.start()
    for i, line in enumerate(lines):
        line[...] = small[i : i + 1, 0 : line.shape[1]]
        back.append(pltpu.make_async_copy(line, vectors[i], sems.at[1, len(pieces) + i]))
        back[-1].start()
    for copy, then in zip(ins, back):
        copy.wait()
        then.start()
    for copy in back:
        copy.wait()


def layer_2x2x4(tokens, lengths, in_weight, out_weight, out_bias, norm_gain, norm_bias, up_weight, up_bias,
                down_weight, down_bias, final_gain, final_bias, cotangent):
    vmem, anywhere = pl.BlockSpec(memory_space=pltpu.VMEM), pl.BlockSpec(memory_space=pl.ANY)

    def v(*shape, dtype=BF16):
        return pltpu.VMEM(shape, dtype)

    dma = pltpu.SemaphoreType.DMA
    scratch = [
        v(WIDTH, FF), v(WIDTH, FF), v(FF, WIDTH),
        v(32, 6144), v(32, 6144), v(4, 2, 2, 2, 8, 128, dtype=F32),
        v(8, WIDTH, dtype=F32), v(8, FF, dtype=F32),
        v(ROWS, WIDTH), v(ROWS, HALF),
        v(HEADS, ROWS, 128), v(HEADS, ROWS, 128), v(HEADS, ROWS, 128),
        v(HEADS, 128, 128), v(HEADS, 128, 128), v(HEADS, 128, 128),
        v(ROWS, ROWS), v(ROWS, 128, dtype=F32), v(ROWS, 128, dtype=F32), v(ROWS, 128),
        v(ROWS, WIDTH, dtype=F32), v(ROWS, WIDTH), v(ROWS, WIDTH),
        v(ROWS, WIDTH, dtype=F32), v(ROWS, 128, dtype=F32), v(ROWS, WIDTH, dtype=F32),
        v(ROWS, WIDTH), v(ROWS, WIDTH), v(4, ROWS, WIDTH), v(ROWS, FF),
        v(FF, ROWS), v(HALF, ROWS), v(ROWS, WIDTH), v(ROWS, WIDTH), v(ROWS, HALF),
        v(ROWS, WIDTH), v(ROWS, 384), v(ROWS, 1152), v(ROWS, WIDTH),
        v(4, 2, 96, WIDTH), v(7, 96, WIDTH),
        v(4, 2, 48, FF), v(7, 48, FF),
        v(96, WIDTH, dtype=F32), v(48, FF, dtype=F32),
        v(4, 2, 2, 8, 128, dtype=F32), v(2, 2, 4, 2, 2, 8, 128, dtype=F32),
        v(4, 2, 8, 128, dtype=F32), v(7, 8, 128, dtype=F32), v(8, 128, dtype=F32),
        v(8, WIDTH, dtype=F32), v(8, FF, dtype=F32),
        v(ROWS, WIDTH), v(ROWS, WIDTH),
        dma((SENDS,)), dma((6 * len(GATHER_UNITS),)), dma((3 * len(REDUCE_UNITS),)), dma((20,)), dma((10,)), dma((2,)),
    ]
    shapes = (
        jax.ShapeDtypeStruct((ROWS, WIDTH), BF16),
        jax.ShapeDtypeStruct((ROWS, WIDTH), F32),
        jax.ShapeDtypeStruct((24, 2304), F32),
        jax.ShapeDtypeStruct((24, WIDTH), F32),
        jax.ShapeDtypeStruct((24, FF), F32),
        jax.ShapeDtypeStruct((96, WIDTH), F32),
    )
    lines = (jax.ShapeDtypeStruct((1, 24), F32),) * 6 + (jax.ShapeDtypeStruct((1, 96), F32),)
    vectors = (out_bias, norm_gain, norm_bias, down_bias, final_gain, final_bias, up_bias)
    made = pl.pallas_call(
        whole_layer,
        out_shape=shapes + (jax.ShapeDtypeStruct((8, 128), F32),),
        in_specs=[anywhere, pl.BlockSpec(memory_space=pltpu.SMEM), anywhere] + [vmem] * 11,
        out_specs=(anywhere,) * 6 + (vmem,),
        scratch_shapes=scratch,
        compiler_params=pltpu.CompilerParams(
            collective_id=0, has_side_effects=True, vmem_limit_bytes=VMEM_LIMIT
        ),
    )(tokens, lengths, cotangent, in_weight, out_weight, up_weight, down_weight, *(b.reshape(1, -1) for b in vectors))
    result, tokens_grad, in_g, out_g, up_g, down_g, *small = pl.pallas_call(
        hand_out,
        out_shape=shapes + lines,
        in_specs=[anywhere] * 6 + [vmem],
        out_specs=(anywhere,) * 13,
        scratch_shapes=[pltpu.VMEM(s.shape, s.dtype) for s in shapes + lines] + [dma((2, 19))],
        compiler_params=pltpu.CompilerParams(vmem_limit_bytes=VMEM_LIMIT),
    )(*made)
    out_bias_g, norm_gain_g, norm_bias_g, down_bias_g, final_gain_g, final_bias_g, up_bias_g = (
        g.reshape(-1) for g in small
    )
    return (result, tokens_grad, in_g, out_g, out_bias_g, norm_gain_g, norm_bias_g, up_g,
            up_bias_g, down_g, down_bias_g, final_gain_g, final_bias_g)


VMEM_LIMIT = 64 * 2**20 - 2**18


def solution(mesh):
    both = ("dp", "fsdp")
    rows, vector = P(both, None), P(both)
    in_specs = (rows, P("dp", None), rows, rows, vector, vector, vector, rows, vector, rows, vector, vector, vector, rows)
    out_specs = (rows, rows, rows, rows, vector, vector, vector, rows, vector, rows, vector, vector, vector)
    body = layer_2x2x4 if dict(mesh.shape) == {"dp": 16, "fsdp": 2} else per_device
    return jax.shard_map(body, mesh=mesh, in_specs=in_specs, out_specs=out_specs, check_vma=False)
```

```python
from functools import partial
import math

import jax
import jax.numpy as jnp
from jax import lax
from jax.experimental import pallas as pl
from jax.experimental.pallas import tpu as pltpu
from jax.sharding import PartitionSpec as P

HEADS = 12
HEAD = 64
BLOCK = 512


HALF_PI = math.pi / 2
NORM_EPS = 1e-05

def prefix(shard, axis, combine, identity, reverse):
    devices, position = (lax.axis_size(axis), lax.axis_index(axis))
    everything = jax.tree.map(lambda part: lax.all_gather(part, axis), shard)
    start = jax.tree.map(
        lambda part, zero: jnp.broadcast_to(jnp.asarray(zero, part.dtype), part.shape),
        shard,
        identity,
    )

    def turn(k, before):
        at = devices - 1 - k if reverse else k
        reached = at > position if reverse else at < position
        new = combine(before, jax.tree.map(lambda part: part[at], everything))
        return jax.tree.map(lambda a, b: jnp.where(reached, a, b), new, before)

    return lax.fori_loop(0, devices, turn, start)


def documents(position, pair):
    first_len = pair[0]
    doc = (position >= first_len).astype(jnp.int32)
    start = doc * first_len
    span = jnp.where(doc == 0, first_len, pair[1])
    angle = HALF_PI * (position - start).astype(jnp.float32) / span.astype(jnp.float32)
    return (doc, angle)


def features(heads, angle):
    active = jax.nn.softplus(heads)
    return jnp.concatenate(
        [active * jnp.cos(angle)[None, :, None], active * jnp.sin(angle)[None, :, None]], axis=2
    )


def layer_norm(rows, gain, shift):
    mean = jnp.mean(rows, axis=-1, keepdims=True)
    centered = rows - mean
    scale = lax.rsqrt(jnp.mean(centered * centered, axis=-1, keepdims=True) + NORM_EPS)
    return centered * scale * gain + shift


def exact_gelu(values):
    return jax.nn.gelu(values, approximate=False)


def merge_state(earlier, later):
    return (
        later[0] + later[2] * earlier[0],
        later[1] + later[2] * earlier[1],
        later[2] * earlier[2],
    )


def block_forward(query, keys, values, doc_blk, state, norm, carry_doc):
    order = jnp.arange(doc_blk.shape[0], dtype=jnp.int32)
    mask = (order[None, :] <= order[:, None]) & (doc_blk[None, :] == doc_blk[:, None])
    raw = jnp.einsum("hif,hjf->hij", query, keys, preferred_element_type=jnp.float32)
    scores = jnp.where(mask[None], raw, 0.0)
    use = (doc_blk == carry_doc).astype(jnp.float32)
    carried = jnp.einsum(
        "hef,hif->hei", state.astype(jnp.bfloat16), query, preferred_element_type=jnp.float32
    )
    numer = (
        jnp.einsum(
            "hej,hij->hei", values, scores.astype(jnp.bfloat16), preferred_element_type=jnp.float32
        )
        + use * carried
    )
    denom = jnp.sum(scores, axis=2) + use * jnp.einsum(
        "hf,hif->hi", norm, query.astype(jnp.float32)
    )
    return (mask, scores, use, numer, denom)


def block_summary(keys, values, doc_blk):
    chosen = doc_blk == doc_blk[-1]
    picked = jnp.where(chosen[None, :, None], keys, jnp.zeros((), keys.dtype))
    state = jnp.einsum("hej,hjf->hef", values, picked, preferred_element_type=jnp.float32)
    norm = jnp.sum(picked.astype(jnp.float32), axis=1)
    return (chosen, picked, state, norm)


def per_device(
    tokens,
    lengths,
    in_weight,
    out_weight,
    out_bias,
    norm_gain,
    norm_bias,
    up_weight,
    up_bias,
    down_weight,
    down_bias,
    final_gain,
    final_bias,
    cotangent,
):
    rows = tokens.shape[0]
    width = tokens.shape[1]
    count = rows // BLOCK
    gathered = (
        lax.all_gather(in_weight, ("dp", "fsdp"), axis=0, tiled=True),
        lax.all_gather(out_weight, ("dp", "fsdp"), axis=0, tiled=True),
        lax.all_gather(out_bias, ("dp", "fsdp"), axis=0, tiled=True),
        lax.all_gather(norm_gain, ("dp", "fsdp"), axis=0, tiled=True),
        lax.all_gather(norm_bias, ("dp", "fsdp"), axis=0, tiled=True),
        lax.all_gather(up_weight, ("dp", "fsdp"), axis=0, tiled=True),
        lax.all_gather(up_bias, ("dp", "fsdp"), axis=0, tiled=True),
        lax.all_gather(down_weight, ("dp", "fsdp"), axis=0, tiled=True),
        lax.all_gather(down_bias, ("dp", "fsdp"), axis=0, tiled=True),
        lax.all_gather(final_gain, ("dp", "fsdp"), axis=0, tiled=True),
        lax.all_gather(final_bias, ("dp", "fsdp"), axis=0, tiled=True),
    )
    (
        inward,
        outward,
        out_shift,
        gain_first,
        shift_first,
        upward,
        up_shift,
        downward,
        down_shift,
        gain_second,
        shift_second,
    ) = gathered
    first = lax.axis_index("fsdp") * rows
    position = first + jnp.arange(rows, dtype=jnp.int32)
    pair = lengths[0]
    doc, angle = documents(position, pair)
    prior_doc = jnp.where(first > 0, (first - 1 >= pair[0]).astype(jnp.int32), -1)
    projected = jnp.dot(tokens, inward, preferred_element_type=jnp.float32)
    query_raw = projected[:, :width].reshape(rows, HEADS, HEAD).transpose(1, 0, 2)
    key_raw = projected[:, width : 2 * width].reshape(rows, HEADS, HEAD).transpose(1, 0, 2)
    query_feat, query_pull = jax.vjp(partial(features, angle=angle), query_raw)
    key_feat, key_pull = jax.vjp(partial(features, angle=angle), key_raw)
    query = query_feat.astype(jnp.bfloat16)
    keys = key_feat.astype(jnp.bfloat16)
    values = (
        projected[:, 2 * width :].reshape(rows, HEADS, HEAD).transpose(1, 2, 0).astype(jnp.bfloat16)
    )
    device_summary = block_summary(keys, values, doc)
    device_keep = (prior_doc == doc[-1]).astype(jnp.float32)
    identity = (
        jnp.zeros_like(device_summary[2]),
        jnp.zeros_like(device_summary[3]),
        jnp.ones((), jnp.float32),
    )
    state, norm, passed = prefix(
        (device_summary[2], device_summary[3], device_keep), "fsdp", merge_state, identity, False
    )
    keys_blk = keys
    values_blk = values
    doc_blk = doc
    carries = [(state, norm, prior_doc)]
    outcome = block_forward(query, keys_blk, values_blk, doc_blk, state, norm, prior_doc)
    ratios = outcome[3] / outcome[4][:, None, :]
    summary = block_summary(keys_blk, values_blk, doc_blk)
    attended = ratios.transpose(2, 0, 1).reshape(rows, width).astype(jnp.bfloat16)
    branch = jnp.dot(attended, outward, preferred_element_type=jnp.float32) + out_shift.astype(
        jnp.float32
    )
    first_sum = tokens.astype(jnp.float32) + branch
    normed, first_pull = jax.vjp(
        layer_norm, first_sum, gain_first.astype(jnp.float32), shift_first.astype(jnp.float32)
    )
    normed_low = normed.astype(jnp.bfloat16)
    hidden = jnp.dot(normed_low, upward, preferred_element_type=jnp.float32) + up_shift.astype(
        jnp.float32
    )
    activated, gelu_pull = jax.vjp(exact_gelu, hidden)
    activated_low = activated.astype(jnp.bfloat16)
    second_sum = (
        normed
        + jnp.dot(activated_low, downward, preferred_element_type=jnp.float32)
        + down_shift.astype(jnp.float32)
    )
    result, second_pull = jax.vjp(
        layer_norm, second_sum, gain_second.astype(jnp.float32), shift_second.astype(jnp.float32)
    )
    again = (
        lax.all_gather(in_weight, ("dp", "fsdp"), axis=0, tiled=True),
        lax.all_gather(out_weight, ("dp", "fsdp"), axis=0, tiled=True),
        lax.all_gather(out_bias, ("dp", "fsdp"), axis=0, tiled=True),
        lax.all_gather(norm_gain, ("dp", "fsdp"), axis=0, tiled=True),
        lax.all_gather(norm_bias, ("dp", "fsdp"), axis=0, tiled=True),
        lax.all_gather(up_weight, ("dp", "fsdp"), axis=0, tiled=True),
        lax.all_gather(up_bias, ("dp", "fsdp"), axis=0, tiled=True),
        lax.all_gather(down_weight, ("dp", "fsdp"), axis=0, tiled=True),
        lax.all_gather(down_bias, ("dp", "fsdp"), axis=0, tiled=True),
        lax.all_gather(final_gain, ("dp", "fsdp"), axis=0, tiled=True),
        lax.all_gather(final_bias, ("dp", "fsdp"), axis=0, tiled=True),
    )
    inward = again[0]
    outward = again[1]
    upward = again[5]
    downward = again[7]
    second_grad, final_gain_grad, final_shift_grad = second_pull(cotangent.astype(jnp.float32))
    down_grad = second_grad.astype(jnp.bfloat16)
    down_weight_grad = jnp.dot(activated_low.T, down_grad, preferred_element_type=jnp.float32)
    down_shift_grad = jnp.sum(down_grad.astype(jnp.float32), axis=0)
    (activated_grad,) = gelu_pull(
        jnp.dot(down_grad, downward.T, preferred_element_type=jnp.float32)
    )
    hidden_grad = activated_grad.astype(jnp.bfloat16)
    up_weight_grad = jnp.dot(normed_low.T, hidden_grad, preferred_element_type=jnp.float32)
    up_shift_grad = jnp.sum(hidden_grad.astype(jnp.float32), axis=0)
    normed_grad = second_grad + jnp.dot(hidden_grad, upward.T, preferred_element_type=jnp.float32)
    first_grad, norm_gain_grad, norm_shift_grad = first_pull(normed_grad)
    branch_grad = first_grad.astype(jnp.bfloat16)
    out_weight_grad = jnp.dot(attended.T, branch_grad, preferred_element_type=jnp.float32)
    out_shift_grad = jnp.sum(branch_grad.astype(jnp.float32), axis=0)
    attended_grad = jnp.dot(branch_grad, outward.T, preferred_element_type=jnp.float32)
    ratio_grad = attended_grad.reshape(rows, HEADS, HEAD).transpose(1, 2, 0)
    index = 0
    keys_blk = keys
    values_blk = values
    doc_blk = doc
    state_in, norm_in, doc_in = carries[index]
    mask, scores, use, numer, denom = block_forward(
        query, keys_blk, values_blk, doc_blk, state_in, norm_in, doc_in
    )
    numer_grad = (ratio_grad / denom[:, None, :]).astype(jnp.bfloat16)
    denom_grad = -jnp.sum(ratio_grad * numer, axis=1) / (denom * denom)
    scores_grad = (
        jnp.einsum("hei,hej->hij", numer_grad, values_blk, preferred_element_type=jnp.float32)
        + denom_grad[:, :, None]
    )
    scores_grad = jnp.where(mask[None], scores_grad, 0.0).astype(jnp.bfloat16)
    used_numer = jnp.where(use[None, None, :] > 0, numer_grad, jnp.zeros((), jnp.bfloat16))
    used_denom = use * denom_grad
    query_part = jnp.einsum(
        "hij,hjf->hif", scores_grad, keys_blk, preferred_element_type=jnp.float32
    )
    query_part = query_part + jnp.einsum(
        "hei,hef->hif",
        used_numer,
        state_in.astype(jnp.bfloat16),
        preferred_element_type=jnp.float32,
    )
    query_grads = query_part + used_denom[:, :, None] * norm_in[:, None, :]
    key_grads = [jnp.einsum("hij,hif->hjf", scores_grad, query, preferred_element_type=jnp.float32)]
    value_grads = [
        jnp.einsum(
            "hei,hij->hej",
            numer_grad,
            scores.astype(jnp.bfloat16),
            preferred_element_type=jnp.float32,
        )
    ]
    contribs = [
        (
            jnp.einsum("hei,hif->hef", used_numer, query, preferred_element_type=jnp.float32),
            jnp.einsum("hi,hif->hf", used_denom, query.astype(jnp.float32)),
        )
    ]
    keeps = [(doc_in == doc_blk[-1]).astype(jnp.float32)]
    local_state = jnp.zeros_like(device_summary[2])
    local_norm = jnp.zeros_like(device_summary[3])
    for index in reversed(range(count)):
        local_state = contribs[index][0] + keeps[index] * local_state
        local_norm = contribs[index][1] + keeps[index] * local_norm
    leave_state, leave_norm, through = prefix(
        (local_state, local_norm, device_keep), "fsdp", merge_state, identity, True
    )
    for index in reversed(range(count)):
        keys_blk = keys
        values_blk = values
        doc_blk = doc
        summary = block_summary(keys_blk, values_blk, doc_blk)
        state_low = leave_state.astype(jnp.bfloat16)
        key_extra = (
            jnp.einsum("hej,hef->hjf", values_blk, state_low, preferred_element_type=jnp.float32)
            + leave_norm[:, None, :]
        )
        key_grads[index] = key_grads[index] + jnp.where(summary[0][None, :, None], key_extra, 0.0)
        value_grads[index] = value_grads[index] + jnp.einsum(
            "hef,hjf->hej", state_low, summary[1], preferred_element_type=jnp.float32
        )
        leave_state = contribs[index][0] + keeps[index] * leave_state
        leave_norm = contribs[index][1] + keeps[index] * leave_norm
    (query_raw_grad,) = query_pull(query_grads)
    (key_raw_grad,) = key_pull(key_grads[0])
    value_grad = value_grads[0].transpose(2, 0, 1).reshape(rows, width)
    projected_grad = jnp.concatenate(
        [
            query_raw_grad.transpose(1, 0, 2).reshape(rows, width),
            key_raw_grad.transpose(1, 0, 2).reshape(rows, width),
            value_grad,
        ],
        axis=1,
    ).astype(jnp.bfloat16)
    in_weight_grad = jnp.dot(tokens.T, projected_grad, preferred_element_type=jnp.float32)
    tokens_grad = first_grad + jnp.dot(projected_grad, inward.T, preferred_element_type=jnp.float32)
    summed = (
        lax.psum_scatter(in_weight_grad, ("dp", "fsdp"), scatter_dimension=0, tiled=True),
        lax.psum_scatter(out_weight_grad, ("dp", "fsdp"), scatter_dimension=0, tiled=True),
        lax.psum_scatter(out_shift_grad, ("dp", "fsdp"), scatter_dimension=0, tiled=True),
        lax.psum_scatter(norm_gain_grad, ("dp", "fsdp"), scatter_dimension=0, tiled=True),
        lax.psum_scatter(norm_shift_grad, ("dp", "fsdp"), scatter_dimension=0, tiled=True),
        lax.psum_scatter(up_weight_grad, ("dp", "fsdp"), scatter_dimension=0, tiled=True),
        lax.psum_scatter(up_shift_grad, ("dp", "fsdp"), scatter_dimension=0, tiled=True),
        lax.psum_scatter(down_weight_grad, ("dp", "fsdp"), scatter_dimension=0, tiled=True),
        lax.psum_scatter(down_shift_grad, ("dp", "fsdp"), scatter_dimension=0, tiled=True),
        lax.psum_scatter(final_gain_grad, ("dp", "fsdp"), scatter_dimension=0, tiled=True),
        lax.psum_scatter(final_shift_grad, ("dp", "fsdp"), scatter_dimension=0, tiled=True),
    )
    return (result.astype(jnp.bfloat16), tokens_grad) + tuple(summed)


MESH = pl.DeviceIdType.MESH
F32 = jnp.float32
BF16 = jnp.bfloat16
ROWS = 512
WIDTH = 768
FF = 3072
HALF = 1536
GATHER_ORDER = ("zyx", "zxy", "xzy", "yzx", "xyz", "yxz", "zyx", "zxy")
DIRECT = (6, 7)
REDUCE_ORDER = ("xyz", "yxz", "yzx", "xzy")


def dot(a, b, ca, cb):
    return lax.dot_general(a, b, (((ca,), (cb,)), ((), ())), preferred_element_type=F32)


class Place:
    def __init__(self):
        self.dp = lax.axis_index("dp")
        self.c = lax.axis_index("fsdp")
        self.x = lax.rem(self.dp, 2)
        self.y = lax.rem(lax.div(self.dp, 2), 2)
        self.z = lax.div(self.dp, 4)

    def peer(self, d, k=1):
        if d == "x":
            return (self.dp + 1 - 2 * self.x, self.c)
        if d == "y":
            return (self.dp + 2 - 4 * self.y, self.c)
        if d == "z":
            return (lax.rem(self.dp + 4 * k, 16), self.c)
        if d == "up":
            return (self.dp + 4, self.c)
        if d == "down":
            return (self.dp - 4, self.c)
        return (self.dp, 1 - self.c)

    def at(self, known, flip=None, z=None):
        out = []
        for d in "zyx":
            if d in known:
                out.append(slice(None))
                continue
            v = getattr(self, d)
            if flip == d:
                v = 1 - v
            if d == "z" and z is not None:
                v = z
            out.append(v)
        return tuple(out)


def remote(src, dst, send, recv, to):
    return pltpu.make_async_remote_copy(
        src_ref=src, dst_ref=dst, send_sem=send, recv_sem=recv, device_id=to, device_id_type=MESH
    )


def guarded(cond, action):
    if cond is None:
        action()
    else:
        pl.when(cond)(action)


class Sends:
    def __init__(self, sems, size):
        self.sems, self.size, self.count, self.open = sems, size, 0, {}

    def start(self, make, cond=None):
        i = self.count % self.size
        self.count += 1
        self.wait(i)
        guarded(cond, lambda: make(self.sems.at[i]).start())
        self.open[i] = (cond, make)
        return i, make

    def wait(self, i):
        if i in self.open:
            cond, make = self.open.pop(i)
            guarded(cond, lambda: make(self.sems.at[i]).wait_send())

    def left(self, handle):
        if self.open.get(handle[0], (None, None))[1] is handle[1]:
            self.wait(handle[0])

    def now_open(self):
        return [(i, make) for i, (_, make) in self.open.items()]

    def finish(self):
        for i in list(self.open):
            self.wait(i)


class Gather:
    def __init__(self, place, units, view, sends, sems):
        self.p, self.units, self.view, self.sends, self.sems = place, units, view, sends, sems
        self.waited = set()

    def order(self, u):
        return GATHER_ORDER[self.units[u][1]]

    def copy(self, u, slot, blocks, to):
        src = self.view(u, blocks, self.p.c)
        return lambda sem: remote(src, src, sem, self.sems.at[6 * u + slot], to)

    def issue(self, u, ph, hop):
        p, o = self.p, self.order(u)
        known, d = o[:ph], o[ph]
        if hop == 1 and ph > 0:
            self.arrive(u, ph - 1)
        if d != "z":
            self.sends.start(self.copy(u, "xy".index(d), p.at(known), p.peer(d)))
            return
        if self.units[u][1] in DIRECT:
            for k in (1, 2, 3):
                self.sends.start(self.copy(u, 2, p.at(known), p.peer("z", k)))
            return
        if hop > 1:
            self.arrive_hop(u, ph, hop - 1)
        up = (jnp.logical_and(p.z < 3, p.z - (hop - 1) >= 0), p.z - (hop - 1), p.peer("up"))
        down = (jnp.logical_and(p.z > 0, p.z + (hop - 1) <= 3), p.z + (hop - 1), p.peer("down"))
        for cond, z, to in (up, down):
            self.sends.start(self.copy(u, 1 + hop, p.at(known, z=z), to), cond)

    def expect(self, u, slot, blocks, core):
        dst = self.view(u, blocks, core)
        remote(dst, dst, self.sems.at[6 * u + slot], self.sems.at[6 * u + slot], self.p.peer("core")).wait_recv()

    def arrive_hop(self, u, ph, hop):
        if (u, ph, hop) in self.waited:
            return
        self.waited.add((u, ph, hop))
        p, known = self.p, self.order(u)[:ph]
        above, below = p.z + hop <= 3, p.z - hop >= 0
        one = jnp.logical_xor(above, below)
        guarded(one, lambda: self.expect(u, 1 + hop, p.at(known), p.c))
        if hop == 1:
            two = jnp.logical_and(above, below)
            guarded(two, lambda: self.expect(u, 1 + hop, (pl.ds(0, 2),) + p.at(known)[1:], p.c))

    def arrive(self, u, ph):
        p, o = self.p, self.order(u)
        known, d = o[:ph], o[ph]
        if d == "z" and self.units[u][1] not in DIRECT:
            for hop in (1, 2, 3):
                self.arrive_hop(u, ph, hop)
        elif (u, ph, 0) not in self.waited:
            self.waited.add((u, ph, 0))
            if d == "z":
                self.expect(u, 2, (pl.ds(0, 3),) + p.at(known)[1:], p.c)
            else:
                self.expect(u, "xy".index(d), p.at(known, flip=d), p.c)

    def shared(self, u, part):
        o = self.order(u)
        if o[2] == "z":
            return self.p.at(o) if part else None
        return self.p.at(o[:2], flip=o[2] if part else None)

    def share(self, u, part):
        if self.shared(u, part):
            self.arrive(u, 1 + part)
            self.sends.start(self.copy(u, 5, self.shared(u, part), self.p.peer("core")))

    def ready(self, u):
        if (u, 0) not in self.waited:
            self.waited.add((u, 0))
            self.expect(u, 5, self.p.at("zyx"), 1 - self.p.c)


class Reduce:
    def __init__(self, place, units, blocks, landing, final, sends, sems):
        self.p, self.units = place, units
        self.blocks, self.landing, self.final = blocks, landing, final
        self.sends, self.sems = sends, sems

    def plan(self, u, ph):
        arr, kind, r0, nr, c0, nc = self.units[u]
        o = REDUCE_ORDER[kind]
        return arr, o[ph], o[ph + 1 :], (pl.ds(r0, nr), pl.ds(c0, nc))

    def moves(self, u, ph):
        p = self.p
        arr, d, left, cut = self.plan(u, ph)
        land = self.landing[arr][min(ph, 1)]
        if d != "z":
            lead = {0: (slice(None), slice(None)), 1: (pl.ds(0, 4),), 2: (6,)}[ph]
            return [(self.sems.at[3 * u + "xy".index(d)], p.at(left, flip=d), p.peer(d), land.at[lead + cut])]
        out = []
        for k in (1, 2, 3):
            lead = (pl.ds(2 * (k - 1), 2),) if ph == 1 else (3 + k,)
            blocks = p.at(left, z=lax.rem(p.z + k, 4))
            out.append((self.sems.at[3 * u + 2], blocks, p.peer("z", k), land.at[lead + cut]))
        return out

    def send(self, u, ph):
        arr, _, _, cut = self.plan(u, ph)
        for sem, sel, to, dst in self.moves(u, ph):
            src = self.blocks[arr].at[sel + cut]
            self.sends.start(lambda send, src=src, dst=dst, sem=sem, to=to: remote(src, dst, send, sem, to))

    def add(self, u, ph):
        p = self.p
        arr, d, left, cut = self.plan(u, ph)
        sem, _, to, dst = self.moves(u, ph)[0]
        if d == "z":
            dst = self.landing[arr][1].at[(pl.ds(0, 6) if ph == 1 else pl.ds(4, 3),) + cut]
        remote(dst, dst, sem, sem, to).wait_recv()
        ref, land = self.blocks[arr], self.landing[arr][min(ph, 1)]
        if ph == 2:
            total = ref[p.at("") + cut].astype(F32)
            for k in (4, 5, 6) if d == "z" else (6,):
                total = total + land[(k,) + cut].astype(F32)
            self.final[arr][cut] = total
            return
        for n in range({0: 8, 1: 4 if d != "z" else 2}[ph]):
            idx = {"z": p.z, "y": p.y, "x": p.x}
            if ph == 0:
                lead, other = divmod(n, 2), left.replace("z", "")
                idx["z"], idx[other] = lead
                leads = [lead]
            else:
                idx[left] = n
                leads = [(n,)] if d != "z" else [(2 * k + n,) for k in range(3)]
            sel = (idx["z"], idx["y"], idx["x"]) + cut
            total = ref[sel].astype(F32)
            for lead in leads:
                total = total + land[lead + cut].astype(F32)
            ref[sel] = total.astype(ref.dtype)


IN_OUT, UP, DOWN, SMALL = range(4)
STEP, ISSUE, SHARE = range(3)
SENDS = 56

GATHER_UNITS = [
    (3, 2, 0, 8, 0, 128), (0, 0, 0, 48, 0, 256), (0, 1, 0, 48, 256, 256), (0, 2, 0, 48, 512, 256), (0, 3, 0, 48, 768, 256),
    (0, 6, 0, 48, 1024, 256), (0, 7, 0, 48, 1280, 256), (1, 6, 0, 48, 0, 256), (1, 7, 0, 48, 512, 256),
    (1, 4, 0, 48, 1024, 128), (1, 5, 0, 48, 1280, 128), (1, 6, 0, 48, 256, 256), (1, 7, 0, 48, 768, 256),
    (1, 4, 0, 48, 1152, 128), (1, 5, 0, 48, 1408, 128), (2, 4, 0, 32, 0, 128), (2, 5, 0, 32, 128, 128), (2, 0, 0, 32, 256, 256),
    (2, 1, 0, 32, 512, 256), (2, 4, 32, 32, 0, 128), (2, 5, 32, 32, 128, 128), (2, 0, 32, 32, 256, 256),
    (2, 1, 32, 32, 512, 256), (2, 4, 64, 32, 0, 128), (2, 5, 64, 32, 128, 128), (2, 0, 64, 32, 256, 256),
    (2, 1, 64, 32, 512, 256),
]
GATHER_PLAN = [
    (1, 19, 0, 1), (1, 15, 0, 1), (1, 26, 0, 1), (1, 22, 0, 1), (1, 17, 0, 1), (1, 18, 0, 1), (1, 21, 0, 1), (1, 25, 0, 1),
    (0, 0, ()), (1, 26, 0, 2), (1, 14, 0, 1), (1, 6, 0, 1), (1, 16, 0, 1), (1, 2, 0, 1), (1, 24, 0, 1), (1, 9, 0, 1),
    (1, 19, 1, 1), (1, 13, 0, 1), (1, 3, 0, 1), (1, 1, 0, 1), (1, 0, 0, 1), (1, 10, 0, 1), (1, 4, 0, 1), (1, 26, 0, 3),
    (1, 20, 0, 1), (1, 23, 0, 1), (1, 24, 1, 1), (1, 5, 0, 1), (2, 24, 0), (1, 13, 1, 1), (1, 6, 1, 1), (1, 16, 1, 1),
    (1, 15, 1, 1), (1, 2, 0, 2), (1, 4, 1, 1), (1, 10, 1, 1), (1, 3, 1, 1), (1, 9, 1, 1), (1, 23, 1, 1), (1, 14, 1, 1),
    (1, 1, 0, 2), (1, 26, 1, 1), (1, 20, 1, 1), (1, 5, 1, 1), (1, 2, 0, 3), (2, 19, 0), (1, 17, 0, 2), (2, 13, 0),
    (1, 25, 0, 2), (1, 6, 2, 1), (1, 0, 1, 1), (1, 4, 1, 2), (1, 2, 1, 1), (1, 1, 0, 3), (1, 3, 1, 2), (1, 21, 0, 2),
    (1, 5, 2, 1), (2, 6, 0), (1, 11, 0, 1), (1, 4, 1, 3), (1, 24, 2, 1), (1, 1, 1, 1), (1, 0, 1, 2), (1, 25, 0, 3),
    (1, 2, 2, 1), (1, 3, 1, 3), (1, 22, 0, 2), (1, 8, 0, 1), (1, 18, 0, 2), (1, 13, 2, 1), (1, 4, 2, 1), (2, 5, 0),
    (1, 12, 0, 1), (1, 1, 2, 1), (1, 3, 2, 1), (1, 22, 0, 3), (1, 16, 2, 1), (2, 3, 0), (2, 5, 1), (1, 0, 1, 3), (1, 17, 0, 3),
    (1, 11, 1, 1), (1, 21, 0, 3), (1, 7, 0, 1), (0, 1, ()), (0, 2, ()), (2, 1, 0), (2, 6, 1), (1, 18, 0, 3), (1, 23, 2, 1),
    (1, 9, 2, 1), (2, 10, 0), (1, 8, 1, 1), (2, 2, 0), (1, 0, 2, 1), (2, 4, 1), (1, 14, 2, 1), (1, 15, 2, 1), (2, 0, 0),
    (1, 20, 2, 1), (1, 10, 2, 1), (2, 4, 0), (1, 25, 1, 1), (1, 19, 2, 1), (1, 16, 2, 2), (2, 3, 1), (1, 24, 2, 2),
    (1, 22, 1, 1), (2, 2, 1), (1, 7, 1, 1), (1, 12, 1, 1), (1, 17, 1, 1), (1, 21, 1, 1), (2, 23, 0), (2, 1, 1), (2, 26, 0),
    (2, 11, 0), (1, 18, 1, 1), (1, 11, 2, 1), (1, 23, 2, 2), (1, 13, 2, 2), (0, 4, (1, 2, 3, 4, 5, 6)), (1, 8, 2, 1),
    (0, 5, ()), (0, 6, ()), (2, 20, 0), (1, 10, 2, 2), (2, 7, 0), (1, 9, 2, 2), (2, 0, 1), (0, 7, ()), (2, 12, 0),
    (1, 12, 2, 1), (1, 19, 2, 2), (2, 8, 0), (1, 7, 2, 1), (1, 26, 2, 1), (2, 25, 0), (0, 3, (0,)), (1, 14, 2, 2), (2, 9, 0),
    (1, 22, 2, 1), (1, 18, 2, 1), (1, 17, 2, 1), (1, 20, 2, 2), (2, 14, 0), (2, 22, 0), (2, 17, 0), (0, 8, ()), (1, 13, 2, 3),
    (0, 9, ()), (0, 10, ()), (2, 21, 0), (0, 11, ()), (2, 8, 1), (1, 10, 2, 3), (1, 21, 2, 1), (0, 12, ()), (1, 9, 2, 3),
    (1, 25, 2, 1), (2, 18, 0), (0, 13, ()), (1, 14, 2, 3), (2, 11, 1), (2, 13, 1), (1, 15, 2, 2), (1, 20, 2, 3), (1, 19, 2, 3),
    (1, 24, 2, 3), (2, 7, 1), (0, 14, ()), (0, 15, ()), (0, 16, ()), (2, 12, 1), (2, 16, 0), (2, 9, 1), (1, 23, 2, 3),
    (2, 10, 1), (1, 16, 2, 3), (2, 14, 1), (2, 15, 0), (0, 17, (7, 11)), (2, 26, 1), (2, 20, 1), (1, 15, 2, 3), (2, 17, 1),
    (0, 18, (8, 12)), (0, 19, (9, 10, 13, 14)), (2, 24, 1), (2, 22, 1), (2, 19, 1), (2, 21, 1), (0, 20, ()), (2, 16, 1),
    (2, 23, 1), (2, 15, 1), (0, 21, ()), (2, 25, 1), (0, 22, ()), (2, 18, 1), (0, 23, (15, 16, 19, 20, 23, 24)),
    (0, 24, (17, 21, 25)), (0, 25, (18, 22, 26)),
]
REDUCE_UNITS = [
    (2, 2, 0, 96, 0, 128), (2, 3, 0, 96, 128, 128), (2, 2, 0, 96, 256, 128), (2, 3, 0, 96, 384, 128), (2, 0, 0, 96, 512, 128),
    (2, 1, 0, 96, 640, 128), (1, 0, 0, 48, 0, 128), (1, 1, 0, 48, 128, 128), (1, 2, 0, 48, 256, 128), (1, 3, 0, 48, 384, 128),
    (1, 0, 0, 48, 512, 256), (1, 1, 0, 48, 768, 256), (1, 0, 0, 48, 1024, 256), (1, 1, 0, 48, 1280, 256),
    (1, 0, 0, 48, 2688, 128), (1, 1, 0, 48, 2816, 256), (1, 0, 0, 48, 1536, 128), (1, 1, 0, 48, 1664, 256),
    (1, 0, 0, 48, 1920, 256), (1, 3, 0, 48, 2176, 128), (1, 0, 0, 48, 2304, 128), (1, 1, 0, 48, 2432, 128),
    (1, 2, 0, 48, 2560, 128), (3, 3, 0, 8, 0, 128),
]
REDUCE_GROUP = [
    0, 0, 0, 0, 0, 0, 1, 1, 1, 1, 1, 1, 1, 1, 2, 2, 3, 3, 3, 3, 3, 3, 3, 4,
]
REDUCE_PLAN = [
    (0, 26), (0, 27), (0, 31), (0, 32), (0, 28), (1, 0, 0), (1, 1, 0), (0, 29), (0, 33), (1, 3, 0), (0, 34), (0, 35), (1, 2, 0),
    (0, 36), (0, 30), (0, 37), (0, 38), (2, 1, 0), (1, 1, 1), (1, 4, 0), (2, 0, 0), (1, 5, 0), (0, 39), (1, 0, 1), (0, 40),
    (1, 8, 0), (1, 7, 0), (0, 41), (2, 3, 0), (0, 43), (2, 2, 0), (1, 10, 0), (0, 44), (1, 2, 1), (0, 48), (2, 5, 0), (2, 4, 0),
    (1, 4, 1), (0, 51), (1, 9, 0), (1, 5, 1), (1, 3, 1), (1, 14, 0), (2, 8, 0), (0, 42), (1, 11, 0), (1, 12, 0), (1, 8, 1),
    (0, 49), (2, 10, 0), (1, 10, 1), (1, 15, 0), (0, 50), (0, 45), (2, 4, 1), (0, 46), (1, 4, 2), (1, 13, 0), (0, 52),
    (2, 5, 1), (0, 53), (2, 7, 0), (0, 47), (2, 14, 0), (2, 11, 0), (2, 9, 0), (1, 11, 1), (1, 9, 1), (1, 7, 1), (0, 54),
    (2, 10, 1), (1, 10, 2), (1, 14, 1), (0, 55), (2, 12, 0), (1, 6, 0), (1, 5, 2), (1, 12, 1), (0, 56), (2, 15, 0), (2, 11, 1),
    (1, 23, 0), (1, 15, 1), (1, 11, 2), (0, 57), (0, 58), (1, 16, 0), (2, 7, 1), (1, 17, 0), (1, 7, 2), (2, 14, 1), (1, 14, 2),
    (0, 59), (1, 19, 0), (2, 15, 1), (1, 15, 2), (2, 6, 0), (1, 18, 0), (2, 23, 0), (2, 3, 1), (2, 13, 0), (0, 60), (1, 13, 1),
    (1, 22, 0), (1, 23, 1), (2, 16, 0), (2, 12, 1), (1, 12, 2), (1, 6, 1), (2, 5, 2), (2, 19, 0), (1, 19, 1), (0, 61),
    (1, 20, 0), (1, 16, 1), (1, 21, 0), (2, 22, 0), (1, 22, 1), (2, 1, 1), (2, 12, 2), (2, 18, 0), (1, 18, 1), (2, 17, 0),
    (2, 6, 1), (2, 8, 1), (2, 14, 2), (1, 6, 2), (1, 3, 2), (2, 16, 1), (1, 17, 1), (1, 16, 2), (2, 0, 1), (2, 21, 0),
    (2, 23, 1), (1, 23, 2), (2, 13, 1), (1, 13, 2), (1, 21, 1), (1, 0, 2), (2, 11, 2), (2, 22, 1), (2, 9, 1), (2, 20, 0),
    (2, 7, 2), (1, 20, 1), (2, 18, 1), (1, 18, 2), (2, 17, 1), (1, 17, 2), (2, 21, 1), (2, 3, 2), (2, 13, 2), (1, 9, 2),
    (1, 1, 2), (1, 22, 2), (1, 21, 2), (2, 6, 2), (2, 4, 2), (2, 20, 1), (2, 2, 1), (2, 16, 2), (2, 10, 2), (1, 2, 2),
    (1, 20, 2), (0, 62), (2, 19, 1), (1, 19, 2), (1, 8, 2), (2, 18, 2), (2, 2, 2), (0, 63), (2, 0, 2), (2, 22, 2), (2, 17, 2),
    (2, 8, 2), (2, 9, 2), (2, 23, 2), (2, 19, 2), (2, 21, 2), (2, 15, 2), (2, 1, 2), (2, 20, 2),
]


def whole_layer(*refs):
    (
        tokens_in, lengths, cot_in, in_w, out_w, up_w, down_w, b0, b1, b2, b3, b4, b5, b6,
        result, tokens_grad, in_g, out_g, up_g, down_g, small_g,
        WQ, WU, WD, stage_s, stage_r, SP, PV, UB, TS, SIG, QF, KF, VX, SES, SER, LER,
        MSK, CS, USE, LAST, RD, ATT, ATS, N1, S1, F1, NL, NLS, ACT, GP, AT, ATS2, DG, DGS, HGS,
        BG, BGS, PGS, OUT, RB0D, RB1D, RB0W, RB1W, FD, FW, SG, SGR, RB0S, RB1S, FS,
        VEC, HID, tokens, cot, send_sems, gather_sems, reduce_sems, core_sems, hbm, load_sems,
    ) = refs
    p = Place()
    c = p.c

    W5 = {IN_OUT: WQ.reshape(4, 2, 2, 48, FF), UP: WU.reshape(4, 2, 2, 48, FF)}
    WD6 = WD.reshape(4, 2, 2, 2, 96, WIDTH)
    AT4 = AT.reshape(16, 2, 96, ROWS)
    ATS3 = ATS2.reshape(16, 96, ROWS)
    DW = ACT.reshape(2048, WIDTH)

    def gather_view(u, blocks, core):
        arr, _, r0, nr, c0, nc = GATHER_UNITS[u]
        if arr == SMALL:
            return SP.at[blocks + (core,)]
        if arr == DOWN:
            return WD6.at[blocks + (core, pl.ds(r0, nr), pl.ds(c0, nc))]
        return W5[arr].at[blocks + (pl.ds(r0, nr), pl.ds(pl.multiple_of(core * HALF + c0, 128), nc))]

    sends = Sends(send_sems, SENDS)
    gather = Gather(p, GATHER_UNITS, gather_view, sends, gather_sems)
    reduce = Reduce(
        p, REDUCE_UNITS,
        {DOWN: DW.at[pl.ds(0, HALF)].reshape(4, 2, 2, 96, WIDTH), UP: W5[UP], SMALL: SG},
        {DOWN: (RB0D, RB1D), UP: (RB0W, RB1W), SMALL: (RB0S, RB1S)},
        {DOWN: FD, UP: FW, SMALL: FS},
        sends, reduce_sems,
    )
    copies, sent, leaving = [], {}, {}

    def to_core(name, src, dst, mine=None):
        sem = core_sems.at[len(sent)]
        sent[name] = (dst if mine is None else mine, sem)
        leaving[name] = sends.start(lambda send: remote(src, dst, send, sem, p.peer("core")))

    def got(name):
        dst, sem = sent[name]
        remote(dst, dst, sem, sem, p.peer("core")).wait_recv()

    def left(name):
        sends.left(leaving[name])

    def write(src, dst):
        copy = pltpu.make_async_copy(src, dst, hbm.at[len(copies)])
        copy.start()
        copies.append(copy)

    def at128(start, size):
        return pl.ds(pl.multiple_of(start, 128), size)

    def rows_loop(body, carry, rows=slice(0, ROWS), size=64):
        for n in range(rows.start, rows.stop, size):
            carry = body(slice(n, n + size), carry)
        return carry

    def mean(v):
        return jnp.sum(v, axis=1, keepdims=True) * (1.0 / WIDTH)

    def fold(v):
        return jnp.sum(v.reshape(-1, 8, v.shape[1]), axis=0)

    def low_lanes(rows):
        return lax.broadcasted_iota(jnp.int32, (rows, 128), 1) < HEAD

    zero = jnp.zeros((8, WIDTH), F32)
    halves, carried = (slice(0, ROWS // 2), slice(ROWS // 2, ROWS)), {}
    first_len, second_len = lengths[0, 0], lengths[0, 1]
    first = c * ROWS
    own_half = at128(c * HALF, HALF)
    out_b, n_gain, n_bias, down_b, f_gain, f_bias = (lambda i=i: PV[i : i + 1, :] for i in range(6))

    loads = [pltpu.make_async_copy(a, b, load_sems.at[i]) for i, (a, b) in enumerate(((tokens_in, tokens), (cot_in, cot)))]
    for copy in loads:
        copy.start()
    bar = pltpu.get_barrier_semaphore()
    for to in (p.peer("x"), p.peer("y"), p.peer("core"), p.peer("z", 1), p.peer("z", 2), p.peer("z", 3)):
        pl.semaphore_signal(bar, inc=1, device_id=to, device_id_type=MESH)
    stage_s[0:24, 0:2304] = in_w[...]
    stage_s[0:24, 2304:3072] = out_w[...]
    stage_s[0:24, 3072:6144] = up_w[...]
    WD6[p.z, p.y, p.x, c] = down_w[...]
    FS[...] = jnp.zeros((8, 128), F32)
    for i, ref in enumerate((b0, b1, b2, b3, b4, b5)):
        FS[i : i + 1, 0:24] = ref[...].astype(F32)
    FS[6:7, 0:96] = b6[...].astype(F32)
    SP[p.z, p.y, p.x, c] = FS[...]
    pl.semaphore_wait(bar, 6)
    to_core("stage", stage_s, stage_r)
    to_core("tokens", tokens_in, TS)

    def prep():
        got("stage")
        mine, other = stage_s[0:24, :].astype(F32), stage_r[0:24, :].astype(F32)
        top, bottom = jnp.where(c == 0, mine, other), jnp.where(c == 0, other, mine)
        share = jnp.concatenate([top, bottom], axis=0).astype(BF16)
        W5[IN_OUT][p.z, p.y, p.x, :, own_half] = jnp.where(c == 0, share[:, 0:HALF], share[:, HALF:FF])
        W5[UP][p.z, p.y, p.x, :, own_half] = jnp.where(c == 0, share[:, FF : FF + HALF], share[:, FF + HALF :])

    def docs(part):
        if part:
            return masks()
        pos = lax.broadcasted_iota(jnp.int32, (ROWS, 128), 0) + first
        doc = (pos >= first_len).astype(jnp.int32)
        span = jnp.where(doc == 0, first_len, second_len).astype(F32)
        angle = HALF_PI * (pos - doc * first_len).astype(F32) / span
        CS[...] = jnp.where(low_lanes(ROWS), jnp.cos(angle), jnp.sin(angle))
        prior_doc = jnp.where(first > 0, (first - 1 >= first_len).astype(jnp.int32), -1)
        last_doc = (first + (ROWS - 1) >= first_len).astype(jnp.int32)
        USE[...] = (doc == prior_doc).astype(F32)
        LAST[...] = (doc == last_doc).astype(BF16)

    def masks():
        row = lax.broadcasted_iota(jnp.int32, (ROWS, ROWS), 0)
        col = lax.broadcasted_iota(jnp.int32, (ROWS, ROWS), 1)
        row_doc = (row + first >= first_len).astype(jnp.int32)
        col_doc = (col + first >= first_len).astype(jnp.int32)
        MSK[...] = ((col <= row) & (row_doc == col_doc)).astype(BF16)

    def params():
        wide = jnp.zeros((8, 256), F32)
        for step, dst in ((24, PV), (96, UB)):
            n = 384 // step
            for g in range(32 // n):
                total = jnp.zeros((8, 384), F32)
                for k in range(n):
                    d = n * g + k
                    tile = SP[d // 8, (d // 4) % 2, (d // 2) % 2, d % 2]
                    total = total + pltpu.roll(jnp.concatenate([tile, wide], axis=1), step * k, 1)
                dst[:, 384 * g : 384 * (g + 1)] = total

    def project(j):
        if j == 0:
            loads[0].wait()
        rows = tokens[...]
        low = low_lanes(ROWS)
        for k, feat in ((0, QF), (1, KF)):
            raw = dot(rows, WQ[:, k * WIDTH + 256 * j : k * WIDTH + 256 * (j + 1)], 1, 0)
            for i in range(2):
                r = raw[:, 128 * i : 128 * (i + 1)]
                e = jnp.exp(-jnp.abs(r))
                active = jnp.maximum(r, 0.0) + jnp.log1p(e)
                slope = jnp.where(r >= 0, 1.0, e) / (1.0 + e)
                at = k * WIDTH + 256 * j + 128 * i
                SIG[:, at : at + 128] = slope.astype(BF16)
                turned = pltpu.roll(active, HEAD, 1)
                feat[4 * j + 2 * i] = (jnp.where(low, active, turned) * CS[...]).astype(BF16)
                feat[4 * j + 2 * i + 1] = (jnp.where(low, turned, active) * CS[...]).astype(BF16)
        value = dot(rows, WQ[:, 2 * WIDTH + 256 * j : 2 * WIDTH + 256 * (j + 1)], 1, 0)
        for i in range(2):
            v = value[:, 128 * i : 128 * (i + 1)]
            VX[4 * j + 2 * i] = jnp.where(low, v, 1.0).astype(BF16)
            VX[4 * j + 2 * i + 1] = jnp.where(low, 1.0, v).astype(BF16)

    def summary():
        def one(h, carry):
            SES[h] = dot(KF[h] * LAST[...], VX[h], 0, 0).astype(BF16)
            return carry

        lax.fori_loop(0, HEADS, one, 0)
        to_core("state", SES, SER)

    def attend(n):
        if n == 0:
            got("state")
        at = slice(128 * n, 128 * (n + 1))
        low = low_lanes(256)
        for half in range(2):
            width = 256 * (half + 1)
            rows = slice(256 * half, width)
            outs = []
            for h in (2 * n, 2 * n + 1):
                q = QF[h, rows, :]
                scores = dot(q, KF[h, 0:width, :], 1, 1).astype(BF16) * MSK[rows, 0:width]
                outs.append(dot(scores, VX[h, 0:width, :], 1, 0) + USE[rows, :] * dot(q, SER[h], 1, 0))
            numer = jnp.where(low, outs[0], outs[1])
            denom = jnp.where(low, pltpu.roll(outs[0], HEAD, 1), pltpu.roll(outs[1], HEAD, 1))
            inverse = 1.0 / denom
            RD[rows, at] = inverse
            ATT[rows, at] = (numer * inverse).astype(BF16)

    def out_project(part):
        if part:
            return norm_first(part - 1)
        to_core("attended", ATT, ATS)
        for j in range(3):
            cols = slice(256 * j, 256 * (j + 1))
            F1[:, cols] = (
                tokens[:, cols].astype(F32)
                + dot(ATT[...], WQ[:, 2304 + 256 * j : 2304 + 256 * (j + 1)], 1, 0)
                + out_b()[:, cols]
            )

    def norm_first(part):
        def norm(at, carry):
            x = F1[at, :]
            centered = x - mean(x)
            scale = lax.rsqrt(mean(centered * centered) + NORM_EPS)
            normal = centered * scale
            N1[at, :] = normal
            S1[at, :] = jnp.broadcast_to(scale, (normal.shape[0], 128))
            NL[at, :] = (normal * n_gain() + n_bias()).astype(BF16)
            return carry

        rows_loop(norm, 0, halves[part])
        if part:
            to_core("normed", NL, NLS)

    def up(j):
        cols = slice(512 * j, 512 * (j + 1))
        hidden = dot(NL[...], WU[:, cols], 1, 0) + UB[6:7, cols]
        phi = 0.5 + 0.5 * lax.erf(hidden * math.sqrt(0.5))
        active = (hidden * phi).astype(BF16)
        slope = phi + hidden * (jnp.exp(-0.5 * hidden * hidden) * (1.0 / math.sqrt(2 * math.pi)))
        GP[:, cols] = slope.astype(BF16)
        AT[cols, :] = active.T
        for piece in range(4):
            a, b = max(512 * j, 768 * piece), min(512 * (j + 1), 768 * (piece + 1))
            if a < b:
                ACT[piece, :, a - 768 * piece : b - 768 * piece] = active[:, a - 512 * j : b - 512 * j]
        if j == 5:
            to_core("activated", AT4.at[:, 1 - c], ATS3)

    def down(j):
        cols = slice(256 * j, 256 * (j + 1))
        total = down_b()[:, cols] + (N1[:, cols] * n_gain()[:, cols] + n_bias()[:, cols])
        for piece in range(4):
            total = total + dot(ACT[piece], WD[768 * piece : 768 * (piece + 1), cols], 1, 0)
        F1[:, cols] = total

    def norm_second(part):
        if part == 0:
            loads[1].wait()

        def norm(at, carry):
            gain_sum, bias_sum, down_sum = carry
            x = F1[at, :]
            centered = x - mean(x)
            scale = lax.rsqrt(mean(centered * centered) + NORM_EPS)
            normal = centered * scale
            OUT[at, :] = (normal * f_gain() + f_bias()).astype(BF16)
            ct = cot[at, :].astype(F32)
            e = ct * f_gain()
            grad = scale * (e - mean(e) - normal * mean(e * normal))
            F1[at, :] = grad
            low = grad.astype(BF16)
            DG[at, :] = low
            return gain_sum + fold(ct * normal), bias_sum + fold(ct), down_sum + fold(low.astype(F32))

        carried["second"] = rows_loop(norm, carried.get("second", (zero, zero, zero)), halves[part])
        to_core(("down", part), DG.at[halves[part]], DGS.at[halves[part]])
        if part:
            for i, s in zip((4, 5, 3), carried["second"]):
                VEC[i : i + 1, :] = jnp.sum(s, axis=0, keepdims=True)
            write(OUT, result)

    def down_weight(j):
        cols = slice(256 * j, 256 * (j + 1))
        if j == 0:
            got("activated")
        part = dot(AT4[:, c].reshape(HALF, ROWS), DG[:, cols], 1, 0)
        if j == 0:
            got(("down", 0))
            got(("down", 1))
        DW[0:HALF, cols] = (part + dot(ATS2[...], DGS[:, cols], 1, 0)).astype(BF16)

    def free_up():
        while gathered:
            sends.left(gathered.pop())

    def hidden_back(j):
        cols = slice(512 * j, 512 * (j + 1))
        grad = dot(DG[...], WD[cols, :], 1, 1) * GP[:, cols].astype(F32)
        low = grad.astype(BF16)
        GP[:, cols] = low
        HID[0:1, cols] = jnp.sum(low.astype(F32), axis=0, keepdims=True)
        if j == 5:
            to_core("hidden", GP.at[:, at128((1 - c) * HALF, HALF)], HGS)

    def normed_back(j):
        cols = slice(256 * j, 256 * (j + 1))
        F1[:, cols] = F1[:, cols] + dot(GP[...], WU[cols, :], 1, 1)

    def up_weight(j):
        if j == 0:
            free_up()
            got("normed")
            got("hidden")
        cols = slice(512 * j, 512 * (j + 1))
        part = dot(NL[...], GP[:, at128(c * HALF + 512 * j, 512)], 0, 0) + dot(NLS[...], HGS[:, cols], 0, 0)
        WU[:, cols] = part.astype(BF16)

    def norm_first_back(part):
        def norm(at, carry):
            gain_sum, bias_sum, out_sum = carry
            g, normal, scale = F1[at, :], N1[at, :], S1[at, 0:1]
            e = g * n_gain()
            grad = scale * (e - mean(e) - normal * mean(e * normal))
            F1[at, :] = grad
            low = grad.astype(BF16)
            BG[at, :] = low
            return gain_sum + fold(g * normal), bias_sum + fold(g), out_sum + fold(low.astype(F32))

        carried["first"] = rows_loop(norm, carried.get("first", (zero, zero, zero)), halves[part])
        if part:
            to_core("branch", BG.at[:, at128((1 - c) * 384, 384)], BGS)
            for i, s in zip((1, 2, 0), carried["first"]):
                VEC[i : i + 1, :] = jnp.sum(s, axis=0, keepdims=True)

    def small_tiles(half):
        line = lax.broadcasted_iota(jnp.int32, (8, 128), 0)
        lane = lax.broadcasted_iota(jnp.int32, (8, 128), 1)
        for d in range(16 * half, 16 * (half + 1)):
            g, k = divmod(d, 16)
            part = VEC[:, 384 * g : 384 * (g + 1)]
            a = (pltpu.roll(part, 384 - 24 * k, 1) if k else part)[:, 0:128]
            g, k = divmod(d, 4)
            part = jnp.broadcast_to(HID[0:1, 384 * g : 384 * (g + 1)], (8, 384))
            b = (pltpu.roll(part, 384 - 96 * k, 1) if k else part)[:, 0:128]
            tile = jnp.where((line < 6) & (lane < 24), a, jnp.where((line == 6) & (lane < 96), b, 0.0))
            SGR[0, d % 2, d // 8, (d // 4) % 2, (d // 2) % 2] = tile
        if half:
            to_core("small", SGR.at[0, 1 - c], SGR.at[1, 0])

    def small_sum():
        got("small")
        SG[...] = SGR[0, c] + SGR[1, 0]

    def slot(h):
        if isinstance(h, int):
            return slice(512 * (h // 4), 512 * (h // 4 + 1)), slice(128 * (h % 4), 128 * (h % 4 + 1))
        return at128(512 * lax.div(h, 4), 512), at128(128 * lax.rem(h, 4), 128)

    def numer_back(j):
        if j == 0:
            left("activated")
            left("state")
        low = low_lanes(ROWS)
        lane = lax.broadcasted_iota(jnp.int32, (ROWS, 128), 1)
        across = low_lanes(128) != (lax.broadcasted_iota(jnp.int32, (128, 128), 0) < HEAD)
        across = across.astype(F32).astype(BF16)
        grads = dot(BG[...], WQ[256 * j : 256 * (j + 1), 2304:FF], 1, 1)
        for i in range(2):
            at = slice(256 * j + 128 * i, 256 * j + 128 * (i + 1))
            ng = grads[:, 128 * i : 128 * (i + 1)] * RD[:, at]
            scaled = ng * ATT[:, at].astype(F32)
            high = scaled.astype(BF16)
            rest = (scaled - high.astype(F32)).astype(BF16)
            dgrad = -(dot(high, across, 1, 0) + dot(rest, across, 1, 0))
            hi = dgrad.astype(BF16).astype(F32)
            beside = jnp.where(
                (lane == 0) | (lane == HEAD), hi, jnp.where((lane == 1) | (lane == HEAD + 1), dgrad - hi, 0.0)
            )
            for par in range(2):
                h = 4 * j + 2 * i + par
                ngx = jnp.where(low, ng, beside) if par == 0 else jnp.where(low, beside, ng)
                AT[slot(h)] = ngx.astype(BF16)
                SES[h] = dot(QF[h], (ngx * USE[...]).astype(BF16), 0, 0).astype(BF16)
        if j == 2:
            to_core("leave", SES, LER)

    def out_weight():
        free_up()
        got("attended")
        part = dot(ATT[...], BG[:, at128(c * 384, 384)], 0, 0)
        got("branch")
        WU[:, 2688:FF] = (part + dot(ATS[...], BGS[...], 0, 0)).astype(BF16)

    def attend_back(j):
        if j == 0:
            left("hidden")
            got("leave")
        n = 3 * (1 - c if j < 3 else c) + j % 3
        low = low_lanes(ROWS)
        lead = c == 0
        last = LAST[...].astype(F32) * jnp.where(lead, 1.0, 0.0).astype(F32)
        m0, m1 = MSK[0:256, 0:256], MSK[256:ROWS, :]
        top, bottom = slice(0, 256), slice(256, ROWS)
        pieces = [], [], []
        for h in (2 * n, 2 * n + 1):
            ngx, qf, kf, vx = AT[slot(h)], QF[h], KF[h], VX[h]
            d0 = dot(ngx[top], vx[top], 1, 1).astype(BF16) * m0
            d1 = dot(ngx[bottom], vx, 1, 1).astype(BF16) * m1
            s0 = dot(qf[top], kf[top], 1, 1).astype(BF16) * m0
            s1 = dot(qf[bottom], kf, 1, 1).astype(BF16) * m1
            q_grad = jnp.concatenate([dot(d0, kf[top], 1, 0), dot(d1, kf, 1, 0)], axis=0)
            k_top = dot(d0, qf[top], 0, 0) + dot(d1[:, top], qf[bottom], 0, 0)
            k_grad = jnp.concatenate([k_top, dot(d1[:, bottom], qf[bottom], 0, 0)], axis=0)
            v_top = dot(s0, ngx[top], 0, 0) + dot(s1[:, top], ngx[bottom], 0, 0)
            v_grad = jnp.concatenate([v_top, dot(s1[:, bottom], ngx[bottom], 0, 0)], axis=0)
            past = dot(jnp.where(lead, vx, ngx), jnp.where(lead, LER[h], SER[h]), 1, 1)
            q_grad = (q_grad + USE[...] * past) * CS[...]
            k_grad = (k_grad + last * past) * CS[...]
            pieces[0].append(q_grad + pltpu.roll(q_grad, HEAD, 1))
            pieces[1].append(k_grad + pltpu.roll(k_grad, HEAD, 1))
            pieces[2].append(v_grad + last * dot(kf, LER[h], 1, 0))
        for k, (even, odd) in enumerate(pieces):
            both = jnp.where(low, even, odd)
            at = at128(k * WIDTH + 128 * n, 128)
            if k < 2:
                both = both * SIG[:, at].astype(F32)
            GP[:, at] = both.astype(BF16)
        if j == 2:
            for k in range(3):
                src = GP.at[:, at128(k * WIDTH + (1 - c) * 384, 384)]
                to_core(("projected", k), src, PGS.at[:, pl.ds(384 * k, 384)])

    def in_weight(j):
        cols = slice(384 * j, 384 * (j + 1))
        if j == 0:
            got("tokens")
        part = dot(tokens[...], GP[:, at128(j * WIDTH + c * 384, 384)], 0, 0)
        got(("projected", j))
        WU[:, HALF + 384 * j : HALF + 384 * (j + 1)] = (part + dot(TS[...], PGS[:, cols], 0, 0)).astype(BF16)

    def tokens_back(j):
        cols = slice(256 * j, 256 * (j + 1))
        F1[:, cols] = F1[:, cols] + dot(GP[:, 0:2304], WQ[cols, 0:2304], 1, 1)
        if j == 2:
            write(F1, tokens_grad)

    steps = []
    for step, count in (
        (prep, 0), (docs, 2), (params, 0), (project, 3), (summary, 0), (attend, 6), (out_project, 3), (up, 6), (down, 3),
        (norm_second, 2), (down_weight, 3), (hidden_back, 6), (normed_back, 3), (up_weight, 3), (norm_first_back, 2),
        (small_tiles, 2), (small_sum, 0), (numer_back, 3), (out_weight, 0), (attend_back, 6),
        (in_weight, 3), (tokens_back, 3),
    ):
        steps += [partial(step, j) for j in range(count)] if count else [step]

    for kind, *op in GATHER_PLAN:
        if kind == STEP:
            for u in op[1]:
                gather.ready(u)
            steps[op[0]]()
        elif kind == ISSUE:
            gather.issue(*op)
        else:
            gather.share(*op)

    gathered = sends.now_open()

    outputs = {1: [(up_g, 0, 0, HALF)], 2: [(out_g, 2688, 0, 384)]}
    outputs[3] = [(in_g, HALF + 384 * k, WIDTH * k, 384) for k in range(3)]
    mine, other = pl.ds(pl.multiple_of(24 * c, 8), 24), pl.ds(pl.multiple_of(24 * (1 - c), 8), 24)
    open_units = list(REDUCE_GROUP)

    def done(u):
        group = REDUCE_GROUP[u]
        open_units.remove(group)
        if group in open_units:
            return
        if group == 0:
            write(FD, down_g)
        elif group == 4:
            small_g[...] = FS[...]
        else:
            for i, (ref, at, to, width) in enumerate(outputs[group]):
                here, there = (ref.at[:, at128(to + core * width, width)] for core in (c, 1 - c))
                to_core((group, i), FW.at[other, pl.ds(at, width)], here, there)
                write(FW.at[mine, pl.ds(at, width)], here)

    for kind, *op in REDUCE_PLAN:
        if kind == STEP:
            steps[op[0]]()
        elif kind == ISSUE:
            reduce.send(*op)
        else:
            reduce.add(*op)
            if op[1] == 2:
                done(op[0])

    for group in outputs:
        for i in range(len(outputs[group])):
            got((group, i))
    sends.finish()
    for copy in copies:
        copy.wait()


def hand_out(*refs):
    made, small, outs, vectors = refs[0:6], refs[6], refs[7:13], refs[13:20]
    held, lines, sems = refs[20:26], refs[26:33], refs[33]
    pieces = []
    for a, b, c in zip(made, held, outs):
        rows = a.shape[0]
        step = 128 if rows == ROWS else rows
        for r in range(0, rows, step):
            pieces.append(tuple(ref.at[pl.ds(r, step)] for ref in (a, b, c)))
    ins = [pltpu.make_async_copy(a, b, sems.at[0, i]) for i, (a, b, _) in enumerate(pieces)]
    back = [pltpu.make_async_copy(b, c, sems.at[1, i]) for i, (_, b, c) in enumerate(pieces)]
    for copy in ins:
        copy.start()
    for i, line in enumerate(lines):
        line[...] = small[i : i + 1, 0 : line.shape[1]]
        back.append(pltpu.make_async_copy(line, vectors[i], sems.at[1, len(pieces) + i]))
        back[-1].start()
    for copy, then in zip(ins, back):
        copy.wait()
        then.start()
    for copy in back:
        copy.wait()


def layer_2x2x4(tokens, lengths, in_weight, out_weight, out_bias, norm_gain, norm_bias, up_weight, up_bias,
                down_weight, down_bias, final_gain, final_bias, cotangent):
    vmem, anywhere = pl.BlockSpec(memory_space=pltpu.VMEM), pl.BlockSpec(memory_space=pl.ANY)

    def v(*shape, dtype=BF16):
        return pltpu.VMEM(shape, dtype)

    dma = pltpu.SemaphoreType.DMA
    scratch = [
        v(WIDTH, FF), v(WIDTH, FF), v(FF, WIDTH),
        v(32, 6144), v(32, 6144), v(4, 2, 2, 2, 8, 128, dtype=F32),
        v(8, WIDTH, dtype=F32), v(8, FF, dtype=F32),
        v(ROWS, WIDTH), v(ROWS, HALF),
        v(HEADS, ROWS, 128), v(HEADS, ROWS, 128), v(HEADS, ROWS, 128),
        v(HEADS, 128, 128), v(HEADS, 128, 128), v(HEADS, 128, 128),
        v(ROWS, ROWS), v(ROWS, 128, dtype=F32), v(ROWS, 128, dtype=F32), v(ROWS, 128),
        v(ROWS, WIDTH, dtype=F32), v(ROWS, WIDTH), v(ROWS, WIDTH),
        v(ROWS, WIDTH, dtype=F32), v(ROWS, 128, dtype=F32), v(ROWS, WIDTH, dtype=F32),
        v(ROWS, WIDTH), v(ROWS, WIDTH), v(4, ROWS, WIDTH), v(ROWS, FF),
        v(FF, ROWS), v(HALF, ROWS), v(ROWS, WIDTH), v(ROWS, WIDTH), v(ROWS, HALF),
        v(ROWS, WIDTH), v(ROWS, 384), v(ROWS, 1152), v(ROWS, WIDTH),
        v(4, 2, 96, WIDTH), v(7, 96, WIDTH),
        v(4, 2, 48, FF), v(7, 48, FF),
        v(96, WIDTH, dtype=F32), v(48, FF, dtype=F32),
        v(4, 2, 2, 8, 128, dtype=F32), v(2, 2, 4, 2, 2, 8, 128, dtype=F32),
        v(4, 2, 8, 128, dtype=F32), v(7, 8, 128, dtype=F32), v(8, 128, dtype=F32),
        v(8, WIDTH, dtype=F32), v(8, FF, dtype=F32),
        v(ROWS, WIDTH), v(ROWS, WIDTH),
        dma((SENDS,)), dma((6 * len(GATHER_UNITS),)), dma((3 * len(REDUCE_UNITS),)), dma((20,)), dma((10,)), dma((2,)),
    ]
    shapes = (
        jax.ShapeDtypeStruct((ROWS, WIDTH), BF16),
        jax.ShapeDtypeStruct((ROWS, WIDTH), F32),
        jax.ShapeDtypeStruct((24, 2304), F32),
        jax.ShapeDtypeStruct((24, WIDTH), F32),
        jax.ShapeDtypeStruct((24, FF), F32),
        jax.ShapeDtypeStruct((96, WIDTH), F32),
    )
    lines = (jax.ShapeDtypeStruct((1, 24), F32),) * 6 + (jax.ShapeDtypeStruct((1, 96), F32),)
    vectors = (out_bias, norm_gain, norm_bias, down_bias, final_gain, final_bias, up_bias)
    made = pl.pallas_call(
        whole_layer,
        out_shape=shapes + (jax.ShapeDtypeStruct((8, 128), F32),),
        in_specs=[anywhere, pl.BlockSpec(memory_space=pltpu.SMEM), anywhere] + [vmem] * 11,
        out_specs=(anywhere,) * 6 + (vmem,),
        scratch_shapes=scratch,
        compiler_params=pltpu.CompilerParams(
            collective_id=0, has_side_effects=True, vmem_limit_bytes=VMEM_LIMIT
        ),
    )(tokens, lengths, cotangent, in_weight, out_weight, up_weight, down_weight, *(b.reshape(1, -1) for b in vectors))
    result, tokens_grad, in_g, out_g, up_g, down_g, *small = pl.pallas_call(
        hand_out,
        out_shape=shapes + lines,
        in_specs=[anywhere] * 6 + [vmem],
        out_specs=(anywhere,) * 13,
        scratch_shapes=[pltpu.VMEM(s.shape, s.dtype) for s in shapes + lines] + [dma((2, 19))],
        compiler_params=pltpu.CompilerParams(vmem_limit_bytes=VMEM_LIMIT),
    )(*made)
    out_bias_g, norm_gain_g, norm_bias_g, down_bias_g, final_gain_g, final_bias_g, up_bias_g = (
        g.reshape(-1) for g in small
    )
    return (result, tokens_grad, in_g, out_g, out_bias_g, norm_gain_g, norm_bias_g, up_g,
            up_bias_g, down_g, down_bias_g, final_gain_g, final_bias_g)


VMEM_LIMIT = 64 * 2**20 - 2**18


def solution(mesh):
    both = ("dp", "fsdp")
    rows, vector = P(both, None), P(both)
    in_specs = (rows, P("dp", None), rows, rows, vector, vector, vector, rows, vector, rows, vector, vector, vector, rows)
    out_specs = (rows, rows, rows, rows, vector, vector, vector, rows, vector, rows, vector, vector, vector)
    body = layer_2x2x4 if dict(mesh.shape) == {"dp": 16, "fsdp": 2} else per_device
    return jax.shard_map(body, mesh=mesh, in_specs=in_specs, out_specs=out_specs, check_vma=False)
```

```python
from functools import partial
import math

import jax
import jax.numpy as jnp
from jax import lax
from jax.experimental import pallas as pl
from jax.experimental.pallas import tpu as pltpu
from jax.sharding import PartitionSpec as P

HEADS = 12
HEAD = 64
BLOCK = 512


HALF_PI = math.pi / 2
NORM_EPS = 1e-05

def prefix(shard, axis, combine, identity, reverse):
    devices, position = (lax.axis_size(axis), lax.axis_index(axis))
    everything = jax.tree.map(lambda part: lax.all_gather(part, axis), shard)
    start = jax.tree.map(
        lambda part, zero: jnp.broadcast_to(jnp.asarray(zero, part.dtype), part.shape),
        shard,
        identity,
    )

    def turn(k, before):
        at = devices - 1 - k if reverse else k
        reached = at > position if reverse else at < position
        new = combine(before, jax.tree.map(lambda part: part[at], everything))
        return jax.tree.map(lambda a, b: jnp.where(reached, a, b), new, before)

    return lax.fori_loop(0, devices, turn, start)


def documents(position, pair):
    first_len = pair[0]
    doc = (position >= first_len).astype(jnp.int32)
    start = doc * first_len
    span = jnp.where(doc == 0, first_len, pair[1])
    angle = HALF_PI * (position - start).astype(jnp.float32) / span.astype(jnp.float32)
    return (doc, angle)


def features(heads, angle):
    active = jax.nn.softplus(heads)
    return jnp.concatenate(
        [active * jnp.cos(angle)[None, :, None], active * jnp.sin(angle)[None, :, None]], axis=2
    )


def layer_norm(rows, gain, shift):
    mean = jnp.mean(rows, axis=-1, keepdims=True)
    centered = rows - mean
    scale = lax.rsqrt(jnp.mean(centered * centered, axis=-1, keepdims=True) + NORM_EPS)
    return centered * scale * gain + shift


def exact_gelu(values):
    return jax.nn.gelu(values, approximate=False)


def merge_state(earlier, later):
    return (
        later[0] + later[2] * earlier[0],
        later[1] + later[2] * earlier[1],
        later[2] * earlier[2],
    )


def block_forward(query, keys, values, doc_blk, state, norm, carry_doc):
    order = jnp.arange(doc_blk.shape[0], dtype=jnp.int32)
    mask = (order[None, :] <= order[:, None]) & (doc_blk[None, :] == doc_blk[:, None])
    raw = jnp.einsum("hif,hjf->hij", query, keys, preferred_element_type=jnp.float32)
    scores = jnp.where(mask[None], raw, 0.0)
    use = (doc_blk == carry_doc).astype(jnp.float32)
    carried = jnp.einsum(
        "hef,hif->hei", state.astype(jnp.bfloat16), query, preferred_element_type=jnp.float32
    )
    numer = (
        jnp.einsum(
            "hej,hij->hei", values, scores.astype(jnp.bfloat16), preferred_element_type=jnp.float32
        )
        + use * carried
    )
    denom = jnp.sum(scores, axis=2) + use * jnp.einsum(
        "hf,hif->hi", norm, query.astype(jnp.float32)
    )
    return (mask, scores, use, numer, denom)


def block_summary(keys, values, doc_blk):
    chosen = doc_blk == doc_blk[-1]
    picked = jnp.where(chosen[None, :, None], keys, jnp.zeros((), keys.dtype))
    state = jnp.einsum("hej,hjf->hef", values, picked, preferred_element_type=jnp.float32)
    norm = jnp.sum(picked.astype(jnp.float32), axis=1)
    return (chosen, picked, state, norm)


def per_device(
    tokens,
    lengths,
    in_weight,
    out_weight,
    out_bias,
    norm_gain,
    norm_bias,
    up_weight,
    up_bias,
    down_weight,
    down_bias,
    final_gain,
    final_bias,
    cotangent,
):
    rows = tokens.shape[0]
    width = tokens.shape[1]
    count = rows // BLOCK
    gathered = (
        lax.all_gather(in_weight, ("dp", "fsdp"), axis=0, tiled=True),
        lax.all_gather(out_weight, ("dp", "fsdp"), axis=0, tiled=True),
        lax.all_gather(out_bias, ("dp", "fsdp"), axis=0, tiled=True),
        lax.all_gather(norm_gain, ("dp", "fsdp"), axis=0, tiled=True),
        lax.all_gather(norm_bias, ("dp", "fsdp"), axis=0, tiled=True),
        lax.all_gather(up_weight, ("dp", "fsdp"), axis=0, tiled=True),
        lax.all_gather(up_bias, ("dp", "fsdp"), axis=0, tiled=True),
        lax.all_gather(down_weight, ("dp", "fsdp"), axis=0, tiled=True),
        lax.all_gather(down_bias, ("dp", "fsdp"), axis=0, tiled=True),
        lax.all_gather(final_gain, ("dp", "fsdp"), axis=0, tiled=True),
        lax.all_gather(final_bias, ("dp", "fsdp"), axis=0, tiled=True),
    )
    (
        inward,
        outward,
        out_shift,
        gain_first,
        shift_first,
        upward,
        up_shift,
        downward,
        down_shift,
        gain_second,
        shift_second,
    ) = gathered
    first = lax.axis_index("fsdp") * rows
    position = first + jnp.arange(rows, dtype=jnp.int32)
    pair = lengths[0]
    doc, angle = documents(position, pair)
    prior_doc = jnp.where(first > 0, (first - 1 >= pair[0]).astype(jnp.int32), -1)
    projected = jnp.dot(tokens, inward, preferred_element_type=jnp.float32)
    query_raw = projected[:, :width].reshape(rows, HEADS, HEAD).transpose(1, 0, 2)
    key_raw = projected[:, width : 2 * width].reshape(rows, HEADS, HEAD).transpose(1, 0, 2)
    query_feat, query_pull = jax.vjp(partial(features, angle=angle), query_raw)
    key_feat, key_pull = jax.vjp(partial(features, angle=angle), key_raw)
    query = query_feat.astype(jnp.bfloat16)
    keys = key_feat.astype(jnp.bfloat16)
    values = (
        projected[:, 2 * width :].reshape(rows, HEADS, HEAD).transpose(1, 2, 0).astype(jnp.bfloat16)
    )
    device_summary = block_summary(keys, values, doc)
    device_keep = (prior_doc == doc[-1]).astype(jnp.float32)
    identity = (
        jnp.zeros_like(device_summary[2]),
        jnp.zeros_like(device_summary[3]),
        jnp.ones((), jnp.float32),
    )
    state, norm, passed = prefix(
        (device_summary[2], device_summary[3], device_keep), "fsdp", merge_state, identity, False
    )
    keys_blk = keys
    values_blk = values
    doc_blk = doc
    carries = [(state, norm, prior_doc)]
    outcome = block_forward(query, keys_blk, values_blk, doc_blk, state, norm, prior_doc)
    ratios = outcome[3] / outcome[4][:, None, :]
    summary = block_summary(keys_blk, values_blk, doc_blk)
    attended = ratios.transpose(2, 0, 1).reshape(rows, width).astype(jnp.bfloat16)
    branch = jnp.dot(attended, outward, preferred_element_type=jnp.float32) + out_shift.astype(
        jnp.float32
    )
    first_sum = tokens.astype(jnp.float32) + branch
    normed, first_pull = jax.vjp(
        layer_norm, first_sum, gain_first.astype(jnp.float32), shift_first.astype(jnp.float32)
    )
    normed_low = normed.astype(jnp.bfloat16)
    hidden = jnp.dot(normed_low, upward, preferred_element_type=jnp.float32) + up_shift.astype(
        jnp.float32
    )
    activated, gelu_pull = jax.vjp(exact_gelu, hidden)
    activated_low = activated.astype(jnp.bfloat16)
    second_sum = (
        normed
        + jnp.dot(activated_low, downward, preferred_element_type=jnp.float32)
        + down_shift.astype(jnp.float32)
    )
    result, second_pull = jax.vjp(
        layer_norm, second_sum, gain_second.astype(jnp.float32), shift_second.astype(jnp.float32)
    )
    again = (
        lax.all_gather(in_weight, ("dp", "fsdp"), axis=0, tiled=True),
        lax.all_gather(out_weight, ("dp", "fsdp"), axis=0, tiled=True),
        lax.all_gather(out_bias, ("dp", "fsdp"), axis=0, tiled=True),
        lax.all_gather(norm_gain, ("dp", "fsdp"), axis=0, tiled=True),
        lax.all_gather(norm_bias, ("dp", "fsdp"), axis=0, tiled=True),
        lax.all_gather(up_weight, ("dp", "fsdp"), axis=0, tiled=True),
        lax.all_gather(up_bias, ("dp", "fsdp"), axis=0, tiled=True),
        lax.all_gather(down_weight, ("dp", "fsdp"), axis=0, tiled=True),
        lax.all_gather(down_bias, ("dp", "fsdp"), axis=0, tiled=True),
        lax.all_gather(final_gain, ("dp", "fsdp"), axis=0, tiled=True),
        lax.all_gather(final_bias, ("dp", "fsdp"), axis=0, tiled=True),
    )
    inward = again[0]
    outward = again[1]
    upward = again[5]
    downward = again[7]
    second_grad, final_gain_grad, final_shift_grad = second_pull(cotangent.astype(jnp.float32))
    down_grad = second_grad.astype(jnp.bfloat16)
    down_weight_grad = jnp.dot(activated_low.T, down_grad, preferred_element_type=jnp.float32)
    down_shift_grad = jnp.sum(down_grad.astype(jnp.float32), axis=0)
    (activated_grad,) = gelu_pull(
        jnp.dot(down_grad, downward.T, preferred_element_type=jnp.float32)
    )
    hidden_grad = activated_grad.astype(jnp.bfloat16)
    up_weight_grad = jnp.dot(normed_low.T, hidden_grad, preferred_element_type=jnp.float32)
    up_shift_grad = jnp.sum(hidden_grad.astype(jnp.float32), axis=0)
    normed_grad = second_grad + jnp.dot(hidden_grad, upward.T, preferred_element_type=jnp.float32)
    first_grad, norm_gain_grad, norm_shift_grad = first_pull(normed_grad)
    branch_grad = first_grad.astype(jnp.bfloat16)
    out_weight_grad = jnp.dot(attended.T, branch_grad, preferred_element_type=jnp.float32)
    out_shift_grad = jnp.sum(branch_grad.astype(jnp.float32), axis=0)
    attended_grad = jnp.dot(branch_grad, outward.T, preferred_element_type=jnp.float32)
    ratio_grad = attended_grad.reshape(rows, HEADS, HEAD).transpose(1, 2, 0)
    index = 0
    keys_blk = keys
    values_blk = values
    doc_blk = doc
    state_in, norm_in, doc_in = carries[index]
    mask, scores, use, numer, denom = block_forward(
        query, keys_blk, values_blk, doc_blk, state_in, norm_in, doc_in
    )
    numer_grad = (ratio_grad / denom[:, None, :]).astype(jnp.bfloat16)
    denom_grad = -jnp.sum(ratio_grad * numer, axis=1) / (denom * denom)
    scores_grad = (
        jnp.einsum("hei,hej->hij", numer_grad, values_blk, preferred_element_type=jnp.float32)
        + denom_grad[:, :, None]
    )
    scores_grad = jnp.where(mask[None], scores_grad, 0.0).astype(jnp.bfloat16)
    used_numer = jnp.where(use[None, None, :] > 0, numer_grad, jnp.zeros((), jnp.bfloat16))
    used_denom = use * denom_grad
    query_part = jnp.einsum(
        "hij,hjf->hif", scores_grad, keys_blk, preferred_element_type=jnp.float32
    )
    query_part = query_part + jnp.einsum(
        "hei,hef->hif",
        used_numer,
        state_in.astype(jnp.bfloat16),
        preferred_element_type=jnp.float32,
    )
    query_grads = query_part + used_denom[:, :, None] * norm_in[:, None, :]
    key_grads = [jnp.einsum("hij,hif->hjf", scores_grad, query, preferred_element_type=jnp.float32)]
    value_grads = [
        jnp.einsum(
            "hei,hij->hej",
            numer_grad,
            scores.astype(jnp.bfloat16),
            preferred_element_type=jnp.float32,
        )
    ]
    contribs = [
        (
            jnp.einsum("hei,hif->hef", used_numer, query, preferred_element_type=jnp.float32),
            jnp.einsum("hi,hif->hf", used_denom, query.astype(jnp.float32)),
        )
    ]
    keeps = [(doc_in == doc_blk[-1]).astype(jnp.float32)]
    local_state = jnp.zeros_like(device_summary[2])
    local_norm = jnp.zeros_like(device_summary[3])
    for index in reversed(range(count)):
        local_state = contribs[index][0] + keeps[index] * local_state
        local_norm = contribs[index][1] + keeps[index] * local_norm
    leave_state, leave_norm, through = prefix(
        (local_state, local_norm, device_keep), "fsdp", merge_state, identity, True
    )
    for index in reversed(range(count)):
        keys_blk = keys
        values_blk = values
        doc_blk = doc
        summary = block_summary(keys_blk, values_blk, doc_blk)
        state_low = leave_state.astype(jnp.bfloat16)
        key_extra = (
            jnp.einsum("hej,hef->hjf", values_blk, state_low, preferred_element_type=jnp.float32)
            + leave_norm[:, None, :]
        )
        key_grads[index] = key_grads[index] + jnp.where(summary[0][None, :, None], key_extra, 0.0)
        value_grads[index] = value_grads[index] + jnp.einsum(
            "hef,hjf->hej", state_low, summary[1], preferred_element_type=jnp.float32
        )
        leave_state = contribs[index][0] + keeps[index] * leave_state
        leave_norm = contribs[index][1] + keeps[index] * leave_norm
    (query_raw_grad,) = query_pull(query_grads)
    (key_raw_grad,) = key_pull(key_grads[0])
    value_grad = value_grads[0].transpose(2, 0, 1).reshape(rows, width)
    projected_grad = jnp.concatenate(
        [
            query_raw_grad.transpose(1, 0, 2).reshape(rows, width),
            key_raw_grad.transpose(1, 0, 2).reshape(rows, width),
            value_grad,
        ],
        axis=1,
    ).astype(jnp.bfloat16)
    in_weight_grad = jnp.dot(tokens.T, projected_grad, preferred_element_type=jnp.float32)
    tokens_grad = first_grad + jnp.dot(projected_grad, inward.T, preferred_element_type=jnp.float32)
    summed = (
        lax.psum_scatter(in_weight_grad, ("dp", "fsdp"), scatter_dimension=0, tiled=True),
        lax.psum_scatter(out_weight_grad, ("dp", "fsdp"), scatter_dimension=0, tiled=True),
        lax.psum_scatter(out_shift_grad, ("dp", "fsdp"), scatter_dimension=0, tiled=True),
        lax.psum_scatter(norm_gain_grad, ("dp", "fsdp"), scatter_dimension=0, tiled=True),
        lax.psum_scatter(norm_shift_grad, ("dp", "fsdp"), scatter_dimension=0, tiled=True),
        lax.psum_scatter(up_weight_grad, ("dp", "fsdp"), scatter_dimension=0, tiled=True),
        lax.psum_scatter(up_shift_grad, ("dp", "fsdp"), scatter_dimension=0, tiled=True),
        lax.psum_scatter(down_weight_grad, ("dp", "fsdp"), scatter_dimension=0, tiled=True),
        lax.psum_scatter(down_shift_grad, ("dp", "fsdp"), scatter_dimension=0, tiled=True),
        lax.psum_scatter(final_gain_grad, ("dp", "fsdp"), scatter_dimension=0, tiled=True),
        lax.psum_scatter(final_shift_grad, ("dp", "fsdp"), scatter_dimension=0, tiled=True),
    )
    return (result.astype(jnp.bfloat16), tokens_grad) + tuple(summed)


MESH = pl.DeviceIdType.MESH
F32 = jnp.float32
BF16 = jnp.bfloat16
ROWS = 512
WIDTH = 768
FF = 3072
HALF = 1536
GATHER_ORDER = ("zyx", "zxy", "xzy", "yzx", "xyz", "yxz", "zyx", "zxy")
DIRECT = (6, 7)
REDUCE_ORDER = ("xyz", "yxz", "yzx", "xzy")


def dot(a, b, ca, cb):
    return lax.dot_general(a, b, (((ca,), (cb,)), ((), ())), preferred_element_type=F32)


class Place:
    def __init__(self):
        self.dp = lax.axis_index("dp")
        self.c = lax.axis_index("fsdp")
        self.x = lax.rem(self.dp, 2)
        self.y = lax.rem(lax.div(self.dp, 2), 2)
        self.z = lax.div(self.dp, 4)

    def peer(self, d, k=1):
        if d == "x":
            return (self.dp + 1 - 2 * self.x, self.c)
        if d == "y":
            return (self.dp + 2 - 4 * self.y, self.c)
        if d == "z":
            return (lax.rem(self.dp + 4 * k, 16), self.c)
        if d == "up":
            return (self.dp + 4, self.c)
        if d == "down":
            return (self.dp - 4, self.c)
        return (self.dp, 1 - self.c)

    def at(self, known, flip=None, z=None):
        out = []
        for d in "zyx":
            if d in known:
                out.append(slice(None))
                continue
            v = getattr(self, d)
            if flip == d:
                v = 1 - v
            if d == "z" and z is not None:
                v = z
            out.append(v)
        return tuple(out)


def remote(src, dst, send, recv, to):
    return pltpu.make_async_remote_copy(
        src_ref=src, dst_ref=dst, send_sem=send, recv_sem=recv, device_id=to, device_id_type=MESH
    )


def guarded(cond, action):
    if cond is None:
        action()
    else:
        pl.when(cond)(action)


class Sends:
    def __init__(self, sems, size):
        self.sems, self.size, self.count, self.open = sems, size, 0, {}

    def start(self, make, cond=None):
        i = self.count % self.size
        self.count += 1
        self.wait(i)
        guarded(cond, lambda: make(self.sems.at[i]).start())
        self.open[i] = (cond, make)
        return i, make

    def wait(self, i):
        if i in self.open:
            cond, make = self.open.pop(i)
            guarded(cond, lambda: make(self.sems.at[i]).wait_send())

    def left(self, handle):
        if self.open.get(handle[0], (None, None))[1] is handle[1]:
            self.wait(handle[0])

    def now_open(self):
        return [(i, make) for i, (_, make) in self.open.items()]

    def finish(self):
        for i in list(self.open):
            self.wait(i)


class Gather:
    def __init__(self, place, units, view, sends, sems):
        self.p, self.units, self.view, self.sends, self.sems = place, units, view, sends, sems
        self.waited = set()

    def order(self, u):
        return GATHER_ORDER[self.units[u][1]]

    def copy(self, u, slot, blocks, to):
        src = self.view(u, blocks, self.p.c)
        return lambda sem: remote(src, src, sem, self.sems.at[6 * u + slot], to)

    def issue(self, u, ph, hop):
        p, o = self.p, self.order(u)
        known, d = o[:ph], o[ph]
        if hop == 1 and ph > 0:
            self.arrive(u, ph - 1)
        if d != "z":
            self.sends.start(self.copy(u, "xy".index(d), p.at(known), p.peer(d)))
            return
        if self.units[u][1] in DIRECT:
            for k in (1, 2, 3):
                self.sends.start(self.copy(u, 2, p.at(known), p.peer("z", k)))
            return
        if hop > 1:
            self.arrive_hop(u, ph, hop - 1)
        up = (jnp.logical_and(p.z < 3, p.z - (hop - 1) >= 0), p.z - (hop - 1), p.peer("up"))
        down = (jnp.logical_and(p.z > 0, p.z + (hop - 1) <= 3), p.z + (hop - 1), p.peer("down"))
        for cond, z, to in (up, down):
            self.sends.start(self.copy(u, 1 + hop, p.at(known, z=z), to), cond)

    def expect(self, u, slot, blocks, core):
        dst = self.view(u, blocks, core)
        remote(dst, dst, self.sems.at[6 * u + slot], self.sems.at[6 * u + slot], self.p.peer("core")).wait_recv()

    def arrive_hop(self, u, ph, hop):
        if (u, ph, hop) in self.waited:
            return
        self.waited.add((u, ph, hop))
        p, known = self.p, self.order(u)[:ph]
        above, below = p.z + hop <= 3, p.z - hop >= 0
        one = jnp.logical_xor(above, below)
        guarded(one, lambda: self.expect(u, 1 + hop, p.at(known), p.c))
        if hop == 1:
            two = jnp.logical_and(above, below)
            guarded(two, lambda: self.expect(u, 1 + hop, (pl.ds(0, 2),) + p.at(known)[1:], p.c))

    def arrive(self, u, ph):
        p, o = self.p, self.order(u)
        known, d = o[:ph], o[ph]
        if d == "z" and self.units[u][1] not in DIRECT:
            for hop in (1, 2, 3):
                self.arrive_hop(u, ph, hop)
        elif (u, ph, 0) not in self.waited:
            self.waited.add((u, ph, 0))
            if d == "z":
                self.expect(u, 2, (pl.ds(0, 3),) + p.at(known)[1:], p.c)
            else:
                self.expect(u, "xy".index(d), p.at(known, flip=d), p.c)

    def shared(self, u, part):
        o = self.order(u)
        if o[2] == "z":
            return self.p.at(o) if part else None
        return self.p.at(o[:2], flip=o[2] if part else None)

    def share(self, u, part):
        if self.shared(u, part):
            self.arrive(u, 1 + part)
            self.sends.start(self.copy(u, 5, self.shared(u, part), self.p.peer("core")))

    def ready(self, u):
        if (u, 0) not in self.waited:
            self.waited.add((u, 0))
            self.expect(u, 5, self.p.at("zyx"), 1 - self.p.c)


class Reduce:
    def __init__(self, place, units, blocks, landing, final, sends, sems):
        self.p, self.units = place, units
        self.blocks, self.landing, self.final = blocks, landing, final
        self.sends, self.sems = sends, sems

    def plan(self, u, ph):
        arr, kind, r0, nr, c0, nc = self.units[u]
        o = REDUCE_ORDER[kind]
        return arr, o[ph], o[ph + 1 :], (pl.ds(r0, nr), pl.ds(c0, nc))

    def moves(self, u, ph):
        p = self.p
        arr, d, left, cut = self.plan(u, ph)
        land = self.landing[arr][min(ph, 1)]
        if d != "z":
            lead = {0: (slice(None), slice(None)), 1: (pl.ds(0, 4),), 2: (6,)}[ph]
            return [(self.sems.at[3 * u + "xy".index(d)], p.at(left, flip=d), p.peer(d), land.at[lead + cut])]
        out = []
        for k in (1, 2, 3):
            lead = (pl.ds(2 * (k - 1), 2),) if ph == 1 else (3 + k,)
            blocks = p.at(left, z=lax.rem(p.z + k, 4))
            out.append((self.sems.at[3 * u + 2], blocks, p.peer("z", k), land.at[lead + cut]))
        return out

    def send(self, u, ph):
        arr, _, _, cut = self.plan(u, ph)
        for sem, sel, to, dst in self.moves(u, ph):
            src = self.blocks[arr].at[sel + cut]
            self.sends.start(lambda send, src=src, dst=dst, sem=sem, to=to: remote(src, dst, send, sem, to))

    def add(self, u, ph):
        p = self.p
        arr, d, left, cut = self.plan(u, ph)
        sem, _, to, dst = self.moves(u, ph)[0]
        if d == "z":
            dst = self.landing[arr][1].at[(pl.ds(0, 6) if ph == 1 else pl.ds(4, 3),) + cut]
        remote(dst, dst, sem, sem, to).wait_recv()
        ref, land = self.blocks[arr], self.landing[arr][min(ph, 1)]
        if ph == 2:
            total = ref[p.at("") + cut].astype(F32)
            for k in (4, 5, 6) if d == "z" else (6,):
                total = total + land[(k,) + cut].astype(F32)
            self.final[arr][cut] = total
            return
        for n in range({0: 8, 1: 4 if d != "z" else 2}[ph]):
            idx = {"z": p.z, "y": p.y, "x": p.x}
            if ph == 0:
                lead, other = divmod(n, 2), left.replace("z", "")
                idx["z"], idx[other] = lead
                leads = [lead]
            else:
                idx[left] = n
                leads = [(n,)] if d != "z" else [(2 * k + n,) for k in range(3)]
            sel = (idx["z"], idx["y"], idx["x"]) + cut
            if len(leads) == 1:
                ref[sel] = ref[sel] + land[leads[0] + cut]
                continue
            total = ref[sel].astype(F32)
            for lead in leads:
                total = total + land[lead + cut].astype(F32)
            ref[sel] = total.astype(ref.dtype)


IN_OUT, UP, DOWN, SMALL = range(4)
STEP, ISSUE, SHARE = range(3)
SENDS = 56

GATHER_UNITS = [
    (3, 2, 0, 8, 0, 128), (0, 0, 0, 48, 0, 256), (0, 1, 0, 48, 256, 256), (0, 2, 0, 48, 512, 256), (0, 3, 0, 48, 768, 256),
    (0, 6, 0, 48, 1024, 256), (0, 7, 0, 48, 1280, 256), (1, 6, 0, 48, 0, 256), (1, 7, 0, 48, 512, 256),
    (1, 4, 0, 48, 1024, 128), (1, 5, 0, 48, 1280, 128), (1, 6, 0, 48, 256, 256), (1, 7, 0, 48, 768, 256),
    (1, 4, 0, 48, 1152, 128), (1, 5, 0, 48, 1408, 128), (2, 4, 0, 32, 0, 128), (2, 5, 0, 32, 128, 128), (2, 0, 0, 32, 256, 256),
    (2, 1, 0, 32, 512, 256), (2, 4, 32, 32, 0, 128), (2, 5, 32, 32, 128, 128), (2, 0, 32, 32, 256, 256),
    (2, 1, 32, 32, 512, 256), (2, 4, 64, 32, 0, 128), (2, 5, 64, 32, 128, 128), (2, 0, 64, 32, 256, 256),
    (2, 1, 64, 32, 512, 256),
]
GATHER_PLAN = [
    (1, 19, 0, 1), (1, 15, 0, 1), (1, 26, 0, 1), (1, 22, 0, 1), (1, 17, 0, 1), (1, 18, 0, 1), (1, 21, 0, 1), (1, 25, 0, 1),
    (0, 0, ()), (1, 26, 0, 2), (1, 14, 0, 1), (1, 6, 0, 1), (1, 16, 0, 1), (1, 2, 0, 1), (1, 24, 0, 1), (1, 9, 0, 1),
    (1, 19, 1, 1), (1, 13, 0, 1), (1, 3, 0, 1), (1, 1, 0, 1), (1, 0, 0, 1), (1, 10, 0, 1), (1, 4, 0, 1), (1, 26, 0, 3),
    (1, 20, 0, 1), (1, 23, 0, 1), (1, 24, 1, 1), (1, 5, 0, 1), (2, 24, 0), (1, 13, 1, 1), (1, 6, 1, 1), (1, 16, 1, 1),
    (1, 15, 1, 1), (1, 2, 0, 2), (1, 4, 1, 1), (1, 10, 1, 1), (1, 3, 1, 1), (1, 9, 1, 1), (1, 23, 1, 1), (1, 14, 1, 1),
    (1, 1, 0, 2), (1, 26, 1, 1), (1, 20, 1, 1), (1, 5, 1, 1), (1, 2, 0, 3), (2, 19, 0), (1, 17, 0, 2), (2, 13, 0),
    (1, 25, 0, 2), (1, 6, 2, 1), (1, 0, 1, 1), (1, 4, 1, 2), (1, 2, 1, 1), (1, 1, 0, 3), (1, 3, 1, 2), (1, 21, 0, 2),
    (1, 5, 2, 1), (2, 6, 0), (1, 11, 0, 1), (1, 4, 1, 3), (1, 24, 2, 1), (1, 1, 1, 1), (1, 0, 1, 2), (1, 25, 0, 3),
    (1, 2, 2, 1), (1, 3, 1, 3), (1, 22, 0, 2), (1, 8, 0, 1), (1, 18, 0, 2), (1, 13, 2, 1), (1, 4, 2, 1), (2, 5, 0),
    (1, 12, 0, 1), (1, 1, 2, 1), (1, 3, 2, 1), (1, 22, 0, 3), (1, 16, 2, 1), (2, 3, 0), (2, 5, 1), (1, 0, 1, 3), (1, 17, 0, 3),
    (1, 11, 1, 1), (1, 21, 0, 3), (1, 7, 0, 1), (0, 1, ()), (0, 2, ()), (2, 1, 0), (2, 6, 1), (1, 18, 0, 3), (1, 23, 2, 1),
    (1, 9, 2, 1), (2, 10, 0), (1, 8, 1, 1), (2, 2, 0), (1, 0, 2, 1), (2, 4, 1), (1, 14, 2, 1), (1, 15, 2, 1), (2, 0, 0),
    (1, 20, 2, 1), (1, 10, 2, 1), (2, 4, 0), (1, 25, 1, 1), (1, 19, 2, 1), (1, 16, 2, 2), (2, 3, 1), (1, 24, 2, 2),
    (1, 22, 1, 1), (2, 2, 1), (1, 7, 1, 1), (1, 12, 1, 1), (1, 17, 1, 1), (1, 21, 1, 1), (2, 23, 0), (2, 1, 1), (2, 26, 0),
    (2, 11, 0), (1, 18, 1, 1), (1, 11, 2, 1), (1, 23, 2, 2), (1, 13, 2, 2), (0, 4, (1, 2, 3, 4, 5, 6)), (1, 8, 2, 1),
    (0, 5, ()), (0, 6, ()), (2, 20, 0), (1, 10, 2, 2), (2, 7, 0), (1, 9, 2, 2), (2, 0, 1), (0, 7, ()), (2, 12, 0),
    (1, 12, 2, 1), (1, 19, 2, 2), (2, 8, 0), (1, 7, 2, 1), (1, 26, 2, 1), (2, 25, 0), (0, 3, (0,)), (1, 14, 2, 2), (2, 9, 0),
    (1, 22, 2, 1), (1, 18, 2, 1), (1, 17, 2, 1), (1, 20, 2, 2), (2, 14, 0), (2, 22, 0), (2, 17, 0), (0, 8, ()), (1, 13, 2, 3),
    (0, 9, ()), (0, 10, ()), (2, 21, 0), (0, 11, ()), (2, 8, 1), (1, 10, 2, 3), (1, 21, 2, 1), (0, 12, ()), (1, 9, 2, 3),
    (1, 25, 2, 1), (2, 18, 0), (0, 13, ()), (1, 14, 2, 3), (2, 11, 1), (2, 13, 1), (1, 15, 2, 2), (1, 20, 2, 3), (1, 19, 2, 3),
    (1, 24, 2, 3), (2, 7, 1), (0, 14, ()), (0, 15, ()), (0, 16, ()), (2, 12, 1), (2, 16, 0), (2, 9, 1), (1, 23, 2, 3),
    (2, 10, 1), (1, 16, 2, 3), (2, 14, 1), (2, 15, 0), (0, 17, (7, 11)), (2, 26, 1), (2, 20, 1), (1, 15, 2, 3), (2, 17, 1),
    (0, 18, (8, 12)), (0, 19, (9, 10, 13, 14)), (2, 24, 1), (2, 22, 1), (2, 19, 1), (2, 21, 1), (0, 20, ()), (2, 16, 1),
    (2, 23, 1), (2, 15, 1), (0, 21, ()), (2, 25, 1), (0, 22, ()), (2, 18, 1), (0, 23, (15, 16, 19, 20, 23, 24)),
    (0, 24, (17, 21, 25)), (0, 25, (18, 22, 26)),
]
REDUCE_UNITS = [
    (2, 2, 0, 96, 0, 128), (2, 3, 0, 96, 128, 128), (2, 2, 0, 96, 256, 128), (2, 3, 0, 96, 384, 128), (2, 0, 0, 96, 512, 128),
    (2, 1, 0, 96, 640, 128), (1, 0, 0, 48, 0, 128), (1, 1, 0, 48, 128, 128), (1, 2, 0, 48, 256, 128), (1, 3, 0, 48, 384, 128),
    (1, 0, 0, 48, 512, 256), (1, 1, 0, 48, 768, 256), (1, 0, 0, 48, 1024, 256), (1, 1, 0, 48, 1280, 256),
    (1, 0, 0, 48, 2688, 128), (1, 1, 0, 48, 2816, 256), (1, 0, 0, 48, 1536, 128), (1, 1, 0, 48, 1664, 256),
    (1, 0, 0, 48, 1920, 256), (1, 3, 0, 48, 2176, 128), (1, 0, 0, 48, 2304, 128), (1, 1, 0, 48, 2432, 128),
    (1, 2, 0, 48, 2560, 128), (3, 3, 0, 8, 0, 128),
]
REDUCE_GROUP = [
    0, 0, 0, 0, 0, 0, 1, 1, 1, 1, 1, 1, 1, 1, 2, 2, 3, 3, 4, 4, 5, 5, 5, 6,
]
REDUCE_PLAN = [
    (0, 26), (0, 27), (0, 31), (0, 32), (0, 28), (1, 0, 0), (1, 1, 0), (0, 29), (0, 33), (1, 3, 0), (0, 34), (0, 35), (1, 2, 0),
    (0, 36), (0, 30), (0, 37), (0, 38), (2, 1, 0), (1, 1, 1), (1, 4, 0), (2, 0, 0), (1, 5, 0), (0, 39), (1, 0, 1), (0, 40),
    (1, 8, 0), (1, 7, 0), (0, 41), (2, 3, 0), (0, 43), (2, 2, 0), (1, 10, 0), (0, 44), (1, 2, 1), (0, 48), (2, 5, 0), (2, 4, 0),
    (1, 4, 1), (0, 51), (1, 9, 0), (1, 5, 1), (1, 3, 1), (1, 14, 0), (2, 8, 0), (0, 42), (1, 11, 0), (1, 12, 0), (1, 8, 1),
    (0, 49), (2, 10, 0), (1, 10, 1), (1, 15, 0), (0, 50), (0, 45), (2, 4, 1), (0, 46), (1, 4, 2), (1, 13, 0), (0, 52),
    (2, 5, 1), (0, 53), (2, 7, 0), (0, 47), (2, 14, 0), (2, 11, 0), (2, 9, 0), (1, 11, 1), (1, 9, 1), (1, 7, 1), (0, 54),
    (2, 10, 1), (1, 10, 2), (1, 14, 1), (0, 55), (2, 12, 0), (1, 6, 0), (1, 5, 2), (1, 12, 1), (0, 56), (2, 15, 0), (2, 11, 1),
    (1, 23, 0), (1, 15, 1), (1, 11, 2), (0, 57), (0, 58), (1, 16, 0), (2, 7, 1), (1, 17, 0), (1, 7, 2), (2, 14, 1), (1, 14, 2),
    (0, 59), (1, 19, 0), (2, 15, 1), (1, 15, 2), (2, 6, 0), (1, 18, 0), (2, 23, 0), (2, 3, 1), (2, 13, 0), (0, 60), (1, 13, 1),
    (1, 22, 0), (1, 23, 1), (2, 16, 0), (2, 12, 1), (1, 12, 2), (1, 6, 1), (2, 5, 2), (2, 19, 0), (1, 19, 1), (0, 61),
    (1, 20, 0), (1, 16, 1), (1, 21, 0), (2, 22, 0), (1, 22, 1), (2, 1, 1), (2, 12, 2), (2, 18, 0), (1, 18, 1), (2, 17, 0),
    (2, 6, 1), (2, 8, 1), (2, 14, 2), (1, 6, 2), (1, 3, 2), (2, 16, 1), (1, 17, 1), (1, 16, 2), (2, 0, 1), (2, 21, 0),
    (2, 23, 1), (1, 23, 2), (2, 13, 1), (1, 13, 2), (1, 21, 1), (1, 0, 2), (2, 11, 2), (2, 22, 1), (2, 9, 1), (2, 20, 0),
    (2, 7, 2), (1, 20, 1), (2, 18, 1), (1, 18, 2), (2, 17, 1), (1, 17, 2), (2, 21, 1), (2, 3, 2), (2, 13, 2), (1, 9, 2),
    (1, 1, 2), (1, 22, 2), (1, 21, 2), (2, 6, 2), (2, 4, 2), (2, 20, 1), (2, 2, 1), (2, 16, 2), (2, 10, 2), (1, 2, 2),
    (1, 20, 2), (0, 62), (2, 19, 1), (1, 19, 2), (1, 8, 2), (2, 18, 2), (2, 2, 2), (0, 63), (2, 0, 2), (2, 22, 2), (2, 17, 2),
    (2, 8, 2), (2, 9, 2), (2, 23, 2), (2, 19, 2), (2, 21, 2), (2, 15, 2), (2, 1, 2), (2, 20, 2),
]


def whole_layer(*refs):
    (
        tokens_in, lengths, cot_in, in_w, out_w, up_w, down_w, b0, b1, b2, b3, b4, b5, b6,
        result, tokens_grad, in_g, out_g, up_g, down_g, small_g,
        WQ, WU, WD, stage_s, stage_r, SP, PV, UB, TS, SIG, QF, KF, VX, SES, SER, LER,
        MSK, CS, USE, LAST, RD, ATT, ATS, N1, S1, F1, NL, NLS, ACT, GP, AT, ATS2, DG, DGS, HGS,
        BG, BGS, PGS, OUT, RB0D, RB1D, RB0W, RB1W, FD, FW, SG, SGR, RB0S, RB1S, FS,
        VEC, HID, tokens, cot, send_sems, gather_sems, reduce_sems, core_sems, hbm, load_sems,
    ) = refs
    p = Place()
    c = p.c

    W5 = {IN_OUT: WQ.reshape(4, 2, 2, 48, FF), UP: WU.reshape(4, 2, 2, 48, FF)}
    WD6 = WD.reshape(4, 2, 2, 2, 96, WIDTH)
    AT4 = AT.reshape(16, 2, 96, ROWS)
    ATS3 = ATS2.reshape(16, 96, ROWS)
    DW = ACT.reshape(2048, WIDTH)

    def gather_view(u, blocks, core):
        arr, _, r0, nr, c0, nc = GATHER_UNITS[u]
        if arr == SMALL:
            return SP.at[blocks + (core,)]
        if arr == DOWN:
            return WD6.at[blocks + (core, pl.ds(r0, nr), pl.ds(c0, nc))]
        return W5[arr].at[blocks + (pl.ds(r0, nr), pl.ds(pl.multiple_of(core * HALF + c0, 128), nc))]

    sends = Sends(send_sems, SENDS)
    gather = Gather(p, GATHER_UNITS, gather_view, sends, gather_sems)
    reduce = Reduce(
        p, REDUCE_UNITS,
        {DOWN: DW.at[pl.ds(0, HALF)].reshape(4, 2, 2, 96, WIDTH), UP: W5[UP], SMALL: SG},
        {DOWN: (RB0D, RB1D), UP: (RB0W, RB1W), SMALL: (RB0S, RB1S)},
        {DOWN: FD, UP: FW, SMALL: FS},
        sends, reduce_sems,
    )
    copies, sent, leaving = [], {}, {}

    def to_core(name, src, dst, mine=None):
        sem = core_sems.at[len(sent)]
        sent[name] = (dst if mine is None else mine, sem)
        leaving[name] = sends.start(lambda send: remote(src, dst, send, sem, p.peer("core")))

    def got(name):
        dst, sem = sent[name]
        remote(dst, dst, sem, sem, p.peer("core")).wait_recv()

    def left(name):
        sends.left(leaving[name])

    def write(src, dst):
        copy = pltpu.make_async_copy(src, dst, hbm.at[len(copies)])
        copy.start()
        copies.append(copy)

    def at128(start, size):
        return pl.ds(pl.multiple_of(start, 128), size)

    def rows_loop(body, carry, rows=slice(0, ROWS), size=64):
        for n in range(rows.start, rows.stop, size):
            carry = body(slice(n, n + size), carry)
        return carry

    def mean(v):
        return jnp.sum(v, axis=1, keepdims=True) * (1.0 / WIDTH)

    def fold(v):
        return jnp.sum(v.reshape(-1, 8, v.shape[1]), axis=0)

    def low_lanes(rows):
        return lax.broadcasted_iota(jnp.int32, (rows, 128), 1) < HEAD

    zero = jnp.zeros((8, WIDTH), F32)
    halves, carried = (slice(0, ROWS // 2), slice(ROWS // 2, ROWS)), {}
    first_len, second_len = lengths[0, 0], lengths[0, 1]
    first = c * ROWS
    own_half = at128(c * HALF, HALF)
    out_b, n_gain, n_bias, down_b, f_gain, f_bias = (lambda i=i: PV[i : i + 1, :] for i in range(6))

    loads = [pltpu.make_async_copy(a, b, load_sems.at[i]) for i, (a, b) in enumerate(((tokens_in, tokens), (cot_in, cot)))]
    for copy in loads:
        copy.start()
    bar = pltpu.get_barrier_semaphore()
    for to in (p.peer("x"), p.peer("y"), p.peer("core"), p.peer("z", 1), p.peer("z", 2), p.peer("z", 3)):
        pl.semaphore_signal(bar, inc=1, device_id=to, device_id_type=MESH)
    stage_s[0:24, 0:2304] = in_w[...]
    stage_s[0:24, 2304:3072] = out_w[...]
    stage_s[0:24, 3072:6144] = up_w[...]
    WD6[p.z, p.y, p.x, c] = down_w[...]
    FS[...] = jnp.zeros((8, 128), F32)
    for i, ref in enumerate((b0, b1, b2, b3, b4, b5)):
        FS[i : i + 1, 0:24] = ref[...].astype(F32)
    FS[6:7, 0:96] = b6[...].astype(F32)
    SP[p.z, p.y, p.x, c] = FS[...]
    pl.semaphore_wait(bar, 6)
    to_core("stage", stage_s, stage_r)
    to_core("tokens", tokens_in, TS)

    def prep():
        got("stage")
        mine, other = stage_s[0:24, :].astype(F32), stage_r[0:24, :].astype(F32)
        top, bottom = jnp.where(c == 0, mine, other), jnp.where(c == 0, other, mine)
        share = jnp.concatenate([top, bottom], axis=0).astype(BF16)
        W5[IN_OUT][p.z, p.y, p.x, :, own_half] = jnp.where(c == 0, share[:, 0:HALF], share[:, HALF:FF])
        W5[UP][p.z, p.y, p.x, :, own_half] = jnp.where(c == 0, share[:, FF : FF + HALF], share[:, FF + HALF :])

    def docs(part):
        if part:
            return masks()
        pos = lax.broadcasted_iota(jnp.int32, (ROWS, 128), 0) + first
        doc = (pos >= first_len).astype(jnp.int32)
        span = jnp.where(doc == 0, first_len, second_len).astype(F32)
        angle = HALF_PI * (pos - doc * first_len).astype(F32) / span
        CS[...] = jnp.where(low_lanes(ROWS), jnp.cos(angle), jnp.sin(angle))
        prior_doc = jnp.where(first > 0, (first - 1 >= first_len).astype(jnp.int32), -1)
        last_doc = (first + (ROWS - 1) >= first_len).astype(jnp.int32)
        USE[...] = (doc == prior_doc).astype(F32)
        LAST[...] = (doc == last_doc).astype(BF16)

    def masks():
        row = lax.broadcasted_iota(jnp.int32, (ROWS, ROWS), 0)
        col = lax.broadcasted_iota(jnp.int32, (ROWS, ROWS), 1)
        row_doc = (row + first >= first_len).astype(jnp.int32)
        col_doc = (col + first >= first_len).astype(jnp.int32)
        MSK[...] = ((col <= row) & (row_doc == col_doc)).astype(BF16)

    def params():
        wide = jnp.zeros((8, 256), F32)
        for step, dst in ((24, PV), (96, UB)):
            n = 384 // step
            for g in range(32 // n):
                total = jnp.zeros((8, 384), F32)
                for k in range(n):
                    d = n * g + k
                    tile = SP[d // 8, (d // 4) % 2, (d // 2) % 2, d % 2]
                    total = total + pltpu.roll(jnp.concatenate([tile, wide], axis=1), step * k, 1)
                dst[:, 384 * g : 384 * (g + 1)] = total

    def project(j):
        if j == 0:
            loads[0].wait()
        rows = tokens[...]
        low = low_lanes(ROWS)
        for k, feat in ((0, QF), (1, KF)):
            raw = dot(rows, WQ[:, k * WIDTH + 256 * j : k * WIDTH + 256 * (j + 1)], 1, 0)
            for i in range(2):
                r = raw[:, 128 * i : 128 * (i + 1)]
                e = jnp.exp(-jnp.abs(r))
                active = jnp.maximum(r, 0.0) + jnp.log1p(e)
                slope = jnp.where(r >= 0, 1.0, e) / (1.0 + e)
                at = k * WIDTH + 256 * j + 128 * i
                SIG[:, at : at + 128] = slope.astype(BF16)
                turned = pltpu.roll(active, HEAD, 1)
                feat[4 * j + 2 * i] = (jnp.where(low, active, turned) * CS[...]).astype(BF16)
                feat[4 * j + 2 * i + 1] = (jnp.where(low, turned, active) * CS[...]).astype(BF16)
        value = dot(rows, WQ[:, 2 * WIDTH + 256 * j : 2 * WIDTH + 256 * (j + 1)], 1, 0)
        for i in range(2):
            v = value[:, 128 * i : 128 * (i + 1)]
            VX[4 * j + 2 * i] = jnp.where(low, v, 1.0).astype(BF16)
            VX[4 * j + 2 * i + 1] = jnp.where(low, 1.0, v).astype(BF16)

    def summary():
        def one(h, carry):
            SES[h] = dot(KF[h] * LAST[...], VX[h], 0, 0).astype(BF16)
            return carry

        lax.fori_loop(0, HEADS, one, 0)
        to_core("state", SES, SER)

    def attend(n):
        if n == 0:
            got("state")
        at = slice(128 * n, 128 * (n + 1))
        low = low_lanes(256)
        for half in range(2):
            width = 256 * (half + 1)
            rows = slice(256 * half, width)
            outs = []
            for h in (2 * n, 2 * n + 1):
                q = QF[h, rows, :]
                scores = dot(q, KF[h, 0:width, :], 1, 1).astype(BF16) * MSK[rows, 0:width]
                outs.append(dot(scores, VX[h, 0:width, :], 1, 0) + USE[rows, :] * dot(q, SER[h], 1, 0))
            numer = jnp.where(low, outs[0], outs[1])
            denom = jnp.where(low, pltpu.roll(outs[0], HEAD, 1), pltpu.roll(outs[1], HEAD, 1))
            inverse = 1.0 / denom
            RD[rows, at] = inverse
            ATT[rows, at] = (numer * inverse).astype(BF16)

    def out_project(part):
        if part:
            return norm_first(part - 1)
        to_core("attended", ATT, ATS)
        for j in range(3):
            cols = slice(256 * j, 256 * (j + 1))
            F1[:, cols] = (
                tokens[:, cols].astype(F32)
                + dot(ATT[...], WQ[:, 2304 + 256 * j : 2304 + 256 * (j + 1)], 1, 0)
                + out_b()[:, cols]
            )

    def norm_first(part):
        def norm(at, carry):
            x = F1[at, :]
            centered = x - mean(x)
            scale = lax.rsqrt(mean(centered * centered) + NORM_EPS)
            normal = centered * scale
            N1[at, :] = normal
            S1[at, :] = jnp.broadcast_to(scale, (normal.shape[0], 128))
            NL[at, :] = (normal * n_gain() + n_bias()).astype(BF16)
            return carry

        rows_loop(norm, 0, halves[part])
        if part:
            to_core("normed", NL, NLS)

    def up(j):
        cols = slice(512 * j, 512 * (j + 1))
        hidden = dot(NL[...], WU[:, cols], 1, 0) + UB[6:7, cols]
        phi = 0.5 + 0.5 * lax.erf(hidden * math.sqrt(0.5))
        active = (hidden * phi).astype(BF16)
        slope = phi + hidden * (jnp.exp(-0.5 * hidden * hidden) * (1.0 / math.sqrt(2 * math.pi)))
        GP[:, cols] = slope.astype(BF16)
        AT[cols, :] = active.T
        for piece in range(4):
            a, b = max(512 * j, 768 * piece), min(512 * (j + 1), 768 * (piece + 1))
            if a < b:
                ACT[piece, :, a - 768 * piece : b - 768 * piece] = active[:, a - 512 * j : b - 512 * j]
        if j == 5:
            to_core("activated", AT4.at[:, 1 - c], ATS3)

    def down(j):
        cols = slice(256 * j, 256 * (j + 1))
        total = down_b()[:, cols] + (N1[:, cols] * n_gain()[:, cols] + n_bias()[:, cols])
        for piece in range(4):
            total = total + dot(ACT[piece], WD[768 * piece : 768 * (piece + 1), cols], 1, 0)
        F1[:, cols] = total

    def norm_second(part):
        if part == 0:
            loads[1].wait()

        def norm(at, carry):
            gain_sum, bias_sum, down_sum = carry
            x = F1[at, :]
            centered = x - mean(x)
            scale = lax.rsqrt(mean(centered * centered) + NORM_EPS)
            normal = centered * scale
            OUT[at, :] = (normal * f_gain() + f_bias()).astype(BF16)
            ct = cot[at, :].astype(F32)
            e = ct * f_gain()
            grad = scale * (e - mean(e) - normal * mean(e * normal))
            F1[at, :] = grad
            low = grad.astype(BF16)
            DG[at, :] = low
            return gain_sum + fold(ct * normal), bias_sum + fold(ct), down_sum + fold(low.astype(F32))

        carried["second"] = rows_loop(norm, carried.get("second", (zero, zero, zero)), halves[part])
        to_core(("down", part), DG.at[halves[part]], DGS.at[halves[part]])
        if part:
            for i, s in zip((4, 5, 3), carried["second"]):
                VEC[i : i + 1, :] = jnp.sum(s, axis=0, keepdims=True)
            write(OUT, result)

    def down_weight(j):
        cols = slice(256 * j, 256 * (j + 1))
        if j == 0:
            got("activated")
        part = dot(AT4[:, c].reshape(HALF, ROWS), DG[:, cols], 1, 0)
        if j == 0:
            got(("down", 0))
            got(("down", 1))
        DW[0:HALF, cols] = (part + dot(ATS2[...], DGS[:, cols], 1, 0)).astype(BF16)

    def free_up():
        while gathered:
            sends.left(gathered.pop())

    def hidden_back(j):
        cols = slice(512 * j, 512 * (j + 1))
        grad = dot(DG[...], WD[cols, :], 1, 1) * GP[:, cols].astype(F32)
        low = grad.astype(BF16)
        GP[:, cols] = low
        HID[0:1, cols] = jnp.sum(low.astype(F32), axis=0, keepdims=True)
        if j == 5:
            to_core("hidden", GP.at[:, at128((1 - c) * HALF, HALF)], HGS)

    def normed_back(j):
        cols = slice(256 * j, 256 * (j + 1))
        F1[:, cols] = F1[:, cols] + dot(GP[...], WU[cols, :], 1, 1)

    def up_weight(j):
        if j == 0:
            free_up()
            got("normed")
            got("hidden")
        cols = slice(512 * j, 512 * (j + 1))
        part = dot(NL[...], GP[:, at128(c * HALF + 512 * j, 512)], 0, 0) + dot(NLS[...], HGS[:, cols], 0, 0)
        WU[:, cols] = part.astype(BF16)

    def norm_first_back(part):
        def norm(at, carry):
            gain_sum, bias_sum, out_sum = carry
            g, normal, scale = F1[at, :], N1[at, :], S1[at, 0:1]
            e = g * n_gain()
            grad = scale * (e - mean(e) - normal * mean(e * normal))
            F1[at, :] = grad
            low = grad.astype(BF16)
            BG[at, :] = low
            return gain_sum + fold(g * normal), bias_sum + fold(g), out_sum + fold(low.astype(F32))

        carried["first"] = rows_loop(norm, carried.get("first", (zero, zero, zero)), halves[part])
        if part:
            to_core("branch", BG.at[:, at128((1 - c) * 384, 384)], BGS)
            for i, s in zip((1, 2, 0), carried["first"]):
                VEC[i : i + 1, :] = jnp.sum(s, axis=0, keepdims=True)

    def small_tiles(half):
        line = lax.broadcasted_iota(jnp.int32, (8, 128), 0)
        lane = lax.broadcasted_iota(jnp.int32, (8, 128), 1)
        for d in range(16 * half, 16 * (half + 1)):
            g, k = divmod(d, 16)
            part = VEC[:, 384 * g : 384 * (g + 1)]
            a = (pltpu.roll(part, 384 - 24 * k, 1) if k else part)[:, 0:128]
            g, k = divmod(d, 4)
            part = jnp.broadcast_to(HID[0:1, 384 * g : 384 * (g + 1)], (8, 384))
            b = (pltpu.roll(part, 384 - 96 * k, 1) if k else part)[:, 0:128]
            tile = jnp.where((line < 6) & (lane < 24), a, jnp.where((line == 6) & (lane < 96), b, 0.0))
            SGR[0, d % 2, d // 8, (d // 4) % 2, (d // 2) % 2] = tile
        if half:
            to_core("small", SGR.at[0, 1 - c], SGR.at[1, 0])

    def small_sum():
        got("small")
        SG[...] = SGR[0, c] + SGR[1, 0]

    def slot(h):
        if isinstance(h, int):
            return slice(512 * (h // 4), 512 * (h // 4 + 1)), slice(128 * (h % 4), 128 * (h % 4 + 1))
        return at128(512 * lax.div(h, 4), 512), at128(128 * lax.rem(h, 4), 128)

    def numer_back(j):
        if j == 0:
            left("activated")
            left("state")
        low = low_lanes(ROWS)
        lane = lax.broadcasted_iota(jnp.int32, (ROWS, 128), 1)
        across = low_lanes(128) != (lax.broadcasted_iota(jnp.int32, (128, 128), 0) < HEAD)
        across = across.astype(F32).astype(BF16)
        grads = dot(BG[...], WQ[256 * j : 256 * (j + 1), 2304:FF], 1, 1)
        for i in range(2):
            at = slice(256 * j + 128 * i, 256 * j + 128 * (i + 1))
            ng = grads[:, 128 * i : 128 * (i + 1)] * RD[:, at]
            scaled = ng * ATT[:, at].astype(F32)
            high = scaled.astype(BF16)
            rest = (scaled - high.astype(F32)).astype(BF16)
            dgrad = -(dot(high, across, 1, 0) + dot(rest, across, 1, 0))
            hi = dgrad.astype(BF16).astype(F32)
            beside = jnp.where(
                (lane == 0) | (lane == HEAD), hi, jnp.where((lane == 1) | (lane == HEAD + 1), dgrad - hi, 0.0)
            )
            for par in range(2):
                h = 4 * j + 2 * i + par
                ngx = jnp.where(low, ng, beside) if par == 0 else jnp.where(low, beside, ng)
                AT[slot(h)] = ngx.astype(BF16)
                SES[h] = dot(QF[h], (ngx * USE[...]).astype(BF16), 0, 0).astype(BF16)
        if j == 2:
            to_core("leave", SES, LER)

    def out_weight():
        free_up()
        got("attended")
        part = dot(ATT[...], BG[:, at128(c * 384, 384)], 0, 0)
        got("branch")
        WU[:, 2688:FF] = (part + dot(ATS[...], BGS[...], 0, 0)).astype(BF16)

    def attend_back(j):
        if j == 0:
            left("hidden")
            got("leave")
        n = 3 * (1 - c if j < 3 else c) + j % 3
        low = low_lanes(ROWS)
        lead = c == 0
        last = LAST[...].astype(F32) * jnp.where(lead, 1.0, 0.0).astype(F32)
        m0, m1 = MSK[0:256, 0:256], MSK[256:ROWS, :]
        top, bottom = slice(0, 256), slice(256, ROWS)
        pieces = [], [], []
        for h in (2 * n, 2 * n + 1):
            ngx, qf, kf, vx = AT[slot(h)], QF[h], KF[h], VX[h]
            d0 = dot(ngx[top], vx[top], 1, 1).astype(BF16) * m0
            d1 = dot(ngx[bottom], vx, 1, 1).astype(BF16) * m1
            s0 = dot(qf[top], kf[top], 1, 1).astype(BF16) * m0
            s1 = dot(qf[bottom], kf, 1, 1).astype(BF16) * m1
            q_grad = jnp.concatenate([dot(d0, kf[top], 1, 0), dot(d1, kf, 1, 0)], axis=0)
            k_top = dot(d0, qf[top], 0, 0) + dot(d1[:, top], qf[bottom], 0, 0)
            k_grad = jnp.concatenate([k_top, dot(d1[:, bottom], qf[bottom], 0, 0)], axis=0)
            v_top = dot(s0, ngx[top], 0, 0) + dot(s1[:, top], ngx[bottom], 0, 0)
            v_grad = jnp.concatenate([v_top, dot(s1[:, bottom], ngx[bottom], 0, 0)], axis=0)
            past = dot(jnp.where(lead, vx, ngx), jnp.where(lead, LER[h], SER[h]), 1, 1)
            q_grad = (q_grad + USE[...] * past) * CS[...]
            k_grad = (k_grad + last * past) * CS[...]
            pieces[0].append(q_grad + pltpu.roll(q_grad, HEAD, 1))
            pieces[1].append(k_grad + pltpu.roll(k_grad, HEAD, 1))
            pieces[2].append(v_grad + last * dot(kf, LER[h], 1, 0))
        for k, (even, odd) in enumerate(pieces):
            both = jnp.where(low, even, odd)
            at = at128(k * WIDTH + 128 * n, 128)
            if k < 2:
                both = both * SIG[:, at].astype(F32)
            GP[:, at] = both.astype(BF16)
        if j == 2:
            for k in range(3):
                src = GP.at[:, at128(k * WIDTH + (1 - c) * 384, 384)]
                to_core(("projected", k), src, PGS.at[:, pl.ds(384 * k, 384)])

    def in_weight(j):
        cols = slice(384 * j, 384 * (j + 1))
        if j == 0:
            got("tokens")
        part = dot(tokens[...], GP[:, at128(j * WIDTH + c * 384, 384)], 0, 0)
        got(("projected", j))
        WU[:, HALF + 384 * j : HALF + 384 * (j + 1)] = (part + dot(TS[...], PGS[:, cols], 0, 0)).astype(BF16)

    def tokens_back(j):
        cols = slice(256 * j, 256 * (j + 1))
        F1[:, cols] = F1[:, cols] + dot(GP[:, 0:2304], WQ[cols, 0:2304], 1, 1)
        if j == 2:
            write(F1, tokens_grad)

    steps = []
    for step, count in (
        (prep, 0), (docs, 2), (params, 0), (project, 3), (summary, 0), (attend, 6), (out_project, 3), (up, 6), (down, 3),
        (norm_second, 2), (down_weight, 3), (hidden_back, 6), (normed_back, 3), (up_weight, 3), (norm_first_back, 2),
        (small_tiles, 2), (small_sum, 0), (numer_back, 3), (out_weight, 0), (attend_back, 6),
        (in_weight, 3), (tokens_back, 3),
    ):
        steps += [partial(step, j) for j in range(count)] if count else [step]

    for kind, *op in GATHER_PLAN:
        if kind == STEP:
            for u in op[1]:
                gather.ready(u)
            steps[op[0]]()
        elif kind == ISSUE:
            gather.issue(*op)
        else:
            gather.share(*op)

    gathered = sends.now_open()

    outputs = {1: [(up_g, 0, 0, HALF)], 2: [(out_g, 2688, 0, 384)]}
    for k in range(3):
        outputs[3 + k] = [(in_g, HALF + 384 * k, WIDTH * k, 384)]
    mine, other = pl.ds(pl.multiple_of(24 * c, 8), 24), pl.ds(pl.multiple_of(24 * (1 - c), 8), 24)
    open_units = list(REDUCE_GROUP)

    def done(u):
        group = REDUCE_GROUP[u]
        open_units.remove(group)
        if group in open_units:
            return
        if group == 0:
            write(FD, down_g)
        elif group == 6:
            small_g[...] = FS[...]
        else:
            for i, (ref, at, to, width) in enumerate(outputs[group]):
                here, there = (ref.at[:, at128(to + core * width, width)] for core in (c, 1 - c))
                to_core((group, i), FW.at[other, pl.ds(at, width)], here, there)
                write(FW.at[mine, pl.ds(at, width)], here)

    for kind, *op in REDUCE_PLAN:
        if kind == STEP:
            steps[op[0]]()
        elif kind == ISSUE:
            reduce.send(*op)
        else:
            reduce.add(*op)
            if op[1] == 2:
                done(op[0])

    for group in outputs:
        for i in range(len(outputs[group])):
            got((group, i))
    sends.finish()
    for copy in copies:
        copy.wait()


def hand_out(*refs):
    made, small, outs, vectors = refs[0:6], refs[6], refs[7:13], refs[13:20]
    held, lines, sems = refs[20:26], refs[26:33], refs[33]
    pieces = []
    for a, b, c in zip(made, held, outs):
        rows = a.shape[0]
        step = 128 if rows == ROWS else rows
        for r in range(0, rows, step):
            pieces.append(tuple(ref.at[pl.ds(r, step)] for ref in (a, b, c)))
    ins = [pltpu.make_async_copy(a, b, sems.at[0, i]) for i, (a, b, _) in enumerate(pieces)]
    back = [pltpu.make_async_copy(b, c, sems.at[1, i]) for i, (_, b, c) in enumerate(pieces)]
    for copy in ins:
        copy.start()
    for i, line in enumerate(lines):
        line[...] = small[i : i + 1, 0 : line.shape[1]]
        back.append(pltpu.make_async_copy(line, vectors[i], sems.at[1, len(pieces) + i]))
        back[-1].start()
    for copy, then in zip(ins, back):
        copy.wait()
        then.start()
    for copy in back:
        copy.wait()


def layer_2x2x4(tokens, lengths, in_weight, out_weight, out_bias, norm_gain, norm_bias, up_weight, up_bias,
                down_weight, down_bias, final_gain, final_bias, cotangent):
    vmem, anywhere = pl.BlockSpec(memory_space=pltpu.VMEM), pl.BlockSpec(memory_space=pl.ANY)

    def v(*shape, dtype=BF16):
        return pltpu.VMEM(shape, dtype)

    dma = pltpu.SemaphoreType.DMA
    scratch = [
        v(WIDTH, FF), v(WIDTH, FF), v(FF, WIDTH),
        v(32, 6144), v(32, 6144), v(4, 2, 2, 2, 8, 128, dtype=F32),
        v(8, WIDTH, dtype=F32), v(8, FF, dtype=F32),
        v(ROWS, WIDTH), v(ROWS, HALF),
        v(HEADS, ROWS, 128), v(HEADS, ROWS, 128), v(HEADS, ROWS, 128),
        v(HEADS, 128, 128), v(HEADS, 128, 128), v(HEADS, 128, 128),
        v(ROWS, ROWS), v(ROWS, 128, dtype=F32), v(ROWS, 128, dtype=F32), v(ROWS, 128),
        v(ROWS, WIDTH, dtype=F32), v(ROWS, WIDTH), v(ROWS, WIDTH),
        v(ROWS, WIDTH, dtype=F32), v(ROWS, 128, dtype=F32), v(ROWS, WIDTH, dtype=F32),
        v(ROWS, WIDTH), v(ROWS, WIDTH), v(4, ROWS, WIDTH), v(ROWS, FF),
        v(FF, ROWS), v(HALF, ROWS), v(ROWS, WIDTH), v(ROWS, WIDTH), v(ROWS, HALF),
        v(ROWS, WIDTH), v(ROWS, 384), v(ROWS, 1152), v(ROWS, WIDTH),
        v(4, 2, 96, WIDTH), v(7, 96, WIDTH),
        v(4, 2, 48, FF), v(7, 48, FF),
        v(96, WIDTH, dtype=F32), v(48, FF, dtype=F32),
        v(4, 2, 2, 8, 128, dtype=F32), v(2, 2, 4, 2, 2, 8, 128, dtype=F32),
        v(4, 2, 8, 128, dtype=F32), v(7, 8, 128, dtype=F32), v(8, 128, dtype=F32),
        v(8, WIDTH, dtype=F32), v(8, FF, dtype=F32),
        v(ROWS, WIDTH), v(ROWS, WIDTH),
        dma((SENDS,)), dma((6 * len(GATHER_UNITS),)), dma((3 * len(REDUCE_UNITS),)), dma((20,)), dma((10,)), dma((2,)),
    ]
    shapes = (
        jax.ShapeDtypeStruct((ROWS, WIDTH), BF16),
        jax.ShapeDtypeStruct((ROWS, WIDTH), F32),
        jax.ShapeDtypeStruct((24, 2304), F32),
        jax.ShapeDtypeStruct((24, WIDTH), F32),
        jax.ShapeDtypeStruct((24, FF), F32),
        jax.ShapeDtypeStruct((96, WIDTH), F32),
    )
    lines = (jax.ShapeDtypeStruct((1, 24), F32),) * 6 + (jax.ShapeDtypeStruct((1, 96), F32),)
    vectors = (out_bias, norm_gain, norm_bias, down_bias, final_gain, final_bias, up_bias)
    made = pl.pallas_call(
        whole_layer,
        out_shape=shapes + (jax.ShapeDtypeStruct((8, 128), F32),),
        in_specs=[anywhere, pl.BlockSpec(memory_space=pltpu.SMEM), anywhere] + [vmem] * 11,
        out_specs=(anywhere,) * 6 + (vmem,),
        scratch_shapes=scratch,
        compiler_params=pltpu.CompilerParams(
            collective_id=0, has_side_effects=True, vmem_limit_bytes=VMEM_LIMIT
        ),
    )(tokens, lengths, cotangent, in_weight, out_weight, up_weight, down_weight, *(b.reshape(1, -1) for b in vectors))
    result, tokens_grad, in_g, out_g, up_g, down_g, *small = pl.pallas_call(
        hand_out,
        out_shape=shapes + lines,
        in_specs=[anywhere] * 6 + [vmem],
        out_specs=(anywhere,) * 13,
        scratch_shapes=[pltpu.VMEM(s.shape, s.dtype) for s in shapes + lines] + [dma((2, 19))],
        compiler_params=pltpu.CompilerParams(vmem_limit_bytes=VMEM_LIMIT),
    )(*made)
    out_bias_g, norm_gain_g, norm_bias_g, down_bias_g, final_gain_g, final_bias_g, up_bias_g = (
        g.reshape(-1) for g in small
    )
    return (result, tokens_grad, in_g, out_g, out_bias_g, norm_gain_g, norm_bias_g, up_g,
            up_bias_g, down_g, down_bias_g, final_gain_g, final_bias_g)


VMEM_LIMIT = 64 * 2**20 - 2**18


def solution(mesh):
    both = ("dp", "fsdp")
    rows, vector = P(both, None), P(both)
    in_specs = (rows, P("dp", None), rows, rows, vector, vector, vector, rows, vector, rows, vector, vector, vector, rows)
    out_specs = (rows, rows, rows, rows, vector, vector, vector, rows, vector, rows, vector, vector, vector)
    body = layer_2x2x4 if dict(mesh.shape) == {"dp": 16, "fsdp": 2} else per_device
    return jax.shard_map(body, mesh=mesh, in_specs=in_specs, out_specs=out_specs, check_vma=False)
```
